32 devices in a mesh: seq: 16 (over z, x, core), fsdp: 2 (over y).
Axes of the slice: x: 2, y: 2, z: 4, core: 2. Of those that a mesh axis runs over, the one named last changes fastest.
Arguments:
- hidden_in: bfloat16 [4, 3072, 1024], P('fsdp', 'seq'), may hold values from -6 to 6
- cotangent: bfloat16 [4, 3072, 1024], P('fsdp', 'seq'), may hold values from -6 to 6
- norm_gain: float32 [1024], replicated, may hold values from 0.5 to 1.5
- in_weight: bfloat16 [1024, 4384], P('fsdp'), may hold values from -0.1875 to 0.1875
- conv_weight: float32 [4, 2304], replicated, may hold values from -3 to 3
- conv_bias: float32 [2304], replicated, may hold values from -0.5 to 0.5
- dt_bias: float32 [32], replicated, may hold values from -6.5 to -2.5
- a_log: float32 [32], replicated, may hold values from 0 to 2.75
- skip_gain: float32 [32], replicated, may hold values from 0.5 to 1.5
- gate_gain: float32 [2048], replicated, may hold values from 0.5 to 1.5
- out_weight: bfloat16 [2048, 1024], P('fsdp'), may hold values from -0.125 to 0.125
Outputs:
- hidden_out: bfloat16 [4, 3072, 1024], P('fsdp', 'seq')
- grad_hidden: float32 [4, 3072, 1024], P('fsdp', 'seq')
- grad_norm_gain: float32 [1024], replicated
- grad_in_weight: float32 [1024, 4384], P('fsdp')
- grad_conv_weight: float32 [4, 2304], replicated
- grad_conv_bias: float32 [2304], replicated
- grad_dt_bias: float32 [32], replicated
- grad_a_log: float32 [32], replicated
- grad_skip_gain: float32 [32], replicated
- grad_gate_gain: float32 [2048], replicated
- grad_out_weight: float32 [2048, 1024], P('fsdp')
The draws below stay inside these ranges and needn't reach their ends.
All inputs are finite; a program needn't handle non-finite values.
Results may differ from the reference program's by a relative error of at most 0.004.
The reference program's roundings to bfloat16 on the way count: a program that leaves them out, or rounds other values in their place, can miss the bound.
Values may be sent and summed in bfloat16 or wider, within the bound.
No kernel may reach another device: no remote copies, remote signals or barrier semaphores. Data moves between devices by JAX's collectives and lax.ppermute only.
A program may use at most 320 MiB of HBM per device.

```python
import jax
import jax.numpy as jnp
from jax import lax

D = 1024
HEADS = 32
HEADDIM = 64
STATE = 128
CONV = 4
SPAN = 256
INNER = 2048
PROJ = 4384
CONV_CH = 2304
LENGTH = 3072
BATCH = 4


def block_levels(own_key, dims, cuts, low, high):
    loudness, own = 1.0, jax.random.fold_in(own_key, 6)
    for position, blocks in cuts:
        draws = jnp.exp(jax.random.uniform(jax.random.fold_in(own, position), (blocks,), jnp.float32, low / len(cuts), high / len(cuts)))
        loudness = loudness * jnp.repeat(draws, dims[position] // blocks).reshape([-1 if axis == position else 1 for axis in range(len(dims))])
    return loudness


def gaussian(rng, shape, spread, most, cuts=(), kind=jnp.bfloat16):
    factor_of = block_levels(rng, shape, cuts, -0.22, 0.18) if cuts else 1.0
    values = jax.random.normal(rng, shape, jnp.float32) * spread * factor_of
    return jnp.minimum(jnp.maximum(values, -most), most).astype(kind)


def setup_inputs(seed: int = 0) -> dict:
    splits = jax.random.split(jax.random.key(seed), 12)
    return {
        "hidden_in": gaussian(splits[0], (BATCH, LENGTH, D), 1.0, 6.0, ((0, 2), (1, 16))),
        "cotangent": gaussian(splits[1], (BATCH, LENGTH, D), 1.0, 6.0, ((0, 2), (1, 16))),
        "norm_gain": jnp.clip(1.0 + 0.1 * jax.random.normal(splits[2], (D,), jnp.float32), 0.5, 1.5),
        "in_weight": gaussian(splits[3], (D, PROJ), D ** -0.5, 0.1875, ((0, 2),)),
        "conv_weight": gaussian(splits[4], (CONV, CONV_CH), CONV ** -0.5, 3.0, (), jnp.float32),
        "conv_bias": jnp.clip(jax.random.uniform(splits[5], (CONV_CH,), jnp.float32, -0.5, 0.5), -0.5, 0.5),
        "dt_bias": jnp.clip(jax.random.uniform(splits[6], (HEADS,), jnp.float32, -6.5, -2.5), -6.5, -2.5),
        "a_log": jnp.clip(jax.random.uniform(splits[7], (HEADS,), jnp.float32, 0.0, 2.75), 0.0, 2.75),
        "skip_gain": jnp.clip(jax.random.uniform(splits[8], (HEADS,), jnp.float32, 0.5, 1.5), 0.5, 1.5),
        "gate_gain": jnp.clip(1.0 + 0.1 * jax.random.normal(splits[9], (INNER,), jnp.float32), 0.5, 1.5),
        "out_weight": gaussian(splits[10], (INNER, D), INNER ** -0.5, 0.125, ((0, 2),)),
    }


norm_eps = 1e-05

@jax.custom_vjp
def low(v):
    return lax.optimization_barrier(v.astype(jnp.bfloat16)).astype(jnp.float32)

@jax.custom_vjp
def low_back(v):
    return v

def low_keep(v):
    return (low(v), None)

def low_pass(kept, grad):
    return (grad,)

def back_keep(v):
    return (v, None)

def back_low(kept, grad):
    return (low(grad),)
low.defvjp(low_keep, low_pass)
low_back.defvjp(back_keep, back_low)

def ssd_span(carried, pieces):
    span_values, span_steps, span_decay, span_write, span_read = pieces
    cumulative = jnp.cumsum(span_decay, axis=0)
    products = jnp.dot(span_read, span_write.T, precision=lax.Precision.HIGHEST)
    differences = cumulative.T[:, :, None] - cumulative.T[:, None, :]
    row_index = lax.broadcasted_iota(jnp.int32, differences.shape, 1)
    col_index = lax.broadcasted_iota(jnp.int32, differences.shape, 2)
    decays = jnp.exp(jnp.where(row_index >= col_index, differences, -jnp.inf))
    weights = products[None, :, :] * decays * span_steps.T[:, None, :]
    within = jnp.einsum('hij,jhp->ihp', weights, span_values, precision=lax.Precision.HIGHEST)
    from_state = jnp.einsum('in,hnp->ihp', span_read, carried, precision=lax.Precision.HIGHEST)
    from_state = from_state * jnp.exp(cumulative)[:, :, None]
    to_end = jnp.exp(cumulative[-1][None, :] - cumulative) * span_steps
    new_state = jnp.exp(cumulative[-1])[:, None, None] * carried + jnp.einsum('jn,jhp->hnp', span_write, span_values * to_end[:, :, None], precision=lax.Precision.HIGHEST)
    return (new_state, within + from_state)

def ssd(values, step_size, log_decay, write_side, read_side):
    length, head_count, head_dim = values.shape
    span_count = length // SPAN
    pieces = (values.reshape(span_count, SPAN, head_count, head_dim), step_size.reshape(span_count, SPAN, head_count), log_decay.reshape(span_count, SPAN, head_count), write_side.reshape(span_count, SPAN, write_side.shape[1]), read_side.reshape(span_count, SPAN, read_side.shape[1]))
    initial = jnp.zeros((head_count, write_side.shape[1], head_dim), jnp.float32)
    _, outputs = lax.scan(jax.checkpoint(ssd_span), initial, pieces)
    return outputs.reshape(length, head_count, head_dim)

def mixer(x_part, dt_raw, shared_part, conv_w, conv_b, dt_shift, log_rate, skip_w):
    length = x_part.shape[0]
    head_count = dt_raw.shape[1]
    head_width = head_count * HEADDIM
    joined = jnp.concatenate([x_part, shared_part], axis=1)
    padded = jnp.pad(joined, ((CONV - 1, 0), (0, 0)))
    convolved = conv_b[None, :] + jnp.zeros_like(joined)
    for offset in range(CONV):
        convolved = convolved + conv_w[offset][None, :] * padded[offset:offset + length]
    activated = jax.nn.silu(convolved)
    values = activated[:, :head_width].reshape(length, head_count, HEADDIM)
    write_side = activated[:, head_width:head_width + STATE]
    read_side = activated[:, head_width + STATE:]
    step_size = jax.nn.softplus(dt_raw + dt_shift[None, :])
    log_decay = -step_size * jnp.exp(log_rate)[None, :]
    scanned = ssd(values, step_size, log_decay, write_side, read_side)
    return (scanned + skip_w[None, :, None] * values).reshape(length, head_width)

def layer(seq_in, norm_w, in_w, conv_w, conv_b, dt_shift, log_rate, skip_w, gate_w, out_w):
    scaled = seq_in * lax.rsqrt(lax.optimization_barrier(jnp.mean(seq_in * seq_in, axis=-1, keepdims=True)) + norm_eps) * norm_w
    projected = low(low_back(jnp.dot(low(scaled), in_w, precision=lax.Precision.HIGHEST)))
    gate_part = projected[:, :INNER]
    x_part = projected[:, INNER:2 * INNER]
    shared_part = projected[:, 2 * INNER:2 * INNER + 2 * STATE]
    dt_raw = projected[:, 2 * INNER + 2 * STATE:]
    mixed = low_back(low(mixer(x_part, dt_raw, shared_part, conv_w, conv_b, dt_shift, log_rate, skip_w)))
    gated = mixed * jax.nn.silu(gate_part)
    normed = gated * lax.rsqrt(lax.optimization_barrier(jnp.mean(gated * gated, axis=-1, keepdims=True)) + norm_eps) * gate_w
    return seq_in + jnp.dot(low(normed), out_w, precision=lax.Precision.HIGHEST)

def reference(hidden_in, cotangent, norm_gain, in_weight, conv_weight, conv_bias, dt_bias, a_log, skip_gain, gate_gain, out_weight):
    params = (norm_gain.astype(jnp.float32), in_weight.astype(jnp.float32), conv_weight.astype(jnp.float32), conv_bias.astype(jnp.float32), dt_bias.astype(jnp.float32), a_log.astype(jnp.float32), skip_gain.astype(jnp.float32), gate_gain.astype(jnp.float32), out_weight.astype(jnp.float32))

    def one_sequence(totals, pair):
        seq_in, seq_cot = pair
        result, backward = jax.vjp(layer, seq_in.astype(jnp.float32), *params)
        grads = backward(seq_cot.astype(jnp.float32))
        totals = tuple((total + grad for total, grad in zip(totals, grads[1:])))
        return (totals, (result.astype(jnp.bfloat16), grads[0]))
    zeros = tuple((jnp.zeros(param.shape, jnp.float32) for param in params))
    totals, (outputs, grad_inputs) = lax.scan(one_sequence, zeros, (hidden_in, cotangent))
    return (outputs, grad_inputs, totals[0], totals[1], totals[2], totals[3], totals[4], totals[5], totals[6], totals[7], totals[8])
```

```python
import functools

import jax
import jax.numpy as jnp
from jax import lax
from jax.experimental import pallas as pl
from jax.experimental.pallas import tpu as pltpu
from jax.sharding import PartitionSpec as P

HEADDIM = 64
STATE = 128
CONV = 4
HALO = 16
EXTRA = 16
norm_eps = 1e-05
VMEM_BYTES = 56 * 1024 * 1024
f32 = jnp.float32
bf16 = jnp.bfloat16


def exact(a, b, dims):
    return lax.dot_general(
        a, b, (dims, ((), ())), precision=lax.Precision.HIGHEST, preferred_element_type=f32
    )


NN = ((1,), (0,))
TN = ((0,), (0,))
NT = ((1,), (1,))


def iota(shape, dim):
    return lax.broadcasted_iota(jnp.int32, shape, dim)


def spread_matrix(heads):
    shape = (heads, heads * HEADDIM)
    return (iota(shape, 1) // HEADDIM == iota(shape, 0)).astype(f32)


def sigmoid(v):
    return 1.0 / (1.0 + jnp.exp(-v))


def softplus(v):
    return jnp.maximum(v, 0.0) + jnp.log1p(jnp.exp(-jnp.abs(v)))


def whole(shape):
    return pl.BlockSpec(shape, lambda g: (0,) * len(shape))


def per_seq(shape):
    return pl.BlockSpec((1,) + shape, lambda g: (g,) + (0,) * len(shape))


def per_dest(shape):
    return pl.BlockSpec(
        (shape[0], 1) + shape[1:], lambda g: (0, g) + (0,) * (len(shape) - 1)
    )


def call(body, grid, in_specs, out_specs, out_shape, scratch=(), flops=0, moved=0):
    return pl.pallas_call(
        body,
        grid=(grid,),
        in_specs=in_specs,
        out_specs=out_specs,
        out_shape=out_shape,
        scratch_shapes=list(scratch),
        compiler_params=pltpu.CompilerParams(vmem_limit_bytes=VMEM_BYTES),
        cost_estimate=pl.CostEstimate(flops=flops, bytes_accessed=moved, transcendentals=0),
    )


def front_body(dests, p_ref, cw_ref, cb_ref, dtb_ref, al_ref, conv_ref, dt_ref, cum_ref, send_ref, xw_ref):
    length = conv_ref.shape[1]
    channels = conv_ref.shape[2]
    heads = dt_ref.shape[2]
    inner = heads * HEADDIM
    step = softplus(p_ref[0, HALO:, channels : channels + heads].astype(f32) + dtb_ref[...])
    decay = -step * jnp.exp(al_ref[...])
    lower = (iota((length, length), 0) >= iota((length, length), 1)).astype(f32)
    cum = exact(lower, decay, NN)
    dt_ref[0] = step
    cum_ref[0] = cum
    last = cum[length - 1 :, :]
    weight = jnp.exp(last - cum) * step
    spread = spread_matrix(heads)
    weight_wide = exact(weight, spread, NN)
    last_wide = exact(jnp.broadcast_to(last, (8, heads)), spread, NN)[0:1]
    write_side = None
    for start in list(range(inner, channels, 128)) + list(range(0, inner, 128)):
        cols = slice(start, start + 128)
        joined = p_ref[0, :, cols].astype(f32)
        total = cb_ref[:, cols]
        for tap in range(CONV):
            low = HALO - (CONV - 1) + tap
            total = total + cw_ref[tap : tap + 1, cols] * joined[low : low + length]
        conv_ref[0, :, cols] = total
        if start == inner:
            write_side = total * sigmoid(total)
        elif start < inner:
            xw_ref[:, cols] = total * sigmoid(total) * weight_wide[:, cols]
    state = exact(write_side, xw_ref[...], TN)
    width = send_ref.shape[3]
    hi = last_wide.astype(bf16)
    rest = last_wide - hi.astype(f32)
    mid = rest.astype(bf16)
    low_part = (rest - mid.astype(f32)).astype(bf16)
    row = iota((EXTRA, inner), 0)
    tail = jnp.where(
        row == 0,
        hi.astype(f32),
        jnp.where(row == 1, mid.astype(f32), jnp.where(row == 2, low_part.astype(f32), 0.0)),
    )
    for dest in range(dests):
        cols = slice(dest * width, (dest + 1) * width)
        send_ref[dest, 0, :STATE, :] = state[:, cols].astype(send_ref.dtype)
        send_ref[dest, 0, STATE:, :] = tail[:, cols].astype(send_ref.dtype)


def scan_front(p_ext, conv_weight, conv_bias, dt_bias, a_log, dests, kind):
    seqs, rows, _ = p_ext.shape
    length = rows - HALO
    heads = dt_bias.shape[0]
    inner = heads * HEADDIM
    channels = inner + 2 * STATE
    width = inner // dests
    return call(
        functools.partial(front_body, dests),
        seqs,
        [
            per_seq(p_ext.shape[1:]),
            whole((CONV, channels)),
            whole((1, channels)),
            whole((1, heads)),
            whole((1, heads)),
        ],
        [
            per_seq((length, channels)),
            per_seq((length, heads)),
            per_seq((length, heads)),
            per_dest((dests, STATE + EXTRA, width)),
        ],
        [
            jax.ShapeDtypeStruct((seqs, length, channels), f32),
            jax.ShapeDtypeStruct((seqs, length, heads), f32),
            jax.ShapeDtypeStruct((seqs, length, heads), f32),
            jax.ShapeDtypeStruct((dests, seqs, STATE + EXTRA, width), kind),
        ],
        [pltpu.VMEM((length, inner), f32)],
        flops=12 * seqs * length * STATE * inner,
        moved=seqs * length * channels * 6,
    )(p_ext, conv_weight, conv_bias[None], dt_bias[None], a_log[None])


def combine_body(recv_ref, start_ref, decay_ref):
    dests, seqs, _, width = recv_ref.shape
    for seq in range(seqs):
        state = jnp.zeros((STATE, width), f32)
        for src in range(dests):
            start_ref[src, seq] = state.astype(start_ref.dtype)
            total = recv_ref[src, seq, STATE:, :].astype(f32)
            decay = jnp.exp(total[0:1] + total[1:2] + total[2:3])
            decay_ref[src, seq] = jnp.broadcast_to(decay, (8, width))
            state = decay * state + recv_ref[src, seq, :STATE, :].astype(f32)


def combine(recv):
    dests, seqs, _, width = recv.shape
    return pl.pallas_call(
        combine_body,
        out_shape=[
            jax.ShapeDtypeStruct((dests, seqs, STATE, width), recv.dtype),
            jax.ShapeDtypeStruct((dests, seqs, 8, width), f32),
        ],
        compiler_params=pltpu.CompilerParams(vmem_limit_bytes=VMEM_BYTES),
        cost_estimate=pl.CostEstimate(
            flops=2 * recv.size, bytes_accessed=4 * recv.size, transcendentals=0
        ),
    )(recv)


def combine_back_body(recv_ref, decay_ref, end_ref):
    dests, seqs, _, width = recv_ref.shape
    for seq in range(seqs):
        state = jnp.zeros((STATE, width), f32)
        for src in reversed(range(dests)):
            end_ref[src, seq] = state.astype(end_ref.dtype)
            state = decay_ref[src, seq, 0:1] * state + recv_ref[src, seq].astype(f32)


def combine_back(recv, decay):
    return pl.pallas_call(
        combine_back_body,
        out_shape=jax.ShapeDtypeStruct(recv.shape, recv.dtype),
        compiler_params=pltpu.CompilerParams(vmem_limit_bytes=VMEM_BYTES),
        cost_estimate=pl.CostEstimate(
            flops=2 * recv.size, bytes_accessed=4 * recv.size, transcendentals=0
        ),
    )(recv, decay)


def columns(array):
    length = array.shape[0]
    eye = (iota((length, length), 0) == iota((length, length), 1)).astype(f32)
    return exact(array, eye, TN)


def within_body(conv_ref, dt_ref, cum_ref, y_ref):
    length = conv_ref.shape[1]
    heads = dt_ref.shape[2]
    inner = heads * HEADDIM
    write_conv = conv_ref[0, :, inner : inner + STATE]
    read_conv = conv_ref[0, :, inner + STATE :]
    products = exact(read_conv * sigmoid(read_conv), write_conv * sigmoid(write_conv), NT)
    cum = cum_ref[0]
    cum_t = columns(cum)
    dt_wide = exact(dt_ref[0], spread_matrix(heads), NN)
    causal = iota((length, length), 0) >= iota((length, length), 1)
    left = iota((length, 2 * HEADDIM), 1) < HEADDIM
    for pair in range(heads // 2):
        cols = slice(pair * 2 * HEADDIM, (pair + 1) * 2 * HEADDIM)
        conv = conv_ref[0, :, cols]
        scaled = conv * sigmoid(conv) * dt_wide[:, cols]
        parts = []
        for head in (2 * pair, 2 * pair + 1):
            gap = cum[:, head : head + 1] - cum_t[head : head + 1, :]
            weights = jnp.exp(jnp.where(causal, gap, -1e30)) * products
            parts.append(exact(weights, scaled, NN))
        y_ref[0, :, cols] = jnp.where(left, parts[0], parts[1])


def scan_within(conv, dt, cum):
    seqs, length, channels = conv.shape
    heads = dt.shape[2]
    inner = heads * HEADDIM
    return call(
        within_body,
        seqs,
        [per_seq((length, channels)), per_seq((length, heads)), per_seq((length, heads))],
        per_seq((length, inner)),
        jax.ShapeDtypeStruct((seqs, length, inner), f32),
        flops=24 * seqs * length * length * inner,
        moved=seqs * length * channels * 8,
    )(conv, dt, cum)


def middle_body(
    y_ref, conv_ref, cum_ref, start_ref, gate_ref, gain_ref, skip_ref, gn_ref,
    normed_ref, gg_ref, gm_ref, send_ref, gain_part_ref, gs_ref, skip_part_ref, cread_ref,
    state_ref, scan_ref, gated_ref,
):
    length = conv_ref.shape[1]
    heads = cum_ref.shape[2]
    inner = heads * HEADDIM
    dests, _, _, width = start_ref.shape
    for dest in range(dests):
        state_ref[:, dest * width : (dest + 1) * width] = start_ref[dest, 0].astype(f32)
    read_conv = conv_ref[0, :, inner + STATE :]
    read_side = read_conv * sigmoid(read_conv)
    spread = spread_matrix(heads)
    grow = jnp.exp(cum_ref[0])
    grow_wide = exact(grow, spread, NN)
    skip_wide = exact(jnp.broadcast_to(skip_ref[...], (8, heads)), spread, NN)[0:1]
    scan_ref[...] = exact(read_side, state_ref[...], NN) * grow_wide + y_ref[0]
    square = jnp.zeros((length, 128), f32)
    for start in range(0, inner, 128):
        cols = slice(start, start + 128)
        conv = conv_ref[0, :, cols]
        mixed = scan_ref[:, cols] + skip_wide[:, cols] * (conv * sigmoid(conv))
        mixed = mixed.astype(bf16).astype(f32)
        gate = gate_ref[0, :, cols].astype(f32)
        gated = mixed * (gate * sigmoid(gate))
        gated_ref[:, cols] = gated
        square = square + gated * gated
    inv = lax.rsqrt(jnp.sum(square, axis=1, keepdims=True) / inner + norm_eps)
    cross = jnp.zeros((length, 128), f32)
    for start in range(0, inner, 128):
        cols = slice(start, start + 128)
        gated = gated_ref[:, cols]
        grad = gn_ref[0, :, cols]
        unit = gated * inv
        normed_ref[0, :, cols] = (unit * gain_ref[:, cols]).astype(bf16)
        gain_part_ref[0, :, cols] = jnp.sum(grad * unit, axis=0, keepdims=True)
        cross = cross + gated * (grad * gain_ref[:, cols])
    mean = jnp.sum(cross, axis=1, keepdims=True) / inner
    factor = inv * inv * inv * mean
    for start in range(0, inner, 128):
        cols = slice(start, start + 128)
        conv = conv_ref[0, :, cols]
        values = conv * sigmoid(conv)
        scanned = scan_ref[:, cols]
        mixed = (scanned + skip_wide[:, cols] * values).astype(bf16).astype(f32)
        gate = gate_ref[0, :, cols].astype(f32)
        sig = sigmoid(gate)
        grad_gated = inv * (gain_ref[:, cols] * gn_ref[0, :, cols]) - gated_ref[:, cols] * factor
        gg_ref[0, :, cols] = (grad_gated * mixed * (sig * (1.0 + gate * (1.0 - sig)))).astype(bf16)
        grad_low = (grad_gated * (gate * sig)).astype(bf16)
        gm_ref[0, :, cols] = grad_low
        grad_mixed = grad_low.astype(f32)
        scan_ref[:, cols] = scanned * grad_mixed
        skip_part_ref[0, :, cols] = jnp.sum(values * grad_mixed, axis=0, keepdims=True)
        gated_ref[:, cols] = grad_mixed * grow_wide[:, cols]
    gs_ref[0] = exact(scan_ref[...], spread, NT)
    cread_ref[0] = exact(gated_ref[...], state_ref[...], NT)
    back = exact(read_side, gated_ref[...], TN)
    for dest in range(dests):
        send_ref[dest, 0] = back[:, dest * width : (dest + 1) * width].astype(send_ref.dtype)


def middle(y, conv, cum, start, gate, gate_gain, skip_gain, grad_normed):
    seqs, length, channels = conv.shape
    heads = cum.shape[2]
    inner = heads * HEADDIM
    dests, _, _, width = start.shape
    row = per_seq((length, inner))
    line = per_seq((1, inner))
    return call(
        middle_body,
        seqs,
        [
            row,
            per_seq((length, channels)),
            per_seq((length, heads)),
            per_dest((dests, STATE, width)),
            row,
            whole((1, inner)),
            whole((1, heads)),
            row,
        ],
        [
            row, row, row,
            per_dest((dests, STATE, width)),
            line,
            per_seq((length, heads)),
            line,
            per_seq((length, STATE)),
        ],
        [
            jax.ShapeDtypeStruct((seqs, length, inner), bf16),
            jax.ShapeDtypeStruct((seqs, length, inner), bf16),
            jax.ShapeDtypeStruct((seqs, length, inner), bf16),
            jax.ShapeDtypeStruct(start.shape, start.dtype),
            jax.ShapeDtypeStruct((seqs, 1, inner), f32),
            jax.ShapeDtypeStruct((seqs, length, heads), f32),
            jax.ShapeDtypeStruct((seqs, 1, inner), f32),
            jax.ShapeDtypeStruct((seqs, length, STATE), f32),
        ],
        [
            pltpu.VMEM((STATE, inner), f32),
            pltpu.VMEM((length, inner), f32),
            pltpu.VMEM((length, inner), f32),
        ],
        flops=36 * seqs * length * STATE * inner,
        moved=seqs * length * channels * 20,
    )(y, conv, cum, start, gate, gate_gain[None], skip_gain[None], grad_normed)


def within_back_body(conv_ref, dt_ref, cum_ref, gm_ref, cread_ref, u_ref, dw_ref, dr_ref):
    length = conv_ref.shape[1]
    heads = dt_ref.shape[2]
    inner = heads * HEADDIM
    write_conv = conv_ref[0, :, inner : inner + STATE]
    read_conv = conv_ref[0, :, inner + STATE :]
    write_side = write_conv * sigmoid(write_conv)
    read_side = read_conv * sigmoid(read_conv)
    products = exact(write_side, read_side, NT)
    cum = cum_ref[0]
    cum_t = columns(cum)
    dt_wide = exact(dt_ref[0], spread_matrix(heads), NN)
    causal = iota((length, length), 0) <= iota((length, length), 1)
    left = iota((length, 2 * HEADDIM), 1) < HEADDIM
    grad_products = jnp.zeros((length, length), f32)
    for pair in range(heads // 2):
        cols = slice(pair * 2 * HEADDIM, (pair + 1) * 2 * HEADDIM)
        conv = conv_ref[0, :, cols]
        scaled = conv * sigmoid(conv) * dt_wide[:, cols]
        grad = gm_ref[0, :, cols].astype(f32)
        parts = []
        for side, head in enumerate((2 * pair, 2 * pair + 1)):
            gap = cum_t[head : head + 1, :] - cum[:, head : head + 1]
            decays = jnp.exp(jnp.where(causal, gap, -1e30))
            parts.append(exact(decays * products, grad, NN))
            own = jnp.where(left if side == 0 else ~left, scaled, 0.0)
            grad_products = grad_products + decays * exact(own, grad, NT)
        u_ref[0, :, cols] = jnp.where(left, parts[0], parts[1])
    dw_ref[0] = exact(grad_products, read_side, NN)
    dr_ref[0] = exact(grad_products, write_side, TN) + cread_ref[0]


def scan_within_back(conv, dt, cum, grad_mixed, cread):
    seqs, length, channels = conv.shape
    heads = dt.shape[2]
    inner = heads * HEADDIM
    side = per_seq((length, STATE))
    return call(
        within_back_body,
        seqs,
        [
            per_seq((length, channels)),
            per_seq((length, heads)),
            per_seq((length, heads)),
            per_seq((length, inner)),
            side,
        ],
        [per_seq((length, inner)), side, side],
        [
            jax.ShapeDtypeStruct((seqs, length, inner), f32),
            jax.ShapeDtypeStruct((seqs, length, STATE), f32),
            jax.ShapeDtypeStruct((seqs, length, STATE), f32),
        ],
        flops=48 * seqs * length * length * inner,
        moved=seqs * length * channels * 10,
    )(conv, dt, cum, grad_mixed, cread)


def back_body(
    u_ref, dw_ref, dr_ref, conv_ref, p_ref, dt_ref, cum_ref, gm_ref, gs_ref,
    start_ref, end_ref, cw_ref, dtb_ref, al_ref, skip_ref,
    dconv_ref, ddt_ref, cwp_ref, cbp_ref, dtp_ref, alp_ref,
    state_ref, xw_ref, xu_ref, xs_ref,
):
    length = conv_ref.shape[1]
    channels = conv_ref.shape[2]
    heads = dt_ref.shape[2]
    inner = heads * HEADDIM
    dests, _, _, width = start_ref.shape
    spread = spread_matrix(heads)
    step = dt_ref[0]
    cum = cum_ref[0]
    last = cum[length - 1 :, :]
    weight = jnp.exp(last - cum)
    step_wide = exact(step, spread, NN)
    weight_wide = exact(weight, spread, NN)
    skip_wide = exact(jnp.broadcast_to(skip_ref[...], (8, heads)), spread, NN)[0:1]
    inner_sum = []
    for dest in range(dests):
        cols = slice(dest * width, (dest + 1) * width)
        end = end_ref[dest, 0].astype(f32)
        state_ref[:, cols] = end
        inner_sum.append(jnp.sum(end * start_ref[dest, 0].astype(f32), axis=0, keepdims=True))
    inner_sum = jnp.concatenate(inner_sum, axis=1)
    write_conv = conv_ref[0, :, inner : inner + STATE]
    write_side = write_conv * sigmoid(write_conv)
    xs_ref[...] = exact(write_side, state_ref[...], NN) * weight_wide

    def conv_back(start, grad):
        cols = slice(start, start + 128)
        conv = conv_ref[0, :, cols]
        sig = sigmoid(conv)
        dconv = grad * (sig * (1.0 + conv * (1.0 - sig)))
        dconv_ref[0, :, cols] = dconv
        cbp_ref[0, :, cols] = jnp.sum(dconv, axis=0, keepdims=True)
        joined = p_ref[0, :, cols].astype(f32)
        for tap in range(CONV):
            low = HALO - (CONV - 1) + tap
            cwp_ref[0, tap : tap + 1, cols] = jnp.sum(
                dconv * joined[low : low + length], axis=0, keepdims=True
            )

    for start in range(0, inner, 128):
        cols = slice(start, start + 128)
        conv = conv_ref[0, :, cols]
        values = conv * sigmoid(conv)
        from_state = xs_ref[:, cols]
        total = u_ref[0, :, cols] + from_state
        xu_ref[:, cols] = values * total
        xs_ref[:, cols] = values * from_state
        xw_ref[:, cols] = values * (step_wide[:, cols] * weight_wide[:, cols])
        grad = step_wide[:, cols] * total + skip_wide[:, cols] * gm_ref[0, :, cols].astype(f32)
        conv_back(start, grad)
    conv_back(inner, dw_ref[0] + exact(xw_ref[...], state_ref[...], NT))
    conv_back(inner + STATE, dr_ref[0])
    direct = exact(xu_ref[...], spread, NT)
    ends = exact(xs_ref[...], spread, NT) * step
    held = exact(jnp.broadcast_to(inner_sum, (8, inner)), spread, NT)[0:1] * jnp.exp(last)
    at_end = jnp.sum(ends, axis=0, keepdims=True) + held
    dcum = gs_ref[0] - step * direct
    dcum = dcum + jnp.where(iota((length, heads), 0) == length - 1, at_end, 0.0)
    upper = (iota((length, length), 0) <= iota((length, length), 1)).astype(f32)
    da = exact(upper, dcum, NN)
    rate = jnp.exp(al_ref[...])
    alp_ref[0] = jnp.sum(da * (-step * rate), axis=0, keepdims=True)
    raw = p_ref[0, HALO:, channels : channels + heads].astype(f32) + dtb_ref[...]
    draw = (direct - da * rate) * sigmoid(raw)
    ddt_ref[0] = draw.astype(bf16)
    dtp_ref[0] = jnp.sum(draw, axis=0, keepdims=True)


def scan_back(u, dw, dr, conv, p_ext, dt, cum, gm, gs, start, end, conv_weight, dt_bias, a_log, skip_gain):
    seqs, length, channels = conv.shape
    heads = dt.shape[2]
    inner = heads * HEADDIM
    dests, _, _, width = start.shape
    row = per_seq((length, inner))
    small = per_seq((length, heads))
    side = per_seq((length, STATE))
    states = per_dest((dests, STATE, width))
    return call(
        back_body,
        seqs,
        [
            row, side, side,
            per_seq((length, channels)),
            per_seq(p_ext.shape[1:]),
            small, small, row, small, states, states,
            whole((CONV, channels)),
            whole((1, heads)),
            whole((1, heads)),
            whole((1, heads)),
        ],
        [
            per_seq((length, channels)),
            small,
            per_seq((CONV, channels)),
            per_seq((1, channels)),
            per_seq((1, heads)),
            per_seq((1, heads)),
        ],
        [
            jax.ShapeDtypeStruct((seqs, length, channels), f32),
            jax.ShapeDtypeStruct((seqs, length, heads), bf16),
            jax.ShapeDtypeStruct((seqs, CONV, channels), f32),
            jax.ShapeDtypeStruct((seqs, 1, channels), f32),
            jax.ShapeDtypeStruct((seqs, 1, heads), f32),
            jax.ShapeDtypeStruct((seqs, 1, heads), f32),
        ],
        [
            pltpu.VMEM((STATE, inner), f32),
            pltpu.VMEM((length, inner), f32),
            pltpu.VMEM((length, inner), f32),
            pltpu.VMEM((length, inner), f32),
        ],
        flops=24 * seqs * length * STATE * inner,
        moved=seqs * length * channels * 24,
    )(u, dw, dr, conv, p_ext, dt, cum, gm, gs, start, end, conv_weight,
      dt_bias[None], a_log[None], skip_gain[None])


def swap(x, axis, flip):
    count = lax.axis_size(axis)
    return lax.ppermute(x, axis, [(slot, slot ^ flip) for slot in range(count)])


def total_over_all(x):
    for axis in ("seq", "fsdp"):
        flip = 1
        while flip < lax.axis_size(axis):
            x = x + swap(x, axis, flip)
            flip *= 2
    return x


def shared_slots():
    slot = lax.axis_index("seq")
    return slot // 4, slot // 2 % 2 == 1, slot % 2 == 1, lax.axis_index("fsdp") == 1


def fast_mesh():
    return lax.axis_size("fsdp") == 2 and lax.axis_size("seq") == 16


def halves(x, flag, axis):
    size = x.shape[axis] // 2
    low = lax.slice_in_dim(x, 0, size, axis=axis)
    high = lax.slice_in_dim(x, size, 2 * size, axis=axis)
    return jnp.where(flag, high, low), jnp.where(flag, low, high)


def join(own, other, flag, axis):
    low = jnp.where(flag, other, own)
    high = jnp.where(flag, own, other)
    return jnp.concatenate([low, high], axis=axis)


def fetch_rows(w):
    _, _, odd, _ = shared_slots()
    mine, _ = halves(w, odd, 0)
    fetched = swap(mine, "fsdp", 1)
    return fetched, swap(fetched, "seq", 1)


def gather_rows(w):
    if not fast_mesh():
        return lax.all_gather(w, "fsdp", axis=0, tiled=True)
    _, _, odd, second = shared_slots()
    fetched, shared = fetch_rows(w)
    return join(w, join(fetched, shared, odd, 0), second, 0)


def reduce_rows(part):
    shard = lax.psum_scatter(part, "fsdp", scatter_dimension=0, tiled=True)
    return lax.psum(shard, "seq")


def fold(total, axis, flip, dim):
    size = total.shape[dim] // 2
    keep = lax.slice_in_dim(total, 0, size, axis=dim)
    give = lax.slice_in_dim(total, size, 2 * size, axis=dim)
    return keep + swap(give.astype(bf16), axis, flip).astype(f32)


def ring(x, shift):
    return lax.ppermute(x, "seq", [(slot, (slot + 4 * shift) % 16) for slot in range(16)])


def scatter_z(total, z):
    size = total.shape[0] // 4
    mine = lax.dynamic_slice_in_dim(total, z * size, size, 0)
    for shift in range(1, 4):
        give = lax.dynamic_slice_in_dim(total, (z + shift) % 4 * size, size, 0)
        mine = mine + ring(give.astype(bf16), shift).astype(f32)
    return mine


def gather_z(mine, z):
    size = mine.shape[0]
    total = jnp.zeros((4 * size,) + mine.shape[1:], mine.dtype)
    total = lax.dynamic_update_slice_in_dim(total, mine, z * size, 0)
    for shift in range(1, 4):
        total = lax.dynamic_update_slice_in_dim(
            total, ring(mine, shift), (z - shift) % 4 * size, 0
        )
    return total


def spread_total(mine):
    z, x, odd, _ = shared_slots()
    total = gather_z(mine.astype(bf16), z)
    total = join(total, swap(total, "seq", 2), x, 1)
    return join(total, swap(total, "seq", 1), odd, 1)


def dot(a, b, dims):
    return lax.dot_general(a, b, (dims, ((), ())), preferred_element_type=f32)


STATE_TYPE = bf16


def per_device(
    hidden_in, cotangent, norm_gain, in_weight, conv_weight, conv_bias,
    dt_bias, a_log, skip_gain, gate_gain, out_weight,
):
    seq_count = lax.axis_size("seq")
    seqs, length, width = hidden_in.shape
    rows = seqs * length
    heads = dt_bias.shape[0]
    inner = heads * HEADDIM
    forward = [(slot, slot + 1) for slot in range(seq_count - 1)]
    backward = [(slot + 1, slot) for slot in range(seq_count - 1)]

    w_gate, w_scan = in_weight[:, :inner], in_weight[:, inner:]
    halo = lax.ppermute(hidden_in[:, length - HALO :], "seq", forward)
    fast = fast_mesh()
    if fast:
        z, x, odd, second = shared_slots()
        scan_fetched, scan_shared = fetch_rows(w_scan)
    else:
        scan_full = gather_rows(w_scan)

    def prenorm(rows_in):
        inv = lax.rsqrt(jnp.mean(rows_in * rows_in, axis=-1, keepdims=True) + norm_eps)
        return inv, (rows_in * inv * norm_gain).astype(bf16)

    residual = hidden_in.astype(f32)
    inv_rms, scaled_low = prenorm(residual)
    _, scaled_halo = prenorm(halo.astype(f32))
    scaled_ext = jnp.concatenate([scaled_halo, scaled_low], axis=1)
    scaled_low = scaled_low.reshape(rows, width)
    scaled_ext = scaled_ext.reshape(seqs * (HALO + length), width)
    if fast:
        ext_own, ext_other = halves(scaled_ext, second, 1)
        ext_fetched, ext_shared = halves(ext_other, odd, 1)
        p_ext = dot(ext_own, w_scan, NN) + dot(ext_fetched, scan_fetched, NN)
        p_ext = p_ext + dot(ext_shared, scan_shared, NN)
    else:
        p_ext = dot(scaled_ext, scan_full, NN)
    p_ext = p_ext.astype(bf16).reshape(seqs, HALO + length, -1)
    conv, dt, cum, send = scan_front(
        p_ext, conv_weight, conv_bias, dt_bias, a_log, seq_count, STATE_TYPE
    )
    recv = lax.all_to_all(send, "seq", split_axis=0, concat_axis=0, tiled=True)
    w_gate, w_out, _ = lax.optimization_barrier((w_gate, out_weight, p_ext))
    gate_full = gather_rows(w_gate)
    out_full = gather_rows(w_out)
    y = scan_within(conv, dt, cum)
    start_heads, decay = combine(recv)
    start = lax.all_to_all(start_heads, "seq", split_axis=0, concat_axis=0, tiled=True)
    gate = dot(scaled_low, gate_full, NN).astype(bf16).reshape(seqs, length, inner)
    grad_rows = cotangent.reshape(rows, width)
    grad_normed = dot(grad_rows, out_full, NT).reshape(seqs, length, inner)
    normed, grad_gate, grad_mixed, back_send, gain_part, gs, skip_part, cread = middle(
        y, conv, cum, start, gate, gate_gain, skip_gain, grad_normed
    )
    back_recv = lax.all_to_all(back_send, "seq", split_axis=0, concat_axis=0, tiled=True)
    u, dw, dr = scan_within_back(conv, dt, cum, grad_mixed, cread)
    end_heads = combine_back(back_recv, decay)
    end = lax.all_to_all(end_heads, "seq", split_axis=0, concat_axis=0, tiled=True)
    normed = normed.reshape(rows, inner)
    grad_gate = grad_gate.reshape(rows, inner)
    hidden_out = (residual.reshape(rows, width) + dot(normed, out_full, NN)).astype(bf16)
    if fast:
        scan_full = join(w_scan, join(scan_fetched, scan_shared, odd, 0), second, 0)
        own_side, other_side = halves(scaled_low, second, 1)
        quarters = [halves(side, odd, 1) for side in (own_side, other_side)]
        eighths = [[halves(quarter, x, 1) for quarter in pair] for pair in quarters]
        by_y = [
            jnp.concatenate([eighths[y][c][k] for y in (0, 1) for k in (0, 1)], axis=1)
            for c in (0, 1)
        ]
        by_x = [
            jnp.concatenate([eighths[y][c][k] for k in (0, 1) for y in (0, 1)], axis=1)
            for c in (0, 1)
        ]

        def near(left, right):
            keep = dot(left, right[0], TN)
            give = dot(left, right[1], TN).astype(bf16)
            return keep + swap(give, "seq", 1).astype(f32)

        def reduce_y(left):
            total = fold(fold(near(left, by_y), "fsdp", 1, 1), "seq", 2, 1)
            return spread_total(scatter_z(total, z))

        def reduce_x(left):
            total = fold(fold(near(left, by_x), "seq", 2, 1), "fsdp", 1, 1)
            return spread_total(scatter_z(total, z))

        sides = [halves(side, x, 1) for side in halves(grad_rows, odd, 1)]
        cot = [jnp.concatenate(side, axis=1) for side in sides]
        total = near(jnp.concatenate(halves(normed, second, 1), axis=1), cot)
        total = fold(fold(total, "seq", 2, 1), "fsdp", 1, 0)
        out_total = spread_total(scatter_z(total, z)).astype(f32)
        gate_total = reduce_y(grad_gate)
    else:
        out_total = reduce_rows(dot(normed, grad_rows, TN))
        gate_total = reduce_rows(dot(scaled_low, grad_gate, TN))
    dconv, ddt, conv_part, bias_part, shift_part, rate_part = scan_back(
        u, dw, dr, conv, p_ext, dt, cum, grad_mixed, gs, start, end,
        conv_weight, dt_bias, a_log, skip_gain,
    )
    after = lax.ppermute(dconv[:, :8], "seq", backward)
    dconv = jnp.concatenate([dconv, after], axis=1)
    grad_joined = jnp.zeros(conv.shape, f32)
    for tap in range(CONV):
        low = CONV - 1 - tap
        grad_joined = grad_joined + conv_weight[tap] * dconv[:, low : low + length]
    grad_scan = jnp.concatenate([grad_joined.astype(bf16), ddt], axis=2).reshape(rows, -1)
    if fast:
        cut = grad_scan.shape[1] // 64 * 32
        pieces = [gate_total, reduce_y(grad_scan[:, :cut]), reduce_x(grad_scan[:, cut:])]
        in_total = jnp.concatenate(pieces, axis=0).astype(f32).T
    else:
        in_total = jnp.concatenate(
            [gate_total, reduce_rows(dot(scaled_low, grad_scan, TN))], axis=1
        )
    grad_scaled = dot(grad_gate, gate_full, NT) + dot(grad_scan, scan_full, NT)
    residual = residual.reshape(rows, width)
    inv_rms = inv_rms.reshape(rows, 1)
    norm_part = jnp.sum(grad_scaled * residual * inv_rms, axis=0)
    f = norm_gain * grad_scaled
    mean = jnp.mean(residual * f, axis=-1, keepdims=True)
    grad_hidden = (
        grad_rows.astype(f32) + inv_rms * f - residual * (inv_rms * inv_rms * inv_rms * mean)
    )
    skip_heads = jnp.sum(skip_part.reshape(seqs, heads, HEADDIM), axis=(0, 2))
    pieces = [
        norm_part,
        jnp.sum(conv_part, axis=0).reshape(-1),
        jnp.sum(bias_part, axis=(0, 1)),
        jnp.sum(shift_part, axis=(0, 1)),
        jnp.sum(rate_part, axis=(0, 1)),
        skip_heads,
        jnp.sum(gain_part, axis=(0, 1)),
    ]
    sums = total_over_all(jnp.concatenate(pieces))
    parts, at = [], 0
    for piece in pieces:
        parts.append(sums[at : at + piece.shape[0]])
        at += piece.shape[0]
    norm_sum, conv_sum, bias_sum, shift_sum, rate_sum, skip_sum, gain_sum = parts
    return (
        hidden_out.reshape(hidden_in.shape),
        grad_hidden.reshape(hidden_in.shape),
        norm_sum,
        in_total,
        conv_sum.reshape(conv_weight.shape),
        bias_sum,
        shift_sum,
        rate_sum,
        skip_sum,
        gain_sum,
        out_total,
    )


def solution(mesh):
    tokens = P("fsdp", "seq", None)
    weights = P("fsdp", None)
    return jax.shard_map(
        per_device,
        mesh=mesh,
        in_specs=(tokens, tokens, P(), weights, P(), P(), P(), P(), P(), P(), weights),
        out_specs=(tokens, tokens, P(), weights, P(), P(), P(), P(), P(), P(), weights),
        check_vma=False,
    )
```

```python
import functools

import jax
import jax.numpy as jnp
from jax import lax
from jax.experimental import pallas as pl
from jax.experimental.pallas import tpu as pltpu
from jax.sharding import PartitionSpec as P

HEADDIM = 64
STATE = 128
CONV = 4
HALO = 16
EXTRA = 16
norm_eps = 1e-05
VMEM_BYTES = 56 * 1024 * 1024
f32 = jnp.float32
bf16 = jnp.bfloat16


def exact(a, b, dims):
    return lax.dot_general(
        a, b, (dims, ((), ())), precision=lax.Precision.HIGHEST, preferred_element_type=f32
    )


NN = ((1,), (0,))
TN = ((0,), (0,))
NT = ((1,), (1,))


def iota(shape, dim):
    return lax.broadcasted_iota(jnp.int32, shape, dim)


def split(a):
    high = a.astype(bf16)
    return high, (a - high.astype(f32)).astype(bf16)


def mxu(a, b, dims):
    return lax.dot_general(a, b, (dims, ((), ())), preferred_element_type=f32)


def dot3(a, b, dims):
    a_high, a_low = split(a)
    b_high, b_low = split(b)
    return mxu(a_high, b_high, dims) + (mxu(a_high, b_low, dims) + mxu(a_low, b_high, dims))


def dot2(a, b, dims):
    a_high, a_low = split(a)
    return mxu(a_high, b, dims) + mxu(a_low, b, dims)


def spread_matrix(heads):
    shape = (heads, heads * HEADDIM)
    return (iota(shape, 1) // HEADDIM == iota(shape, 0)).astype(f32).astype(bf16)


def widen(a, spread):
    high, low = split(a)
    return mxu(jnp.concatenate([high, low], axis=1), jnp.concatenate([spread, spread], axis=0), NN)


def widen_row(a, spread):
    high, low = split(jnp.broadcast_to(a, (16, a.shape[1])))
    rest = a - high[0:1].astype(f32) - low[0:1].astype(f32)
    rest = jnp.broadcast_to(rest, (16, a.shape[1])).astype(bf16)
    return (mxu(high, spread, NN) + (mxu(low, spread, NN) + mxu(rest, spread, NN)))[0:1]


def sigmoid(v):
    return 1.0 / (1.0 + jnp.exp(-v))


def softplus(v):
    return jnp.maximum(v, 0.0) + jnp.log1p(jnp.exp(-jnp.abs(v)))


def whole(shape):
    return pl.BlockSpec(shape, lambda g: (0,) * len(shape))


def per_seq(shape):
    return pl.BlockSpec((1,) + shape, lambda g: (g,) + (0,) * len(shape))


def per_dest(shape):
    return pl.BlockSpec(
        (shape[0], 1) + shape[1:], lambda g: (0, g) + (0,) * (len(shape) - 1)
    )


def call(body, grid, in_specs, out_specs, out_shape, scratch=(), flops=0, moved=0):
    return pl.pallas_call(
        body,
        grid=(grid,),
        in_specs=in_specs,
        out_specs=out_specs,
        out_shape=out_shape,
        scratch_shapes=list(scratch),
        compiler_params=pltpu.CompilerParams(vmem_limit_bytes=VMEM_BYTES),
        cost_estimate=pl.CostEstimate(flops=flops, bytes_accessed=moved, transcendentals=0),
    )


def front_body(dests, p_ref, cw_ref, cb_ref, dtb_ref, al_ref, conv_ref, dt_ref, cum_ref, send_ref, xw_ref):
    length = conv_ref.shape[1]
    channels = conv_ref.shape[2]
    heads = dt_ref.shape[2]
    inner = heads * HEADDIM
    step = softplus(p_ref[0, HALO:, channels : channels + heads].astype(f32) + dtb_ref[...])
    decay = -step * jnp.exp(al_ref[...])
    lower = (iota((length, length), 0) >= iota((length, length), 1)).astype(f32)
    cum = exact(lower, decay, NN)
    dt_ref[0] = step
    cum_ref[0] = cum
    last = cum[length - 1 :, :]
    weight = jnp.exp(last - cum) * step
    spread = spread_matrix(heads)
    weight_wide = widen(weight, spread)
    last_wide = widen_row(last, spread)
    write_side = None
    for start in list(range(inner, channels, 128)) + list(range(0, inner, 128)):
        cols = slice(start, start + 128)
        joined = p_ref[0, :, cols].astype(f32)
        total = cb_ref[:, cols]
        for tap in range(CONV):
            low = HALO - (CONV - 1) + tap
            total = total + cw_ref[tap : tap + 1, cols] * joined[low : low + length]
        conv_ref[0, :, cols] = total
        if start == inner:
            write_side = total * sigmoid(total)
        elif start < inner:
            xw_ref[:, cols] = total * sigmoid(total) * weight_wide[:, cols]
    state = dot3(write_side, xw_ref[...], TN)
    width = send_ref.shape[3]
    hi = last_wide.astype(bf16)
    rest = last_wide - hi.astype(f32)
    mid = rest.astype(bf16)
    low_part = (rest - mid.astype(f32)).astype(bf16)
    row = iota((EXTRA, inner), 0)
    tail = jnp.where(
        row == 0,
        hi.astype(f32),
        jnp.where(row == 1, mid.astype(f32), jnp.where(row == 2, low_part.astype(f32), 0.0)),
    )
    for dest in range(dests):
        cols = slice(dest * width, (dest + 1) * width)
        send_ref[dest, 0, :STATE, :] = state[:, cols].astype(send_ref.dtype)
        send_ref[dest, 0, STATE:, :] = tail[:, cols].astype(send_ref.dtype)


def scan_front(p_ext, conv_weight, conv_bias, dt_bias, a_log, dests, kind):
    seqs, rows, _ = p_ext.shape
    length = rows - HALO
    heads = dt_bias.shape[0]
    inner = heads * HEADDIM
    channels = inner + 2 * STATE
    width = inner // dests
    return call(
        functools.partial(front_body, dests),
        seqs,
        [
            per_seq(p_ext.shape[1:]),
            whole((CONV, channels)),
            whole((1, channels)),
            whole((1, heads)),
            whole((1, heads)),
        ],
        [
            per_seq((length, channels)),
            per_seq((length, heads)),
            per_seq((length, heads)),
            per_dest((dests, STATE + EXTRA, width)),
        ],
        [
            jax.ShapeDtypeStruct((seqs, length, channels), f32),
            jax.ShapeDtypeStruct((seqs, length, heads), f32),
            jax.ShapeDtypeStruct((seqs, length, heads), f32),
            jax.ShapeDtypeStruct((dests, seqs, STATE + EXTRA, width), kind),
        ],
        [pltpu.VMEM((length, inner), f32)],
        flops=12 * seqs * length * STATE * inner,
        moved=seqs * length * channels * 6,
    )(p_ext, conv_weight, conv_bias[None], dt_bias[None], a_log[None])


def combine_body(recv_ref, start_ref, decay_ref):
    dests, seqs, _, width = recv_ref.shape
    for seq in range(seqs):
        state = jnp.zeros((STATE, width), f32)
        for src in range(dests):
            start_ref[src, seq] = state.astype(start_ref.dtype)
            total = recv_ref[src, seq, STATE:, :].astype(f32)
            decay = jnp.exp(total[0:1] + total[1:2] + total[2:3])
            decay_ref[src, seq] = jnp.broadcast_to(decay, (8, width))
            state = decay * state + recv_ref[src, seq, :STATE, :].astype(f32)


def combine(recv):
    dests, seqs, _, width = recv.shape
    return pl.pallas_call(
        combine_body,
        out_shape=[
            jax.ShapeDtypeStruct((dests, seqs, STATE, width), recv.dtype),
            jax.ShapeDtypeStruct((dests, seqs, 8, width), f32),
        ],
        compiler_params=pltpu.CompilerParams(vmem_limit_bytes=VMEM_BYTES),
        cost_estimate=pl.CostEstimate(
            flops=2 * recv.size, bytes_accessed=4 * recv.size, transcendentals=0
        ),
    )(recv)


def combine_back_body(recv_ref, decay_ref, end_ref):
    dests, seqs, _, width = recv_ref.shape
    for seq in range(seqs):
        state = jnp.zeros((STATE, width), f32)
        for src in reversed(range(dests)):
            end_ref[src, seq] = state.astype(end_ref.dtype)
            state = decay_ref[src, seq, 0:1] * state + recv_ref[src, seq].astype(f32)


def combine_back(recv, decay):
    return pl.pallas_call(
        combine_back_body,
        out_shape=jax.ShapeDtypeStruct(recv.shape, recv.dtype),
        compiler_params=pltpu.CompilerParams(vmem_limit_bytes=VMEM_BYTES),
        cost_estimate=pl.CostEstimate(
            flops=2 * recv.size, bytes_accessed=4 * recv.size, transcendentals=0
        ),
    )(recv, decay)


def columns(array):
    length = array.shape[0]
    eye = (iota((length, length), 0) == iota((length, length), 1)).astype(f32)
    return exact(array, eye, TN)


def within_body(conv_ref, dt_ref, cum_ref, y_ref):
    length = conv_ref.shape[1]
    heads = dt_ref.shape[2]
    inner = heads * HEADDIM
    write_conv = conv_ref[0, :, inner : inner + STATE]
    read_conv = conv_ref[0, :, inner + STATE :]
    products = dot3(read_conv * sigmoid(read_conv), write_conv * sigmoid(write_conv), NT)
    cum = cum_ref[0]
    cum_t = columns(cum)
    dt_wide = widen(dt_ref[0], spread_matrix(heads))
    causal = iota((length, length), 0) >= iota((length, length), 1)
    left = iota((length, 2 * HEADDIM), 1) < HEADDIM
    for pair in range(heads // 2):
        cols = slice(pair * 2 * HEADDIM, (pair + 1) * 2 * HEADDIM)
        conv = conv_ref[0, :, cols]
        scaled = conv * sigmoid(conv) * dt_wide[:, cols]
        terms = []
        for head in (2 * pair, 2 * pair + 1):
            gap = cum[:, head : head + 1] - cum_t[head : head + 1, :]
            terms += split(jnp.exp(jnp.where(causal, gap, -1e30)) * products)
        every = mxu(
            jnp.concatenate(terms, axis=0), jnp.concatenate(split(scaled), axis=1), NN
        )
        high, low = every[:, : 2 * HEADDIM], every[:, 2 * HEADDIM :]
        parts = [
            high[at : at + length] + (low[at : at + length] + high[at + length : at + 2 * length])
            for at in (0, 2 * length)
        ]
        y_ref[0, :, cols] = jnp.where(left, parts[0], parts[1])


def scan_within(conv, dt, cum):
    seqs, length, channels = conv.shape
    heads = dt.shape[2]
    inner = heads * HEADDIM
    return call(
        within_body,
        seqs,
        [per_seq((length, channels)), per_seq((length, heads)), per_seq((length, heads))],
        per_seq((length, inner)),
        jax.ShapeDtypeStruct((seqs, length, inner), f32),
        flops=24 * seqs * length * length * inner,
        moved=seqs * length * channels * 8,
    )(conv, dt, cum)


def middle_body(
    y_ref, conv_ref, cum_ref, start_ref, gate_ref, gain_ref, skip_ref, gn_ref,
    normed_ref, gg_ref, gm_ref, send_ref, gain_part_ref, gs_ref, skip_part_ref, cread_ref,
    state_ref, scan_ref, gated_ref,
):
    length = conv_ref.shape[1]
    heads = cum_ref.shape[2]
    inner = heads * HEADDIM
    dests, _, _, width = start_ref.shape
    for dest in range(dests):
        state_ref[:, dest * width : (dest + 1) * width] = start_ref[dest, 0]
    read_conv = conv_ref[0, :, inner + STATE :]
    read_side = read_conv * sigmoid(read_conv)
    spread = spread_matrix(heads)
    grow = jnp.exp(cum_ref[0])
    grow_wide = widen(grow, spread)
    skip_wide = widen_row(skip_ref[...], spread)
    scan_ref[...] = dot2(read_side, state_ref[...], NN) * grow_wide + y_ref[0]
    square = jnp.zeros((length, 128), f32)
    for start in range(0, inner, 128):
        cols = slice(start, start + 128)
        conv = conv_ref[0, :, cols]
        mixed = scan_ref[:, cols] + skip_wide[:, cols] * (conv * sigmoid(conv))
        mixed = mixed.astype(bf16).astype(f32)
        gate = gate_ref[0, :, cols].astype(f32)
        gated = mixed * (gate * sigmoid(gate))
        gated_ref[:, cols] = gated
        square = square + gated * gated
    inv = lax.rsqrt(jnp.sum(square, axis=1, keepdims=True) / inner + norm_eps)
    cross = jnp.zeros((length, 128), f32)
    for start in range(0, inner, 128):
        cols = slice(start, start + 128)
        gated = gated_ref[:, cols]
        grad = gn_ref[0, :, cols]
        unit = gated * inv
        normed_ref[0, :, cols] = (unit * gain_ref[:, cols]).astype(bf16)
        gain_part_ref[0, :, cols] = jnp.sum(grad * unit, axis=0, keepdims=True)
        cross = cross + gated * (grad * gain_ref[:, cols])
    mean = jnp.sum(cross, axis=1, keepdims=True) / inner
    factor = inv * inv * inv * mean
    for start in range(0, inner, 128):
        cols = slice(start, start + 128)
        conv = conv_ref[0, :, cols]
        values = conv * sigmoid(conv)
        scanned = scan_ref[:, cols]
        mixed = (scanned + skip_wide[:, cols] * values).astype(bf16).astype(f32)
        gate = gate_ref[0, :, cols].astype(f32)
        sig = sigmoid(gate)
        grad_gated = inv * (gain_ref[:, cols] * gn_ref[0, :, cols]) - gated_ref[:, cols] * factor
        gg_ref[0, :, cols] = (grad_gated * mixed * (sig * (1.0 + gate * (1.0 - sig)))).astype(bf16)
        grad_low = (grad_gated * (gate * sig)).astype(bf16)
        gm_ref[0, :, cols] = grad_low
        grad_mixed = grad_low.astype(f32)
        scan_ref[:, cols] = scanned * grad_mixed
        skip_part_ref[0, :, cols] = jnp.sum(values * grad_mixed, axis=0, keepdims=True)
        gated_ref[:, cols] = grad_mixed * grow_wide[:, cols]
    gs_ref[0] = dot2(scan_ref[...], spread, NT)
    cread_ref[0] = dot2(gated_ref[...], state_ref[...], NT)
    back = dot3(read_side, gated_ref[...], TN)
    for dest in range(dests):
        send_ref[dest, 0] = back[:, dest * width : (dest + 1) * width].astype(send_ref.dtype)


def middle(y, conv, cum, start, gate, gate_gain, skip_gain, grad_normed):
    seqs, length, channels = conv.shape
    heads = cum.shape[2]
    inner = heads * HEADDIM
    dests, _, _, width = start.shape
    row = per_seq((length, inner))
    line = per_seq((1, inner))
    return call(
        middle_body,
        seqs,
        [
            row,
            per_seq((length, channels)),
            per_seq((length, heads)),
            per_dest((dests, STATE, width)),
            row,
            whole((1, inner)),
            whole((1, heads)),
            row,
        ],
        [
            row, row, row,
            per_dest((dests, STATE, width)),
            line,
            per_seq((length, heads)),
            line,
            per_seq((length, STATE)),
        ],
        [
            jax.ShapeDtypeStruct((seqs, length, inner), bf16),
            jax.ShapeDtypeStruct((seqs, length, inner), bf16),
            jax.ShapeDtypeStruct((seqs, length, inner), bf16),
            jax.ShapeDtypeStruct(start.shape, start.dtype),
            jax.ShapeDtypeStruct((seqs, 1, inner), f32),
            jax.ShapeDtypeStruct((seqs, length, heads), f32),
            jax.ShapeDtypeStruct((seqs, 1, inner), f32),
            jax.ShapeDtypeStruct((seqs, length, STATE), f32),
        ],
        [
            pltpu.VMEM((STATE, inner), start.dtype),
            pltpu.VMEM((length, inner), f32),
            pltpu.VMEM((length, inner), f32),
        ],
        flops=12 * seqs * length * STATE * inner,
        moved=seqs * length * channels * 20,
    )(y, conv, cum, start, gate, gate_gain[None], skip_gain[None], grad_normed)


def within_back_body(conv_ref, dt_ref, cum_ref, gm_ref, cread_ref, u_ref, dw_ref, dr_ref):
    length = conv_ref.shape[1]
    heads = dt_ref.shape[2]
    inner = heads * HEADDIM
    write_conv = conv_ref[0, :, inner : inner + STATE]
    read_conv = conv_ref[0, :, inner + STATE :]
    write_side = write_conv * sigmoid(write_conv)
    read_side = read_conv * sigmoid(read_conv)
    products = dot3(write_side, read_side, NT)
    cum = cum_ref[0]
    cum_t = columns(cum)
    dt_wide = widen(dt_ref[0], spread_matrix(heads))
    causal = iota((length, length), 0) <= iota((length, length), 1)
    left = iota((length, 2 * HEADDIM), 1) < HEADDIM
    grad_products = jnp.zeros((length, length), f32)
    for pair in range(heads // 2):
        cols = slice(pair * 2 * HEADDIM, (pair + 1) * 2 * HEADDIM)
        conv = conv_ref[0, :, cols]
        scaled = conv * sigmoid(conv) * dt_wide[:, cols]
        grad = gm_ref[0, :, cols]
        terms, own, decays = [], [], []
        for side, head in enumerate((2 * pair, 2 * pair + 1)):
            gap = cum_t[head : head + 1, :] - cum[:, head : head + 1]
            decays.append(jnp.exp(jnp.where(causal, gap, -1e30)))
            terms += split(decays[side] * products)
            own += split(jnp.where(left if side == 0 else ~left, scaled, 0.0))
        every = mxu(jnp.concatenate(terms, axis=0), grad, NN)
        cross = mxu(jnp.concatenate(own, axis=0), grad, NT)
        parts = []
        for side, at in enumerate((0, 2 * length)):
            parts.append(every[at : at + length] + every[at + length : at + 2 * length])
            cross_head = cross[at : at + length] + cross[at + length : at + 2 * length]
            grad_products = grad_products + decays[side] * cross_head
        u_ref[0, :, cols] = jnp.where(left, parts[0], parts[1])
    dw_ref[0] = dot3(grad_products, read_side, NN)
    dr_ref[0] = dot3(grad_products, write_side, TN) + cread_ref[0]


def scan_within_back(conv, dt, cum, grad_mixed, cread):
    seqs, length, channels = conv.shape
    heads = dt.shape[2]
    inner = heads * HEADDIM
    side = per_seq((length, STATE))
    return call(
        within_back_body,
        seqs,
        [
            per_seq((length, channels)),
            per_seq((length, heads)),
            per_seq((length, heads)),
            per_seq((length, inner)),
            side,
        ],
        [per_seq((length, inner)), side, side],
        [
            jax.ShapeDtypeStruct((seqs, length, inner), f32),
            jax.ShapeDtypeStruct((seqs, length, STATE), f32),
            jax.ShapeDtypeStruct((seqs, length, STATE), f32),
        ],
        flops=48 * seqs * length * length * inner,
        moved=seqs * length * channels * 10,
    )(conv, dt, cum, grad_mixed, cread)


def back_body(
    u_ref, dw_ref, dr_ref, conv_ref, p_ref, dt_ref, cum_ref, gm_ref, gs_ref,
    start_ref, end_ref, cw_ref, dtb_ref, al_ref, skip_ref,
    dconv_ref, ddt_ref, cwp_ref, cbp_ref, dtp_ref, alp_ref,
    state_ref, xw_ref, xu_ref, xs_ref,
):
    length = conv_ref.shape[1]
    channels = conv_ref.shape[2]
    heads = dt_ref.shape[2]
    inner = heads * HEADDIM
    dests, _, _, width = start_ref.shape
    spread = spread_matrix(heads)
    step = dt_ref[0]
    cum = cum_ref[0]
    last = cum[length - 1 :, :]
    weight = jnp.exp(last - cum)
    step_wide = widen(step, spread)
    weight_wide = widen(weight, spread)
    skip_wide = widen_row(skip_ref[...], spread)
    inner_sum = []
    for dest in range(dests):
        cols = slice(dest * width, (dest + 1) * width)
        state_ref[:, cols] = end_ref[dest, 0]
        end = end_ref[dest, 0].astype(f32)
        inner_sum.append(jnp.sum(end * start_ref[dest, 0].astype(f32), axis=0, keepdims=True))
    inner_sum = jnp.concatenate(inner_sum, axis=1)
    write_conv = conv_ref[0, :, inner : inner + STATE]
    write_side = write_conv * sigmoid(write_conv)
    xs_ref[...] = dot2(write_side, state_ref[...], NN) * weight_wide

    def conv_back(start, grad):
        cols = slice(start, start + 128)
        conv = conv_ref[0, :, cols]
        sig = sigmoid(conv)
        dconv = grad * (sig * (1.0 + conv * (1.0 - sig)))
        dconv_ref[0, :, cols] = dconv
        cbp_ref[0, :, cols] = jnp.sum(dconv, axis=0, keepdims=True)
        joined = p_ref[0, :, cols].astype(f32)
        for tap in range(CONV):
            low = HALO - (CONV - 1) + tap
            cwp_ref[0, tap : tap + 1, cols] = jnp.sum(
                dconv * joined[low : low + length], axis=0, keepdims=True
            )

    for start in range(0, inner, 128):
        cols = slice(start, start + 128)
        conv = conv_ref[0, :, cols]
        values = conv * sigmoid(conv)
        from_state = xs_ref[:, cols]
        total = u_ref[0, :, cols] + from_state
        xu_ref[:, cols] = values * total
        xs_ref[:, cols] = values * from_state
        xw_ref[:, cols] = values * (step_wide[:, cols] * weight_wide[:, cols])
        grad = step_wide[:, cols] * total + skip_wide[:, cols] * gm_ref[0, :, cols].astype(f32)
        conv_back(start, grad)
    conv_back(inner, dw_ref[0] + dot2(xw_ref[...], state_ref[...], NT))
    conv_back(inner + STATE, dr_ref[0])
    direct = dot2(xu_ref[...], spread, NT)
    ends = dot2(xs_ref[...], spread, NT) * step
    held = dot2(jnp.broadcast_to(inner_sum, (16, inner)), spread, NT)[0:1] * jnp.exp(last)
    at_end = jnp.sum(ends, axis=0, keepdims=True) + held
    dcum = gs_ref[0] - step * direct
    dcum = dcum + jnp.where(iota((length, heads), 0) == length - 1, at_end, 0.0)
    upper = (iota((length, length), 0) <= iota((length, length), 1)).astype(f32)
    da = exact(upper, dcum, NN)
    rate = jnp.exp(al_ref[...])
    alp_ref[0] = jnp.sum(da * (-step * rate), axis=0, keepdims=True)
    raw = p_ref[0, HALO:, channels : channels + heads].astype(f32) + dtb_ref[...]
    draw = (direct - da * rate) * sigmoid(raw)
    ddt_ref[0] = draw.astype(bf16)
    dtp_ref[0] = jnp.sum(draw, axis=0, keepdims=True)


def scan_back(u, dw, dr, conv, p_ext, dt, cum, gm, gs, start, end, conv_weight, dt_bias, a_log, skip_gain):
    seqs, length, channels = conv.shape
    heads = dt.shape[2]
    inner = heads * HEADDIM
    dests, _, _, width = start.shape
    row = per_seq((length, inner))
    small = per_seq((length, heads))
    side = per_seq((length, STATE))
    states = per_dest((dests, STATE, width))
    return call(
        back_body,
        seqs,
        [
            row, side, side,
            per_seq((length, channels)),
            per_seq(p_ext.shape[1:]),
            small, small, row, small, states, states,
            whole((CONV, channels)),
            whole((1, heads)),
            whole((1, heads)),
            whole((1, heads)),
        ],
        [
            per_seq((length, channels)),
            small,
            per_seq((CONV, channels)),
            per_seq((1, channels)),
            per_seq((1, heads)),
            per_seq((1, heads)),
        ],
        [
            jax.ShapeDtypeStruct((seqs, length, channels), f32),
            jax.ShapeDtypeStruct((seqs, length, heads), bf16),
            jax.ShapeDtypeStruct((seqs, CONV, channels), f32),
            jax.ShapeDtypeStruct((seqs, 1, channels), f32),
            jax.ShapeDtypeStruct((seqs, 1, heads), f32),
            jax.ShapeDtypeStruct((seqs, 1, heads), f32),
        ],
        [
            pltpu.VMEM((STATE, inner), end.dtype),
            pltpu.VMEM((length, inner), f32),
            pltpu.VMEM((length, inner), f32),
            pltpu.VMEM((length, inner), f32),
        ],
        flops=10 * seqs * length * STATE * inner,
        moved=seqs * length * channels * 24,
    )(u, dw, dr, conv, p_ext, dt, cum, gm, gs, start, end, conv_weight,
      dt_bias[None], a_log[None], skip_gain[None])


def swap(x, axis, flip):
    count = lax.axis_size(axis)
    return lax.ppermute(x, axis, [(slot, slot ^ flip) for slot in range(count)])


def total_over_all(x):
    for axis in ("seq", "fsdp"):
        flip = 1
        while flip < lax.axis_size(axis):
            x = x + swap(x, axis, flip)
            flip *= 2
    return x


def shared_slots():
    slot = lax.axis_index("seq")
    return slot // 4, slot // 2 % 2 == 1, slot % 2 == 1, lax.axis_index("fsdp") == 1


def fast_mesh():
    return lax.axis_size("fsdp") == 2 and lax.axis_size("seq") == 16


def halves(x, flag, axis):
    size = x.shape[axis] // 2
    low = lax.slice_in_dim(x, 0, size, axis=axis)
    high = lax.slice_in_dim(x, size, 2 * size, axis=axis)
    return jnp.where(flag, high, low), jnp.where(flag, low, high)


def join(own, other, flag, axis):
    low = jnp.where(flag, other, own)
    high = jnp.where(flag, own, other)
    return jnp.concatenate([low, high], axis=axis)


def fetch_rows(w, after=None):
    _, _, odd, _ = shared_slots()
    mine, _ = halves(w, odd, 0)
    fetched = swap(mine, "fsdp", 1)
    if after is not None:
        fetched, _ = lax.optimization_barrier((fetched, after))
    return fetched, swap(fetched, "seq", 1)


def gather_rows(w, after=None):
    if not fast_mesh():
        return lax.all_gather(w, "fsdp", axis=0, tiled=True)
    _, _, odd, second = shared_slots()
    fetched, shared = fetch_rows(w, after)
    return join(w, join(fetched, shared, odd, 0), second, 0)


def reduce_rows(part):
    shard = lax.psum_scatter(part, "fsdp", scatter_dimension=0, tiled=True)
    return lax.psum(shard, "seq")


def fold(total, axis, flip, dim):
    size = total.shape[dim] // 2
    keep = lax.slice_in_dim(total, 0, size, axis=dim)
    give = lax.slice_in_dim(total, size, 2 * size, axis=dim)
    return keep + swap(give.astype(bf16), axis, flip).astype(f32)


def ring(x, shift):
    return lax.ppermute(x, "seq", [(slot, (slot + 4 * shift) % 16) for slot in range(16)])


def scatter_z(total, z):
    size = total.shape[0] // 4
    mine = lax.dynamic_slice_in_dim(total, z * size, size, 0)
    for shift in range(1, 4):
        give = lax.dynamic_slice_in_dim(total, (z + shift) % 4 * size, size, 0)
        mine = mine + ring(give.astype(bf16), shift).astype(f32)
    return mine


def spread_total(mine):
    total = mine.astype(bf16)
    total = jnp.concatenate([total] + [ring(total, shift) for shift in range(1, 4)], axis=0)
    total = jnp.concatenate([total, swap(total, "seq", 2)], axis=1)
    return total, swap(total, "seq", 1)


def place_body(bases, slots_ref, *refs):
    out_ref = refs[-1]
    z, x, core = slots_ref[0], slots_ref[1], slots_ref[2]
    for piece, base in enumerate(bases):
        for side in range(2):
            src = refs[2 * piece + side]
            rows, cols = src.shape[0] // 4, src.shape[1] // 2
            for shift in range(4):
                row = pl.multiple_of(base + lax.rem(z + 4 - shift, 4) * rows, 8)
                for k in range(2):
                    at = lax.rem(core + side, 2) * 2 + lax.rem(x + k, 2)
                    out_ref[pl.ds(row, rows), pl.ds(pl.multiple_of(at * cols, 128), cols)] = src[
                        shift * rows : (shift + 1) * rows, k * cols : (k + 1) * cols
                    ].astype(f32)


def place(slots, pieces, shape):
    bases, flat, base = [], [], 0
    for own, other in pieces:
        bases.append(base)
        base += own.shape[0]
        flat += [own, other]
    return pl.pallas_call(
        functools.partial(place_body, bases),
        in_specs=[pl.BlockSpec(memory_space=pltpu.SMEM)]
        + [pl.BlockSpec(memory_space=pltpu.VMEM)] * len(flat),
        out_specs=pl.BlockSpec(memory_space=pltpu.VMEM),
        out_shape=jax.ShapeDtypeStruct(shape, f32),
        compiler_params=pltpu.CompilerParams(vmem_limit_bytes=VMEM_BYTES),
        cost_estimate=pl.CostEstimate(
            flops=0, bytes_accessed=6 * shape[0] * shape[1], transcendentals=0
        ),
    )(slots, *flat)


def dot(a, b, dims):
    return lax.dot_general(a, b, (dims, ((), ())), preferred_element_type=f32)


STATE_TYPE = bf16


def per_device(
    hidden_in, cotangent, norm_gain, in_weight, conv_weight, conv_bias,
    dt_bias, a_log, skip_gain, gate_gain, out_weight,
):
    seq_count = lax.axis_size("seq")
    seqs, length, width = hidden_in.shape
    rows = seqs * length
    heads = dt_bias.shape[0]
    inner = heads * HEADDIM
    forward = [(slot, slot + 1) for slot in range(seq_count - 1)]
    backward = [(slot + 1, slot) for slot in range(seq_count - 1)]

    w_gate, w_scan = in_weight[:, :inner], in_weight[:, inner:]
    fast = fast_mesh()
    if fast:
        z, x, odd, second = shared_slots()
        scan_fetched, scan_shared = fetch_rows(w_scan)
    else:
        scan_full = gather_rows(w_scan)

    def prenorm(rows_in):
        inv = lax.rsqrt(jnp.mean(rows_in * rows_in, axis=-1, keepdims=True) + norm_eps)
        return inv, (rows_in * inv * norm_gain).astype(bf16)

    residual = hidden_in.astype(f32)
    inv_rms, scaled_low = prenorm(residual)
    halo = lax.optimization_barrier((hidden_in, scaled_low))[0][:, length - HALO :]
    halo = lax.ppermute(halo, "seq", forward)
    _, scaled_halo = prenorm(halo.astype(f32))
    scaled_ext = jnp.concatenate([scaled_halo, scaled_low], axis=1)
    scaled_low = scaled_low.reshape(rows, width)
    scaled_ext = scaled_ext.reshape(seqs * (HALO + length), width)
    if fast:
        ext_own, ext_other = halves(scaled_ext, second, 1)
        ext_fetched, ext_shared = halves(ext_other, odd, 1)
        p_ext = dot(ext_own, w_scan, NN) + dot(ext_fetched, scan_fetched, NN)
        p_ext = p_ext + dot(ext_shared, scan_shared, NN)
    else:
        p_ext = dot(scaled_ext, scan_full, NN)
    p_ext = p_ext.astype(bf16).reshape(seqs, HALO + length, -1)
    conv, dt, cum, send = scan_front(
        p_ext, conv_weight, conv_bias, dt_bias, a_log, seq_count, STATE_TYPE
    )
    recv = lax.all_to_all(send, "seq", split_axis=0, concat_axis=0, tiled=True)
    w_gate, w_out, conv = lax.optimization_barrier((w_gate, out_weight, conv))
    y = scan_within(conv, dt, cum)
    gate_full = gather_rows(w_gate, y)
    out_full = gather_rows(w_out, y)
    start_heads, decay = combine(recv)
    start = lax.all_to_all(start_heads, "seq", split_axis=0, concat_axis=0, tiled=True)
    gate = dot(scaled_low, gate_full, NN).astype(bf16).reshape(seqs, length, inner)
    grad_rows = cotangent.reshape(rows, width)
    grad_normed = dot(grad_rows, out_full, NT).reshape(seqs, length, inner)
    normed, grad_gate, grad_mixed, back_send, gain_part, gs, skip_part, cread = middle(
        y, conv, cum, start, gate, gate_gain, skip_gain, grad_normed
    )
    back_recv = lax.all_to_all(back_send, "seq", split_axis=0, concat_axis=0, tiled=True)
    u, dw, dr = scan_within_back(conv, dt, cum, grad_mixed, cread)
    end_heads = combine_back(back_recv, decay)
    end = lax.all_to_all(end_heads, "seq", split_axis=0, concat_axis=0, tiled=True)
    normed = normed.reshape(rows, inner)
    grad_gate = grad_gate.reshape(rows, inner)
    hidden_out = (residual.reshape(rows, width) + dot(normed, out_full, NN)).astype(bf16)
    if fast:
        scan_full = join(w_scan, join(scan_fetched, scan_shared, odd, 0), second, 0)
        own_side, other_side = halves(scaled_low, second, 1)
        quarters = [halves(side, odd, 1) for side in (own_side, other_side)]
        eighths = [[halves(quarter, x, 1) for quarter in pair] for pair in quarters]
        by_y = [
            jnp.concatenate([eighths[y][c][k] for y in (0, 1) for k in (0, 1)], axis=1)
            for c in (0, 1)
        ]
        by_x = [
            jnp.concatenate([eighths[y][c][k] for k in (0, 1) for y in (0, 1)], axis=1)
            for c in (0, 1)
        ]
        slots = jnp.stack([z, x.astype(jnp.int32), odd.astype(jnp.int32)]).astype(jnp.int32)

        def near(left, right):
            keep = dot(left, right[0], TN)
            give = dot(left, right[1], TN).astype(bf16)
            return keep + swap(give, "seq", 1).astype(f32)

        sides = [halves(side, x, 1) for side in halves(grad_rows, odd, 1)]
        cot = [jnp.concatenate(side, axis=1) for side in sides]
        normed_late, gate_late, _ = lax.optimization_barrier((normed, grad_gate, u))
        total = near(jnp.concatenate(halves(normed_late, second, 1), axis=1), cot)
        out_part = fold(total, "fsdp", 1, 0)
        gate_part = fold(near(gate_late, by_y), "fsdp", 1, 1)
        out_part, gate_part, end = lax.optimization_barrier((out_part, gate_part, end))
        out_pair = spread_total(scatter_z(fold(out_part, "seq", 2, 1), z))
        gate_pair = spread_total(scatter_z(fold(gate_part, "seq", 2, 1), z))
        out_total = place(slots, [out_pair], out_weight.shape)
    else:
        out_total = reduce_rows(dot(normed, grad_rows, TN))
        gate_total = reduce_rows(dot(scaled_low, grad_gate, TN))
    dconv, ddt, conv_part, bias_part, shift_part, rate_part = scan_back(
        u, dw, dr, conv, p_ext, dt, cum, grad_mixed, gs, start, end,
        conv_weight, dt_bias, a_log, skip_gain,
    )
    after = lax.ppermute(dconv[:, :8], "seq", backward)
    dconv = jnp.concatenate([dconv, after], axis=1)
    grad_joined = jnp.zeros(conv.shape, f32)
    for tap in range(CONV):
        low = CONV - 1 - tap
        grad_joined = grad_joined + conv_weight[tap] * dconv[:, low : low + length]
    grad_scan = jnp.concatenate([grad_joined.astype(bf16), ddt], axis=2).reshape(rows, -1)
    if fast:
        cut = grad_scan.shape[1] // 64 * 32
        first = near(grad_scan[:, :cut], by_y)
        rest = near(grad_scan[:, cut:], by_x)
        first = fold(fold(first, "fsdp", 1, 1), "seq", 2, 1)
        rest = fold(fold(rest, "seq", 2, 1), "fsdp", 1, 1)
        pairs = [gate_pair, spread_total(scatter_z(first, z)), spread_total(scatter_z(rest, z))]
        in_total = place(slots, pairs, in_weight.shape[::-1]).T
    else:
        in_total = jnp.concatenate(
            [gate_total, reduce_rows(dot(scaled_low, grad_scan, TN))], axis=1
        )
    grad_scaled = dot(grad_gate, gate_full, NT) + dot(grad_scan, scan_full, NT)
    residual = residual.reshape(rows, width)
    inv_rms = inv_rms.reshape(rows, 1)
    norm_part = jnp.sum(grad_scaled * residual * inv_rms, axis=0)
    f = norm_gain * grad_scaled
    mean = jnp.mean(residual * f, axis=-1, keepdims=True)
    grad_hidden = (
        grad_rows.astype(f32) + inv_rms * f - residual * (inv_rms * inv_rms * inv_rms * mean)
    )
    skip_heads = jnp.sum(skip_part.reshape(seqs, heads, HEADDIM), axis=(0, 2))
    pieces = [
        norm_part,
        jnp.sum(conv_part, axis=0).reshape(-1),
        jnp.sum(bias_part, axis=(0, 1)),
        jnp.sum(shift_part, axis=(0, 1)),
        jnp.sum(rate_part, axis=(0, 1)),
        skip_heads,
        jnp.sum(gain_part, axis=(0, 1)),
    ]
    sums = total_over_all(jnp.concatenate(pieces))
    parts, at = [], 0
    for piece in pieces:
        parts.append(sums[at : at + piece.shape[0]])
        at += piece.shape[0]
    norm_sum, conv_sum, bias_sum, shift_sum, rate_sum, skip_sum, gain_sum = parts
    return (
        hidden_out.reshape(hidden_in.shape),
        grad_hidden.reshape(hidden_in.shape),
        norm_sum,
        in_total,
        conv_sum.reshape(conv_weight.shape),
        bias_sum,
        shift_sum,
        rate_sum,
        skip_sum,
        gain_sum,
        out_total,
    )


def solution(mesh):
    tokens = P("fsdp", "seq", None)
    weights = P("fsdp", None)
    return jax.shard_map(
        per_device,
        mesh=mesh,
        in_specs=(tokens, tokens, P(), weights, P(), P(), P(), P(), P(), P(), weights),
        out_specs=(tokens, tokens, P(), weights, P(), P(), P(), P(), P(), P(), weights),
        check_vma=False,
    )
```

```python
import functools

import jax
import jax.numpy as jnp
from jax import lax
from jax.experimental import pallas as pl
from jax.experimental.pallas import tpu as pltpu
from jax.sharding import PartitionSpec as P

HEADDIM = 64
STATE = 128
CONV = 4
HALO = 16
EXTRA = 16
norm_eps = 1e-05
VMEM_BYTES = 56 * 1024 * 1024
f32 = jnp.float32
bf16 = jnp.bfloat16


def exact(a, b, dims):
    return lax.dot_general(
        a, b, (dims, ((), ())), precision=lax.Precision.HIGHEST, preferred_element_type=f32
    )


NN = ((1,), (0,))
TN = ((0,), (0,))
NT = ((1,), (1,))


def iota(shape, dim):
    return lax.broadcasted_iota(jnp.int32, shape, dim)


def split(a):
    high = a.astype(bf16)
    return high, (a - high.astype(f32)).astype(bf16)


def mxu(a, b, dims):
    return lax.dot_general(a, b, (dims, ((), ())), preferred_element_type=f32)


def dot3(a, b, dims):
    a_high, a_low = split(a)
    b_high, b_low = split(b)
    return mxu(a_high, b_high, dims) + (mxu(a_high, b_low, dims) + mxu(a_low, b_high, dims))


def dot2(a, b, dims):
    a_high, a_low = split(a)
    return mxu(a_high, b, dims) + mxu(a_low, b, dims)


def spread_matrix(heads):
    shape = (heads, heads * HEADDIM)
    return (iota(shape, 1) // HEADDIM == iota(shape, 0)).astype(f32).astype(bf16)


def widen(a, spread):
    high, low = split(a)
    return mxu(jnp.concatenate([high, low], axis=1), jnp.concatenate([spread, spread], axis=0), NN)


def widen_row(a, spread):
    high, low = split(jnp.broadcast_to(a, (16, a.shape[1])))
    rest = a - high[0:1].astype(f32) - low[0:1].astype(f32)
    rest = jnp.broadcast_to(rest, (16, a.shape[1])).astype(bf16)
    return (mxu(high, spread, NN) + (mxu(low, spread, NN) + mxu(rest, spread, NN)))[0:1]


def sigmoid(v):
    return 1.0 / (1.0 + jnp.exp(-v))


def start_sums(ref):
    @pl.when(pl.program_id(0) == 0)
    def _():
        ref[...] = jnp.zeros(ref.shape, f32)


def softplus(v):
    return jnp.maximum(v, 0.0) + jnp.log1p(jnp.exp(-jnp.abs(v)))


def whole(shape):
    return pl.BlockSpec(shape, lambda g: (0,) * len(shape))


def per_seq(shape):
    return pl.BlockSpec((1,) + shape, lambda g: (g,) + (0,) * len(shape))


def per_dest(shape):
    return pl.BlockSpec(
        (shape[0], 1) + shape[1:], lambda g: (0, g) + (0,) * (len(shape) - 1)
    )


def cost(micros):
    return pl.CostEstimate(flops=0, bytes_accessed=int(micros * 3.5e6), transcendentals=0)


def call(body, grid, in_specs, out_specs, out_shape, scratch=(), micros=10):
    return pl.pallas_call(
        body,
        grid=(grid,),
        in_specs=in_specs,
        out_specs=out_specs,
        out_shape=out_shape,
        scratch_shapes=list(scratch),
        compiler_params=pltpu.CompilerParams(vmem_limit_bytes=VMEM_BYTES),
        cost_estimate=cost(micros),
    )


def front_body(dests, p_ref, cw_ref, cb_ref, dtb_ref, al_ref, conv_ref, dt_ref, cum_ref, send_ref, xw_ref):
    length = conv_ref.shape[1]
    channels = conv_ref.shape[2]
    heads = dt_ref.shape[2]
    inner = heads * HEADDIM
    step = softplus(p_ref[0, HALO:, channels : channels + heads].astype(f32) + dtb_ref[...])
    decay = -step * jnp.exp(al_ref[...])
    lower = (iota((length, length), 0) >= iota((length, length), 1)).astype(f32)
    cum = exact(lower, decay, NN)
    dt_ref[0] = step
    cum_ref[0] = cum
    last = cum[length - 1 :, :]
    weight = jnp.exp(last - cum) * step
    spread = spread_matrix(heads)
    weight_wide = widen(weight, spread)
    last_wide = widen_row(last, spread)
    write_side = None
    for start in list(range(inner, channels, 128)) + list(range(0, inner, 128)):
        cols = slice(start, start + 128)
        joined = p_ref[0, :, cols].astype(f32)
        total = cb_ref[:, cols]
        for tap in range(CONV):
            low = HALO - (CONV - 1) + tap
            total = total + cw_ref[tap : tap + 1, cols] * joined[low : low + length]
        conv_ref[0, :, cols] = total
        if start == inner:
            write_side = total * sigmoid(total)
        elif start < inner:
            xw_ref[:, cols] = total * sigmoid(total) * weight_wide[:, cols]
    state = dot3(write_side, xw_ref[...], TN)
    width = send_ref.shape[3]
    hi = last_wide.astype(bf16)
    rest = last_wide - hi.astype(f32)
    mid = rest.astype(bf16)
    low_part = (rest - mid.astype(f32)).astype(bf16)
    row = iota((EXTRA, inner), 0)
    tail = jnp.where(
        row == 0,
        hi.astype(f32),
        jnp.where(row == 1, mid.astype(f32), jnp.where(row == 2, low_part.astype(f32), 0.0)),
    )
    for dest in range(dests):
        cols = slice(dest * width, (dest + 1) * width)
        send_ref[dest, 0, :STATE, :] = state[:, cols].astype(send_ref.dtype)
        send_ref[dest, 0, STATE:, :] = tail[:, cols].astype(send_ref.dtype)


def scan_front(p_ext, conv_weight, conv_bias, dt_bias, a_log, dests, kind):
    seqs, rows, _ = p_ext.shape
    length = rows - HALO
    heads = dt_bias.shape[0]
    inner = heads * HEADDIM
    channels = inner + 2 * STATE
    width = inner // dests
    return call(
        functools.partial(front_body, dests),
        seqs,
        [
            per_seq(p_ext.shape[1:]),
            whole((CONV, channels)),
            whole((1, channels)),
            whole((1, heads)),
            whole((1, heads)),
        ],
        [
            per_seq((length, channels)),
            per_seq((length, heads)),
            per_seq((length, heads)),
            per_dest((dests, STATE + EXTRA, width)),
        ],
        [
            jax.ShapeDtypeStruct((seqs, length, channels), f32),
            jax.ShapeDtypeStruct((seqs, length, heads), f32),
            jax.ShapeDtypeStruct((seqs, length, heads), f32),
            jax.ShapeDtypeStruct((dests, seqs, STATE + EXTRA, width), kind),
        ],
        [pltpu.VMEM((length, inner), f32)],
        micros=9,
    )(p_ext, conv_weight, conv_bias[None], dt_bias[None], a_log[None])


def combine_body(recv_ref, start_ref, decay_ref):
    dests, seqs, _, width = recv_ref.shape
    for seq in range(seqs):
        state = jnp.zeros((STATE, width), f32)
        for src in range(dests):
            start_ref[src, seq] = state.astype(start_ref.dtype)
            total = recv_ref[src, seq, STATE:, :].astype(f32)
            decay = jnp.exp(total[0:1] + total[1:2] + total[2:3])
            decay_ref[src, seq] = jnp.broadcast_to(decay, (8, width))
            state = decay * state + recv_ref[src, seq, :STATE, :].astype(f32)


def combine(recv):
    dests, seqs, _, width = recv.shape
    return pl.pallas_call(
        combine_body,
        out_shape=[
            jax.ShapeDtypeStruct((dests, seqs, STATE, width), recv.dtype),
            jax.ShapeDtypeStruct((dests, seqs, 8, width), f32),
        ],
        compiler_params=pltpu.CompilerParams(vmem_limit_bytes=VMEM_BYTES),
        cost_estimate=cost(2.5),
    )(recv)


def combine_back_body(recv_ref, decay_ref, end_ref):
    dests, seqs, _, width = recv_ref.shape
    for seq in range(seqs):
        state = jnp.zeros((STATE, width), f32)
        for src in reversed(range(dests)):
            end_ref[src, seq] = state.astype(end_ref.dtype)
            state = decay_ref[src, seq, 0:1] * state + recv_ref[src, seq].astype(f32)


def combine_back(recv, decay):
    return pl.pallas_call(
        combine_back_body,
        out_shape=jax.ShapeDtypeStruct(recv.shape, recv.dtype),
        compiler_params=pltpu.CompilerParams(vmem_limit_bytes=VMEM_BYTES),
        cost_estimate=cost(2.5),
    )(recv, decay)


def columns(array):
    length = array.shape[0]
    eye = (iota((length, length), 0) == iota((length, length), 1)).astype(f32)
    return exact(array, eye, TN)


def within_body(conv_ref, dt_ref, cum_ref, y_ref):
    length = conv_ref.shape[1]
    heads = dt_ref.shape[2]
    inner = heads * HEADDIM
    write_conv = conv_ref[0, :, inner : inner + STATE]
    read_conv = conv_ref[0, :, inner + STATE :]
    products = dot3(read_conv * sigmoid(read_conv), write_conv * sigmoid(write_conv), NT)
    cum = cum_ref[0]
    cum_t = columns(cum)
    dt_wide = widen(dt_ref[0], spread_matrix(heads))
    causal = iota((length, length), 0) >= iota((length, length), 1)
    left = iota((length, 2 * HEADDIM), 1) < HEADDIM
    for pair in range(heads // 2):
        cols = slice(pair * 2 * HEADDIM, (pair + 1) * 2 * HEADDIM)
        conv = conv_ref[0, :, cols]
        scaled = conv * sigmoid(conv) * dt_wide[:, cols]
        terms = []
        for head in (2 * pair, 2 * pair + 1):
            gap = cum[:, head : head + 1] - cum_t[head : head + 1, :]
            terms += split(jnp.exp(jnp.where(causal, gap, -1e30)) * products)
        every = mxu(
            jnp.concatenate(terms, axis=0), jnp.concatenate(split(scaled), axis=1), NN
        )
        high, low = every[:, : 2 * HEADDIM], every[:, 2 * HEADDIM :]
        parts = [
            high[at : at + length] + (low[at : at + length] + high[at + length : at + 2 * length])
            for at in (0, 2 * length)
        ]
        y_ref[0, :, cols] = jnp.where(left, parts[0], parts[1])


def scan_within(conv, dt, cum):
    seqs, length, channels = conv.shape
    heads = dt.shape[2]
    inner = heads * HEADDIM
    return call(
        within_body,
        seqs,
        [per_seq((length, channels)), per_seq((length, heads)), per_seq((length, heads))],
        per_seq((length, inner)),
        jax.ShapeDtypeStruct((seqs, length, inner), f32),
        micros=9,
    )(conv, dt, cum)


def middle_body(
    y_ref, conv_ref, cum_ref, start_ref, gate_ref, gain_ref, skip_ref, gn_ref,
    normed_ref, gg_ref, gm_ref, send_ref, sums_ref, gs_ref, cread_ref,
    state_ref, scan_ref, gated_ref,
):
    length = conv_ref.shape[1]
    heads = cum_ref.shape[2]
    inner = heads * HEADDIM
    dests, _, _, width = start_ref.shape
    for dest in range(dests):
        state_ref[:, dest * width : (dest + 1) * width] = start_ref[dest, 0]
    read_conv = conv_ref[0, :, inner + STATE :]
    read_side = read_conv * sigmoid(read_conv)
    spread = spread_matrix(heads)
    grow = jnp.exp(cum_ref[0])
    grow_wide = widen(grow, spread)
    skip_wide = widen_row(skip_ref[...], spread)
    scan_ref[...] = dot2(read_side, state_ref[...], NN) * grow_wide + y_ref[0]
    start_sums(sums_ref)
    square = jnp.zeros((length, 128), f32)
    for start in range(0, inner, 128):
        cols = slice(start, start + 128)
        conv = conv_ref[0, :, cols]
        mixed = scan_ref[:, cols] + skip_wide[:, cols] * (conv * sigmoid(conv))
        mixed = mixed.astype(bf16).astype(f32)
        gate = gate_ref[0, :, cols].astype(f32)
        gated = mixed * (gate * sigmoid(gate))
        gated_ref[:, cols] = gated
        square = square + gated * gated
    inv = lax.rsqrt(jnp.sum(square, axis=1, keepdims=True) / inner + norm_eps)
    cross = jnp.zeros((length, 128), f32)
    for start in range(0, inner, 128):
        cols = slice(start, start + 128)
        gated = gated_ref[:, cols]
        grad = gn_ref[0, :, cols]
        unit = gated * inv
        normed_ref[0, :, cols] = (unit * gain_ref[:, cols]).astype(bf16)
        sums_ref[0:1, cols] += jnp.sum(grad * unit, axis=0, keepdims=True)
        cross = cross + gated * (grad * gain_ref[:, cols])
    mean = jnp.sum(cross, axis=1, keepdims=True) / inner
    factor = inv * inv * inv * mean
    for start in range(0, inner, 128):
        cols = slice(start, start + 128)
        conv = conv_ref[0, :, cols]
        values = conv * sigmoid(conv)
        scanned = scan_ref[:, cols]
        mixed = (scanned + skip_wide[:, cols] * values).astype(bf16).astype(f32)
        gate = gate_ref[0, :, cols].astype(f32)
        sig = sigmoid(gate)
        grad_gated = inv * (gain_ref[:, cols] * gn_ref[0, :, cols]) - gated_ref[:, cols] * factor
        gg_ref[0, :, cols] = (grad_gated * mixed * (sig * (1.0 + gate * (1.0 - sig)))).astype(bf16)
        grad_low = (grad_gated * (gate * sig)).astype(bf16)
        gm_ref[0, :, cols] = grad_low
        grad_mixed = grad_low.astype(f32)
        scan_ref[:, cols] = scanned * grad_mixed
        sums_ref[1:2, cols] += jnp.sum(values * grad_mixed, axis=0, keepdims=True)
        gated_ref[:, cols] = grad_mixed * grow_wide[:, cols]
    gs_ref[0] = dot2(scan_ref[...], spread, NT)
    cread_ref[0] = dot2(gated_ref[...], state_ref[...], NT)
    back = dot3(read_side, gated_ref[...], TN)
    for dest in range(dests):
        send_ref[dest, 0] = back[:, dest * width : (dest + 1) * width].astype(send_ref.dtype)


def middle(y, conv, cum, start, gate, gate_gain, skip_gain, grad_normed):
    seqs, length, channels = conv.shape
    heads = cum.shape[2]
    inner = heads * HEADDIM
    dests, _, _, width = start.shape
    row = per_seq((length, inner))
    return call(
        middle_body,
        seqs,
        [
            row,
            per_seq((length, channels)),
            per_seq((length, heads)),
            per_dest((dests, STATE, width)),
            row,
            whole((1, inner)),
            whole((1, heads)),
            row,
        ],
        [
            row, row, row,
            per_dest((dests, STATE, width)),
            whole((8, inner)),
            per_seq((length, heads)),
            per_seq((length, STATE)),
        ],
        [
            jax.ShapeDtypeStruct((seqs, length, inner), bf16),
            jax.ShapeDtypeStruct((seqs, length, inner), bf16),
            jax.ShapeDtypeStruct((seqs, length, inner), bf16),
            jax.ShapeDtypeStruct(start.shape, start.dtype),
            jax.ShapeDtypeStruct((8, inner), f32),
            jax.ShapeDtypeStruct((seqs, length, heads), f32),
            jax.ShapeDtypeStruct((seqs, length, STATE), f32),
        ],
        [
            pltpu.VMEM((STATE, inner), start.dtype),
            pltpu.VMEM((length, inner), f32),
            pltpu.VMEM((length, inner), f32),
        ],
        micros=14,
    )(y, conv, cum, start, gate, gate_gain[None], skip_gain[None], grad_normed)


def within_back_body(conv_ref, dt_ref, cum_ref, gm_ref, cread_ref, u_ref, dw_ref, dr_ref):
    length = conv_ref.shape[1]
    heads = dt_ref.shape[2]
    inner = heads * HEADDIM
    write_conv = conv_ref[0, :, inner : inner + STATE]
    read_conv = conv_ref[0, :, inner + STATE :]
    write_side = write_conv * sigmoid(write_conv)
    read_side = read_conv * sigmoid(read_conv)
    products = dot3(write_side, read_side, NT)
    cum = cum_ref[0]
    cum_t = columns(cum)
    dt_wide = widen(dt_ref[0], spread_matrix(heads))
    causal = iota((length, length), 0) <= iota((length, length), 1)
    left = iota((length, 2 * HEADDIM), 1) < HEADDIM
    grad_products = jnp.zeros((length, length), f32)
    for pair in range(heads // 2):
        cols = slice(pair * 2 * HEADDIM, (pair + 1) * 2 * HEADDIM)
        conv = conv_ref[0, :, cols]
        scaled = conv * sigmoid(conv) * dt_wide[:, cols]
        grad = gm_ref[0, :, cols]
        terms, own, decays = [], [], []
        for side, head in enumerate((2 * pair, 2 * pair + 1)):
            gap = cum_t[head : head + 1, :] - cum[:, head : head + 1]
            decays.append(jnp.exp(jnp.where(causal, gap, -1e30)))
            terms += split(decays[side] * products)
            own += split(jnp.where(left if side == 0 else ~left, scaled, 0.0))
        every = mxu(jnp.concatenate(terms, axis=0), grad, NN)
        cross = mxu(jnp.concatenate(own, axis=0), grad, NT)
        parts = []
        for side, at in enumerate((0, 2 * length)):
            parts.append(every[at : at + length] + every[at + length : at + 2 * length])
            cross_head = cross[at : at + length] + cross[at + length : at + 2 * length]
            grad_products = grad_products + decays[side] * cross_head
        u_ref[0, :, cols] = jnp.where(left, parts[0], parts[1])
    dw_ref[0] = dot3(grad_products, read_side, NN)
    dr_ref[0] = dot3(grad_products, write_side, TN) + cread_ref[0]


def scan_within_back(conv, dt, cum, grad_mixed, cread):
    seqs, length, channels = conv.shape
    heads = dt.shape[2]
    inner = heads * HEADDIM
    side = per_seq((length, STATE))
    return call(
        within_back_body,
        seqs,
        [
            per_seq((length, channels)),
            per_seq((length, heads)),
            per_seq((length, heads)),
            per_seq((length, inner)),
            side,
        ],
        [per_seq((length, inner)), side, side],
        [
            jax.ShapeDtypeStruct((seqs, length, inner), f32),
            jax.ShapeDtypeStruct((seqs, length, STATE), f32),
            jax.ShapeDtypeStruct((seqs, length, STATE), f32),
        ],
        micros=14,
    )(conv, dt, cum, grad_mixed, cread)


def back_body(
    u_ref, dw_ref, dr_ref, conv_ref, p_ref, dt_ref, cum_ref, gm_ref, gs_ref,
    start_ref, end_ref, cw_ref, dtb_ref, al_ref, skip_ref,
    grad_ref, head_ref, tail_ref, sums_ref,
    state_ref, xw_ref, xu_ref, xs_ref,
):
    length = conv_ref.shape[1]
    channels = conv_ref.shape[2]
    heads = dt_ref.shape[2]
    inner = heads * HEADDIM
    dests, _, _, width = start_ref.shape
    spread = spread_matrix(heads)
    step = dt_ref[0]
    cum = cum_ref[0]
    last = cum[length - 1 :, :]
    weight = jnp.exp(last - cum)
    step_wide = widen(step, spread)
    weight_wide = widen(weight, spread)
    skip_wide = widen_row(skip_ref[...], spread)
    inner_sum = []
    for dest in range(dests):
        cols = slice(dest * width, (dest + 1) * width)
        state_ref[:, cols] = end_ref[dest, 0]
        end = end_ref[dest, 0].astype(f32)
        inner_sum.append(jnp.sum(end * start_ref[dest, 0].astype(f32), axis=0, keepdims=True))
    inner_sum = jnp.concatenate(inner_sum, axis=1)
    write_conv = conv_ref[0, :, inner : inner + STATE]
    write_side = write_conv * sigmoid(write_conv)
    xs_ref[...] = dot2(write_side, state_ref[...], NN) * weight_wide

    start_sums(sums_ref)

    def conv_back(start, grad):
        cols = slice(start, start + 128)
        conv = conv_ref[0, :, cols]
        sig = sigmoid(conv)
        dconv = grad * (sig * (1.0 + conv * (1.0 - sig)))
        sums_ref[CONV : CONV + 1, cols] += jnp.sum(dconv, axis=0, keepdims=True)
        joined = p_ref[0, :, cols].astype(f32)
        padded = jnp.concatenate([dconv, jnp.zeros((8, 128), f32)], axis=0)
        grad_joined = cw_ref[CONV - 1 : CONV, cols] * dconv
        for tap in range(CONV):
            low = HALO - (CONV - 1) + tap
            sums_ref[tap : tap + 1, cols] += jnp.sum(
                dconv * joined[low : low + length], axis=0, keepdims=True
            )
            if tap < CONV - 1:
                low = CONV - 1 - tap
                grad_joined = grad_joined + cw_ref[tap : tap + 1, cols] * padded[low : low + length]
        grad_ref[0, :, cols] = grad_joined.astype(bf16)
        head_ref[0, :, cols] = dconv[:8]
        tail_ref[0, :, cols] = grad_joined[length - 8 :]

    for start in range(0, inner, 128):
        cols = slice(start, start + 128)
        conv = conv_ref[0, :, cols]
        values = conv * sigmoid(conv)
        from_state = xs_ref[:, cols]
        total = u_ref[0, :, cols] + from_state
        xu_ref[:, cols] = values * total
        xs_ref[:, cols] = values * from_state
        xw_ref[:, cols] = values * (step_wide[:, cols] * weight_wide[:, cols])
        grad = step_wide[:, cols] * total + skip_wide[:, cols] * gm_ref[0, :, cols].astype(f32)
        conv_back(start, grad)
    conv_back(inner, dw_ref[0] + dot2(xw_ref[...], state_ref[...], NT))
    conv_back(inner + STATE, dr_ref[0])
    direct = dot2(xu_ref[...], spread, NT)
    ends = dot2(xs_ref[...], spread, NT) * step
    held = dot2(jnp.broadcast_to(inner_sum, (16, inner)), spread, NT)[0:1] * jnp.exp(last)
    at_end = jnp.sum(ends, axis=0, keepdims=True) + held
    dcum = gs_ref[0] - step * direct
    dcum = dcum + jnp.where(iota((length, heads), 0) == length - 1, at_end, 0.0)
    upper = (iota((length, length), 0) <= iota((length, length), 1)).astype(f32)
    da = exact(upper, dcum, NN)
    rate = jnp.exp(al_ref[...])
    sums_ref[CONV + 2 : CONV + 3, :heads] += jnp.sum(da * (-step * rate), axis=0, keepdims=True)
    raw = p_ref[0, HALO:, channels : channels + heads].astype(f32) + dtb_ref[...]
    draw = (direct - da * rate) * sigmoid(raw)
    grad_ref[0, :, channels:] = draw.astype(bf16)
    sums_ref[CONV + 1 : CONV + 2, :heads] += jnp.sum(draw, axis=0, keepdims=True)


def scan_back(u, dw, dr, conv, p_ext, dt, cum, gm, gs, start, end, conv_weight, dt_bias, a_log, skip_gain):
    seqs, length, channels = conv.shape
    heads = dt.shape[2]
    inner = heads * HEADDIM
    dests, _, _, width = start.shape
    row = per_seq((length, inner))
    small = per_seq((length, heads))
    side = per_seq((length, STATE))
    states = per_dest((dests, STATE, width))
    return call(
        back_body,
        seqs,
        [
            row, side, side,
            per_seq((length, channels)),
            per_seq(p_ext.shape[1:]),
            small, small, row, small, states, states,
            whole((CONV, channels)),
            whole((1, heads)),
            whole((1, heads)),
            whole((1, heads)),
        ],
        [
            per_seq((length, channels + heads)),
            per_seq((8, channels)),
            per_seq((8, channels)),
            whole((8, channels)),
        ],
        [
            jax.ShapeDtypeStruct((seqs, length, channels + heads), bf16),
            jax.ShapeDtypeStruct((seqs, 8, channels), f32),
            jax.ShapeDtypeStruct((seqs, 8, channels), f32),
            jax.ShapeDtypeStruct((8, channels), f32),
        ],
        [
            pltpu.VMEM((STATE, inner), end.dtype),
            pltpu.VMEM((length, inner), f32),
            pltpu.VMEM((length, inner), f32),
            pltpu.VMEM((length, inner), f32),
        ],
        micros=14,
    )(u, dw, dr, conv, p_ext, dt, cum, gm, gs, start, end, conv_weight,
      dt_bias[None], a_log[None], skip_gain[None])


def swap(x, axis, flip):
    count = lax.axis_size(axis)
    return lax.ppermute(x, axis, [(slot, slot ^ flip) for slot in range(count)])


def total_over_all(x):
    for axis in ("seq", "fsdp"):
        flip = 1
        while flip < lax.axis_size(axis):
            x = x + swap(x, axis, flip)
            flip *= 2
    return x


def shared_slots():
    slot = lax.axis_index("seq")
    return slot // 4, slot // 2 % 2 == 1, slot % 2 == 1, lax.axis_index("fsdp") == 1


def fast_mesh():
    return lax.axis_size("fsdp") == 2 and lax.axis_size("seq") == 16


def halves(x, flag, axis):
    size = x.shape[axis] // 2
    low = lax.slice_in_dim(x, 0, size, axis=axis)
    high = lax.slice_in_dim(x, size, 2 * size, axis=axis)
    return jnp.where(flag, high, low), jnp.where(flag, low, high)


def join(own, other, flag, axis):
    low = jnp.where(flag, other, own)
    high = jnp.where(flag, own, other)
    return jnp.concatenate([low, high], axis=axis)


def after(x, *others):
    return lax.optimization_barrier((x,) + others)[0]


def fetch_rows(w, late=None):
    _, _, odd, _ = shared_slots()
    mine, _ = halves(w, odd, 0)
    fetched = swap(mine, "fsdp", 1)
    if late is not None:
        fetched = after(fetched, late)
    return fetched, swap(fetched, "seq", 1)


def gather_rows(w, late=None):
    if not fast_mesh():
        return lax.all_gather(w, "fsdp", axis=0, tiled=True)
    _, _, odd, second = shared_slots()
    fetched, shared = fetch_rows(w, late)
    return join(w, join(fetched, shared, odd, 0), second, 0)


def reduce_rows(part):
    shard = lax.psum_scatter(part, "fsdp", scatter_dimension=0, tiled=True)
    return lax.psum(shard, "seq")


def send_half(total, axis, flip, dim):
    size = total.shape[dim] // 2
    keep = lax.slice_in_dim(total, 0, size, axis=dim)
    give = lax.slice_in_dim(total, size, 2 * size, axis=dim)
    return keep, swap(give.astype(bf16), axis, flip)


def take(sent, *others):
    keep, *got = sent
    for piece in got:
        keep = keep + after(piece, *others).astype(f32) if others else keep + piece.astype(f32)
    return keep


def ring(x, shift):
    return lax.ppermute(x, "seq", [(slot, (slot + 4 * shift) % 16) for slot in range(16)])


def send_z(total, z):
    size = total.shape[0] // 4
    sent = [lax.dynamic_slice_in_dim(total, z * size, size, 0)]
    for shift in range(1, 4):
        give = lax.dynamic_slice_in_dim(total, (z + shift) % 4 * size, size, 0)
        sent.append(ring(give.astype(bf16), shift))
    return sent


def gather_z(mine):
    mine = mine.astype(bf16)
    return jnp.concatenate([mine] + [ring(mine, shift) for shift in range(1, 4)], axis=0)


def gather_columns(total, *others):
    if others:
        total = after(total, *others)
    total = jnp.concatenate([total, swap(total, "seq", 2)], axis=1)
    return total, swap(total, "seq", 1)


def place_body(bases, slots_ref, *refs):
    out_ref = refs[-1]
    z, x, core = slots_ref[0], slots_ref[1], slots_ref[2]
    for piece, base in enumerate(bases):
        for side in range(2):
            src = refs[2 * piece + side]
            rows, cols = src.shape[0] // 4, src.shape[1] // 2
            for shift in range(4):
                row = pl.multiple_of(base + lax.rem(z + 4 - shift, 4) * rows, 8)
                for k in range(2):
                    at = lax.rem(core + side, 2) * 2 + lax.rem(x + k, 2)
                    out_ref[pl.ds(row, rows), pl.ds(pl.multiple_of(at * cols, 128), cols)] = src[
                        shift * rows : (shift + 1) * rows, k * cols : (k + 1) * cols
                    ].astype(f32)


def place(slots, pieces, shape):
    bases, flat, base = [], [], 0
    for own, other in pieces:
        bases.append(base)
        base += own.shape[0]
        flat += [own, other]
    return pl.pallas_call(
        functools.partial(place_body, bases),
        in_specs=[pl.BlockSpec(memory_space=pltpu.SMEM)]
        + [pl.BlockSpec(memory_space=pltpu.VMEM)] * len(flat),
        out_specs=pl.BlockSpec(memory_space=pltpu.VMEM),
        out_shape=jax.ShapeDtypeStruct(shape, f32),
        compiler_params=pltpu.CompilerParams(vmem_limit_bytes=VMEM_BYTES),
        cost_estimate=cost(6),
    )(slots, *flat)


def dot(a, b, dims):
    return lax.dot_general(a, b, (dims, ((), ())), preferred_element_type=f32)


STATE_TYPE = bf16


def per_device(
    hidden_in, cotangent, norm_gain, in_weight, conv_weight, conv_bias,
    dt_bias, a_log, skip_gain, gate_gain, out_weight,
):
    seq_count = lax.axis_size("seq")
    seqs, length, width = hidden_in.shape
    rows = seqs * length
    heads = dt_bias.shape[0]
    inner = heads * HEADDIM
    forward = [(slot, slot + 1) for slot in range(seq_count - 1)]
    backward = [(slot + 1, slot) for slot in range(seq_count - 1)]

    w_gate, w_scan = in_weight[:, :inner], in_weight[:, inner:]
    fast = fast_mesh()
    if fast:
        z, x, odd, second = shared_slots()
        scan_fetched, scan_shared = fetch_rows(w_scan)
    else:
        scan_full = gather_rows(w_scan)

    def prenorm(rows_in):
        inv = lax.rsqrt(jnp.mean(rows_in * rows_in, axis=-1, keepdims=True) + norm_eps)
        return inv, (rows_in * inv * norm_gain).astype(bf16)

    residual = hidden_in.astype(f32)
    inv_rms, scaled_low = prenorm(residual)
    halo = lax.optimization_barrier((hidden_in, scaled_low))[0][:, length - HALO :]
    halo = lax.ppermute(halo, "seq", forward)
    _, scaled_halo = prenorm(halo.astype(f32))
    scaled_ext = jnp.concatenate([scaled_halo, scaled_low], axis=1)
    scaled_low = scaled_low.reshape(rows, width)
    scaled_ext = scaled_ext.reshape(seqs * (HALO + length), width)
    if fast:
        ext_own, ext_other = halves(scaled_ext, second, 1)
        ext_fetched, ext_shared = halves(ext_other, odd, 1)
        p_ext = dot(ext_own, w_scan, NN) + dot(ext_fetched, scan_fetched, NN)
        p_ext = p_ext + dot(ext_shared, scan_shared, NN)
    else:
        p_ext = dot(scaled_ext, scan_full, NN)
    p_ext = p_ext.astype(bf16).reshape(seqs, HALO + length, -1)
    conv, dt, cum, send = scan_front(
        p_ext, conv_weight, conv_bias, dt_bias, a_log, seq_count, STATE_TYPE
    )
    recv = lax.all_to_all(send, "seq", split_axis=0, concat_axis=0, tiled=True)
    w_gate, w_out = after(w_gate, conv), after(out_weight, conv)
    y = scan_within(conv, dt, cum)
    start_heads, decay = combine(recv)
    gate_full = gather_rows(w_gate, start_heads)
    out_full = gather_rows(w_out, start_heads)
    start = lax.all_to_all(start_heads, "seq", split_axis=0, concat_axis=0, tiled=True)
    gate = dot(scaled_low, gate_full, NN).astype(bf16).reshape(seqs, length, inner)
    grad_rows = cotangent.reshape(rows, width)
    grad_normed = dot(grad_rows, out_full, NT).reshape(seqs, length, inner)
    normed, grad_gate, grad_mixed, back_send, gate_sums, gs, cread = middle(
        y, conv, cum, start, gate, gate_gain, skip_gain, grad_normed
    )
    back_recv = lax.all_to_all(back_send, "seq", split_axis=0, concat_axis=0, tiled=True)
    end_heads = combine_back(back_recv, decay)
    u, dw, dr = scan_within_back(conv, dt, cum, after(grad_mixed, back_recv), cread)
    end = lax.all_to_all(end_heads, "seq", split_axis=0, concat_axis=0, tiled=True)
    normed = normed.reshape(rows, inner)
    grad_gate = grad_gate.reshape(rows, inner)
    hidden_out = (residual.reshape(rows, width) + dot(normed, out_full, NN)).astype(bf16)
    if fast:
        scan_full = join(w_scan, join(scan_fetched, scan_shared, odd, 0), second, 0)
        own_side, other_side = halves(scaled_low, second, 1)
        quarters = [halves(side, odd, 1) for side in (own_side, other_side)]
        eighths = [[halves(quarter, x, 1) for quarter in pair] for pair in quarters]
        by_y = [
            jnp.concatenate([eighths[y][c][k] for y in (0, 1) for k in (0, 1)], axis=1)
            for c in (0, 1)
        ]
        by_x = [
            jnp.concatenate([eighths[y][c][k] for k in (0, 1) for y in (0, 1)], axis=1)
            for c in (0, 1)
        ]
        slots = jnp.stack([z, x.astype(jnp.int32), odd.astype(jnp.int32)]).astype(jnp.int32)

        def near(left, right, late=None):
            keep = dot(left, right[0], TN)
            got = swap(dot(left, right[1], TN).astype(bf16), "seq", 1)
            return keep + (got if late is None else after(got, late)).astype(f32)

        sides = [halves(side, x, 1) for side in halves(grad_rows, odd, 1)]
        cot = [jnp.concatenate(side, axis=1) for side in sides]
        out_left = jnp.concatenate(halves(normed, second, 1), axis=1)
        out_cores = near(out_left, cot, end_heads)
        gate_cores = near(grad_gate, by_y, end_heads)
        out_y = send_half(out_cores, "fsdp", 1, 0)
        gate_y = send_half(gate_cores, "fsdp", 1, 1)
    else:
        out_total = reduce_rows(dot(normed, grad_rows, TN))
        gate_total = reduce_rows(dot(scaled_low, grad_gate, TN))
    grad_scan, head, tail, conv_sums = scan_back(
        u, dw, dr, conv, p_ext, dt, cum, grad_mixed, gs, start, end,
        conv_weight, dt_bias, a_log, skip_gain,
    )
    following = lax.ppermute(head, "seq", backward)
    if fast:
        out_x = send_half(take(out_y, grad_scan), "seq", 2, 1)
    for place_in in range(CONV - 1):
        row = 8 - (CONV - 1) + place_in
        for tap in range(place_in + 1):
            tail = tail.at[:, row].add(conv_weight[tap] * following[:, place_in - tap])
    grad_scan = lax.dynamic_update_slice(grad_scan, tail.astype(bf16), (0, length - 8, 0))
    grad_scan = grad_scan.reshape(rows, -1)
    if fast:
        cut = grad_scan.shape[1] // 64 * 32
        first = near(grad_scan[:, :cut], by_y)
        rest = near(grad_scan[:, cut:], by_x)
        first_y = send_half(first, "fsdp", 1, 1)
        rest_x = send_half(rest, "seq", 2, 1)
        gate_x = send_half(take(gate_y, first), "seq", 2, 1)
        out_z = send_z(take(out_x, first), z)
        first_x = send_half(take(first_y), "seq", 2, 1)
        rest_y = send_half(take(rest_x), "fsdp", 1, 1)
        gate_z = send_z(take(gate_x, first_x[1]), z)
        out_mine = take(out_z, first_x[1])
        first_z = send_z(take(first_x), z)
        rest_z = send_z(take(rest_y), z)
        out_rows = gather_z(out_mine)
        gate_rows = gather_z(take(gate_z, first_z[1]))
        first_rows = gather_z(take(first_z))
        rest_rows = gather_z(take(rest_z))
        out_pair = gather_columns(out_rows, first_z[1])
        gate_pair = gather_columns(gate_rows, first_rows)
        pairs = [gate_pair, gather_columns(first_rows), gather_columns(rest_rows)]
        out_total = place(slots, [out_pair], out_weight.shape)
        in_total = place(slots, pairs, in_weight.shape[::-1]).T
    else:
        in_total = jnp.concatenate(
            [gate_total, reduce_rows(dot(scaled_low, grad_scan, TN))], axis=1
        )
    grad_scaled = dot(grad_gate, gate_full, NT) + dot(grad_scan, scan_full, NT)
    residual = residual.reshape(rows, width)
    inv_rms = inv_rms.reshape(rows, 1)
    norm_part = jnp.sum(grad_scaled * residual * inv_rms, axis=0)
    f = norm_gain * grad_scaled
    mean = jnp.mean(residual * f, axis=-1, keepdims=True)
    grad_hidden = (
        grad_rows.astype(f32) + inv_rms * f - residual * (inv_rms * inv_rms * inv_rms * mean)
    )
    lanes = conv_sums.shape[1]
    wide = [conv_sums[: CONV + 3], gate_sums[:2], norm_part[None]]
    wide = [jnp.pad(part, ((0, 0), (0, lanes - part.shape[1]))) for part in wide]
    sums = total_over_all(jnp.concatenate(wide, axis=0))
    conv_sum, bias_sum = sums[:CONV], sums[CONV]
    shift_sum, rate_sum = sums[CONV + 1, :heads], sums[CONV + 2, :heads]
    gain_sum = sums[CONV + 3, :inner]
    skip_sum = jnp.sum(sums[CONV + 4, :inner].reshape(heads, HEADDIM), axis=1)
    norm_sum = sums[CONV + 5, :width]
    return (
        hidden_out.reshape(hidden_in.shape),
        grad_hidden.reshape(hidden_in.shape),
        norm_sum,
        in_total,
        conv_sum,
        bias_sum,
        shift_sum,
        rate_sum,
        skip_sum,
        gain_sum,
        out_total,
    )


def solution(mesh):
    tokens = P("fsdp", "seq", None)
    weights = P("fsdp", None)
    return jax.shard_map(
        per_device,
        mesh=mesh,
        in_specs=(tokens, tokens, P(), weights, P(), P(), P(), P(), P(), P(), weights),
        out_specs=(tokens, tokens, P(), weights, P(), P(), P(), P(), P(), P(), weights),
        check_vma=False,
    )
```

```python
import functools

import jax
import jax.numpy as jnp
from jax import lax
from jax.experimental import pallas as pl
from jax.experimental.pallas import tpu as pltpu
from jax.sharding import PartitionSpec as P

HEADDIM = 64
STATE = 128
CONV = 4
HALO = 16
EXTRA = 16
norm_eps = 1e-05
VMEM_BYTES = 56 * 1024 * 1024
f32 = jnp.float32
bf16 = jnp.bfloat16


def exact(a, b, dims):
    return lax.dot_general(
        a, b, (dims, ((), ())), precision=lax.Precision.HIGHEST, preferred_element_type=f32
    )


NN = ((1,), (0,))
TN = ((0,), (0,))
NT = ((1,), (1,))


def iota(shape, dim):
    return lax.broadcasted_iota(jnp.int32, shape, dim)


def split(a):
    high = a.astype(bf16)
    return high, (a - high.astype(f32)).astype(bf16)


def mxu(a, b, dims):
    return lax.dot_general(a, b, (dims, ((), ())), preferred_element_type=f32)


def dot3(a, b, dims):
    a_high, a_low = split(a)
    b_high, b_low = split(b)
    return mxu(a_high, b_high, dims) + (mxu(a_high, b_low, dims) + mxu(a_low, b_high, dims))


def dot2(a, b, dims):
    a_high, a_low = split(a)
    return mxu(a_high, b, dims) + mxu(a_low, b, dims)


def spread_matrix(heads):
    shape = (heads, heads * HEADDIM)
    return (iota(shape, 1) // HEADDIM == iota(shape, 0)).astype(f32).astype(bf16)


def widen(a, spread):
    high, low = split(a)
    return mxu(jnp.concatenate([high, low], axis=1), jnp.concatenate([spread, spread], axis=0), NN)


def widen_row(a, spread):
    high, low = split(jnp.broadcast_to(a, (16, a.shape[1])))
    rest = a - high[0:1].astype(f32) - low[0:1].astype(f32)
    rest = jnp.broadcast_to(rest, (16, a.shape[1])).astype(bf16)
    return (mxu(high, spread, NN) + (mxu(low, spread, NN) + mxu(rest, spread, NN)))[0:1]


def groups(inner, body, carry):
    def step(group, carry):
        return body(pl.ds(pl.multiple_of(group * 128, 128), 128), carry)

    return lax.fori_loop(0, inner // 128, step, carry, unroll=2)


def sigmoid(v):
    return 0.5 * jnp.tanh(0.5 * v) + 0.5


def start_sums(ref):
    @pl.when(pl.program_id(0) == 0)
    def _():
        ref[...] = jnp.zeros(ref.shape, f32)


def softplus(v):
    return jnp.maximum(v, 0.0) + jnp.log1p(jnp.exp(-jnp.abs(v)))


def whole(shape):
    return pl.BlockSpec(shape, lambda g: (0,) * len(shape))


def per_seq(shape):
    return pl.BlockSpec((1,) + shape, lambda g: (g,) + (0,) * len(shape))


def per_dest(shape):
    return pl.BlockSpec(
        (shape[0], 1) + shape[1:], lambda g: (0, g) + (0,) * (len(shape) - 1)
    )


def cost(micros):
    return pl.CostEstimate(flops=0, bytes_accessed=int(micros * 0.7e6), transcendentals=0)


def call(body, grid, in_specs, out_specs, out_shape, scratch=(), micros=10):
    return pl.pallas_call(
        body,
        grid=(grid,),
        in_specs=in_specs,
        out_specs=out_specs,
        out_shape=out_shape,
        scratch_shapes=list(scratch),
        compiler_params=pltpu.CompilerParams(vmem_limit_bytes=VMEM_BYTES),
        cost_estimate=cost(micros),
    )


def front_body(dests, p_ref, cw_ref, cb_ref, dtb_ref, al_ref, conv_ref, dt_ref, cum_ref, send_ref, xw_ref):
    length = conv_ref.shape[1]
    channels = conv_ref.shape[2]
    heads = dt_ref.shape[2]
    inner = heads * HEADDIM
    step = softplus(p_ref[0, HALO:, channels : channels + heads].astype(f32) + dtb_ref[...])
    decay = -step * jnp.exp(al_ref[...])
    lower = (iota((length, length), 0) >= iota((length, length), 1)).astype(f32)
    cum = exact(lower, decay, NN)
    dt_ref[0] = step
    cum_ref[0] = cum
    last = cum[length - 1 :, :]
    weight = jnp.exp(last - cum) * step
    spread = spread_matrix(heads)
    weight_wide = widen(weight, spread)
    last_wide = widen_row(last, spread)
    write_side = None
    for start in list(range(inner, channels, 128)) + list(range(0, inner, 128)):
        cols = slice(start, start + 128)
        joined = p_ref[0, :, cols].astype(f32)
        total = cb_ref[:, cols]
        for tap in range(CONV):
            low = HALO - (CONV - 1) + tap
            total = total + cw_ref[tap : tap + 1, cols] * joined[low : low + length]
        conv_ref[0, :, cols] = total
        if start == inner:
            write_side = total * sigmoid(total)
        elif start < inner:
            xw_ref[:, cols] = total * sigmoid(total) * weight_wide[:, cols]
    state = dot3(write_side, xw_ref[...], TN)
    width = send_ref.shape[3]
    hi = last_wide.astype(bf16)
    rest = last_wide - hi.astype(f32)
    mid = rest.astype(bf16)
    low_part = (rest - mid.astype(f32)).astype(bf16)
    row = iota((EXTRA, inner), 0)
    tail = jnp.where(
        row == 0,
        hi.astype(f32),
        jnp.where(row == 1, mid.astype(f32), jnp.where(row == 2, low_part.astype(f32), 0.0)),
    )
    for dest in range(dests):
        cols = slice(dest * width, (dest + 1) * width)
        send_ref[dest, 0, :STATE, :] = state[:, cols].astype(send_ref.dtype)
        send_ref[dest, 0, STATE:, :] = tail[:, cols].astype(send_ref.dtype)


def scan_front(p_ext, conv_weight, conv_bias, dt_bias, a_log, dests, kind):
    seqs, rows, _ = p_ext.shape
    length = rows - HALO
    heads = dt_bias.shape[0]
    inner = heads * HEADDIM
    channels = inner + 2 * STATE
    width = inner // dests
    return call(
        functools.partial(front_body, dests),
        seqs,
        [
            per_seq(p_ext.shape[1:]),
            whole((CONV, channels)),
            whole((1, channels)),
            whole((1, heads)),
            whole((1, heads)),
        ],
        [
            per_seq((length, channels)),
            per_seq((length, heads)),
            per_seq((length, heads)),
            per_dest((dests, STATE + EXTRA, width)),
        ],
        [
            jax.ShapeDtypeStruct((seqs, length, channels), f32),
            jax.ShapeDtypeStruct((seqs, length, heads), f32),
            jax.ShapeDtypeStruct((seqs, length, heads), f32),
            jax.ShapeDtypeStruct((dests, seqs, STATE + EXTRA, width), kind),
        ],
        [pltpu.VMEM((length, inner), f32)],
        micros=9,
    )(p_ext, conv_weight, conv_bias[None], dt_bias[None], a_log[None])


def combine_body(recv_ref, *refs):
    start_ref, decay_ref = refs[-2:]
    dests, seqs, _, width = recv_ref.shape
    for seq in range(seqs):
        state = jnp.zeros((STATE, width), f32)
        for src in range(dests):
            start_ref[src, seq] = state.astype(start_ref.dtype)
            total = recv_ref[src, seq, STATE:, :].astype(f32)
            decay = jnp.exp(total[0:1] + total[1:2] + total[2:3])
            decay_ref[src, seq] = jnp.broadcast_to(decay, (8, width))
            state = decay * state + recv_ref[src, seq, :STATE, :].astype(f32)


def combine(recv, ready):
    dests, seqs, _, width = recv.shape
    return pl.pallas_call(
        combine_body,
        in_specs=[pl.BlockSpec(memory_space=pltpu.VMEM)]
        + [pl.BlockSpec(memory_space=pl.ANY)] * len(ready),
        out_shape=[
            jax.ShapeDtypeStruct((dests, seqs, STATE, width), recv.dtype),
            jax.ShapeDtypeStruct((dests, seqs, 8, width), f32),
        ],
        compiler_params=pltpu.CompilerParams(vmem_limit_bytes=VMEM_BYTES),
        cost_estimate=cost(2.5),
    )(recv, *ready)


def combine_back_body(recv_ref, decay_ref, *refs):
    end_ref = refs[-1]
    dests, seqs, _, width = recv_ref.shape
    for seq in range(seqs):
        state = jnp.zeros((STATE, width), f32)
        for src in reversed(range(dests)):
            end_ref[src, seq] = state.astype(end_ref.dtype)
            state = decay_ref[src, seq, 0:1] * state + recv_ref[src, seq].astype(f32)


def combine_back(recv, decay, ready):
    return pl.pallas_call(
        combine_back_body,
        in_specs=[pl.BlockSpec(memory_space=pltpu.VMEM)] * 2
        + [pl.BlockSpec(memory_space=pl.ANY)] * len(ready),
        out_shape=jax.ShapeDtypeStruct(recv.shape, recv.dtype),
        compiler_params=pltpu.CompilerParams(vmem_limit_bytes=VMEM_BYTES),
        cost_estimate=cost(2.5),
    )(recv, decay, *ready)


def columns(array):
    length = array.shape[0]
    eye = (iota((length, length), 0) == iota((length, length), 1)).astype(f32)
    return exact(array, eye, TN)


def within_body(conv_ref, dt_ref, cum_ref, skip_ref, y_ref):
    length = conv_ref.shape[1]
    heads = dt_ref.shape[2]
    inner = heads * HEADDIM
    write_conv = conv_ref[0, :, inner : inner + STATE]
    read_conv = conv_ref[0, :, inner + STATE :]
    products = dot3(read_conv * sigmoid(read_conv), write_conv * sigmoid(write_conv), NT)
    cum = cum_ref[0]
    cum_t = columns(cum)
    spread = spread_matrix(heads)
    dt_wide = widen(dt_ref[0], spread)
    skip_wide = widen_row(skip_ref[...], spread)
    causal = iota((length, length), 0) >= iota((length, length), 1)
    left = iota((length, 2 * HEADDIM), 1) < HEADDIM
    for pair in range(heads // 2):
        cols = slice(pair * 2 * HEADDIM, (pair + 1) * 2 * HEADDIM)
        conv = conv_ref[0, :, cols]
        values = conv * sigmoid(conv)
        scaled = values * dt_wide[:, cols]
        terms = []
        for head in (2 * pair, 2 * pair + 1):
            gap = cum[:, head : head + 1] - cum_t[head : head + 1, :]
            terms += split(jnp.exp(jnp.where(causal, gap, -1e30)) * products)
        every = mxu(
            jnp.concatenate(terms, axis=0), jnp.concatenate(split(scaled), axis=1), NN
        )
        high, low = every[:, : 2 * HEADDIM], every[:, 2 * HEADDIM :]
        parts = [
            high[at : at + length] + (low[at : at + length] + high[at + length : at + 2 * length])
            for at in (0, 2 * length)
        ]
        y_ref[0, :, cols] = jnp.where(left, parts[0], parts[1]) + skip_wide[:, cols] * values


def scan_within(conv, dt, cum, skip_gain):
    seqs, length, channels = conv.shape
    heads = dt.shape[2]
    inner = heads * HEADDIM
    return call(
        within_body,
        seqs,
        [
            per_seq((length, channels)),
            per_seq((length, heads)),
            per_seq((length, heads)),
            whole((1, heads)),
        ],
        per_seq((length, inner)),
        jax.ShapeDtypeStruct((seqs, length, inner), f32),
        micros=9,
    )(conv, dt, cum, skip_gain[None])


def middle_body(
    y_ref, conv_ref, cum_ref, start_ref, gate_ref, gain_ref, gn_ref,
    normed_ref, gg_ref, gm_ref, send_ref, sums_ref, gs_ref, cread_ref,
    state_ref, scan_ref, gated_ref, grow_ref,
):
    length = cum_ref.shape[1]
    heads = cum_ref.shape[2]
    inner = heads * HEADDIM
    dests, _, _, width = start_ref.shape
    for dest in range(dests):
        state_ref[:, dest * width : (dest + 1) * width] = start_ref[dest, 0]
    read_conv = conv_ref[0]
    read_side = read_conv * sigmoid(read_conv)
    spread = spread_matrix(heads)
    grow_ref[...] = widen(jnp.exp(cum_ref[0]), spread)
    scan_ref[...] = dot2(read_side, state_ref[...], NN) * grow_ref[...] + y_ref[0]
    start_sums(sums_ref)

    def gate_step(cols, square):
        mixed = scan_ref[:, cols].astype(bf16).astype(f32)
        gate = gate_ref[0, :, cols].astype(f32)
        gated = mixed * (gate * sigmoid(gate))
        gated_ref[:, cols] = gated
        return square + gated * gated

    zeros = jnp.zeros((length, 128), f32)
    square = groups(inner, gate_step, zeros)
    inv = lax.rsqrt(jnp.sum(square, axis=1, keepdims=True) / inner + norm_eps)

    def norm_step(cols, cross):
        grad = gn_ref[0, :, cols]
        unit = gated_ref[:, cols] * inv
        normed_ref[0, :, cols] = (unit * gain_ref[:, cols]).astype(bf16)
        per_gain = grad * unit
        sums_ref[0:1, cols] += jnp.sum(per_gain, axis=0, keepdims=True)
        return cross + per_gain * gain_ref[:, cols]

    cross = groups(inner, norm_step, zeros)
    mean = jnp.sum(cross, axis=1, keepdims=True) / inner
    factor = inv * inv * mean

    def grad_step(cols, carry):
        scanned = scan_ref[:, cols]
        gate = gate_ref[0, :, cols].astype(f32)
        sig = sigmoid(gate)
        grad_gated = inv * (gain_ref[:, cols] * gn_ref[0, :, cols]) - gated_ref[:, cols] * factor
        mixed = scanned.astype(bf16).astype(f32)
        gg_ref[0, :, cols] = (grad_gated * mixed * (sig * (1.0 + gate * (1.0 - sig)))).astype(bf16)
        grad_low = (grad_gated * (gate * sig)).astype(bf16)
        gm_ref[0, :, cols] = grad_low
        grad_mixed = grad_low.astype(f32)
        scan_ref[:, cols] = scanned * grad_mixed
        gated_ref[:, cols] = grad_mixed * grow_ref[:, cols]
        return carry

    groups(inner, grad_step, 0)
    gs_ref[0] = dot2(scan_ref[...], spread, NT)
    cread_ref[0] = dot2(gated_ref[...], state_ref[...], NT)
    back = dot3(read_side, gated_ref[...], TN)
    for dest in range(dests):
        send_ref[dest, 0] = back[:, dest * width : (dest + 1) * width].astype(send_ref.dtype)


def middle(y, conv, cum, start, gate, gate_gain, grad_normed):
    seqs, length, channels = conv.shape
    heads = cum.shape[2]
    inner = heads * HEADDIM
    dests, _, _, width = start.shape
    row = per_seq((length, inner))
    return call(
        middle_body,
        seqs,
        [
            row,
            pl.BlockSpec((1, length, STATE), lambda g: (g, 0, inner // STATE + 1)),
            per_seq((length, heads)),
            per_dest((dests, STATE, width)),
            row,
            whole((1, inner)),
            row,
        ],
        [
            row, row, row,
            per_dest((dests, STATE, width)),
            whole((8, inner)),
            per_seq((length, heads)),
            per_seq((length, STATE)),
        ],
        [
            jax.ShapeDtypeStruct((seqs, length, inner), bf16),
            jax.ShapeDtypeStruct((seqs, length, inner), bf16),
            jax.ShapeDtypeStruct((seqs, length, inner), bf16),
            jax.ShapeDtypeStruct(start.shape, start.dtype),
            jax.ShapeDtypeStruct((8, inner), f32),
            jax.ShapeDtypeStruct((seqs, length, heads), f32),
            jax.ShapeDtypeStruct((seqs, length, STATE), f32),
        ],
        [
            pltpu.VMEM((STATE, inner), start.dtype),
            pltpu.VMEM((length, inner), f32),
            pltpu.VMEM((length, inner), f32),
            pltpu.VMEM((length, inner), f32),
        ],
        micros=12,
    )(y, conv, cum, start, gate, gate_gain[None], grad_normed)


def within_back_body(
    conv_ref, dt_ref, cum_ref, gm_ref, cread_ref, u_ref, dw_ref, dr_ref, xg_ref, prod_ref
):
    length = conv_ref.shape[1]
    heads = dt_ref.shape[2]
    inner = heads * HEADDIM
    write_conv = conv_ref[0, :, inner : inner + STATE]
    read_conv = conv_ref[0, :, inner + STATE :]
    write_side = write_conv * sigmoid(write_conv)
    read_side = read_conv * sigmoid(read_conv)
    products = dot3(write_side, read_side, NT)
    cum = cum_ref[0]
    cum_t = columns(cum)
    spread = spread_matrix(heads)
    dt_wide = widen(dt_ref[0], spread)
    causal = iota((length, length), 0) <= iota((length, length), 1)
    left = iota((length, 2 * HEADDIM), 1) < HEADDIM
    grad_products = jnp.zeros((length, length), f32)
    for pair in range(heads // 2):
        cols = slice(pair * 2 * HEADDIM, (pair + 1) * 2 * HEADDIM)
        conv = conv_ref[0, :, cols]
        values = conv * sigmoid(conv)
        scaled = values * dt_wide[:, cols]
        grad = gm_ref[0, :, cols]
        prod_ref[:, cols] = values * grad.astype(f32)
        terms, own, decays = [], [], []
        for side, head in enumerate((2 * pair, 2 * pair + 1)):
            gap = cum_t[head : head + 1, :] - cum[:, head : head + 1]
            decays.append(jnp.exp(jnp.where(causal, gap, -1e30)))
            terms += split(decays[side] * products)
            own += split(jnp.where(left if side == 0 else ~left, scaled, 0.0))
        every = mxu(jnp.concatenate(terms, axis=0), grad, NN)
        cross = mxu(jnp.concatenate(own, axis=0), grad, NT)
        parts = []
        for side, at in enumerate((0, 2 * length)):
            parts.append(every[at : at + length] + every[at + length : at + 2 * length])
            cross_head = cross[at : at + length] + cross[at + length : at + 2 * length]
            grad_products = grad_products + decays[side] * cross_head
        u_ref[0, :, cols] = jnp.where(left, parts[0], parts[1])
    xg_ref[0] = dot2(prod_ref[...], spread, NT)
    dw_ref[0] = dot3(grad_products, read_side, NN)
    dr_ref[0] = dot3(grad_products, write_side, TN) + cread_ref[0]


def scan_within_back(conv, dt, cum, grad_mixed, cread):
    seqs, length, channels = conv.shape
    heads = dt.shape[2]
    inner = heads * HEADDIM
    side = per_seq((length, STATE))
    return call(
        within_back_body,
        seqs,
        [
            per_seq((length, channels)),
            per_seq((length, heads)),
            per_seq((length, heads)),
            per_seq((length, inner)),
            side,
        ],
        [per_seq((length, inner)), side, side, per_seq((length, heads))],
        [
            jax.ShapeDtypeStruct((seqs, length, inner), f32),
            jax.ShapeDtypeStruct((seqs, length, STATE), f32),
            jax.ShapeDtypeStruct((seqs, length, STATE), f32),
            jax.ShapeDtypeStruct((seqs, length, heads), f32),
        ],
        [pltpu.VMEM((length, inner), f32)],
        micros=14,
    )(conv, dt, cum, grad_mixed, cread)


def back_body(
    u_ref, dw_ref, dr_ref, xg_ref, conv_ref, p_ref, dt_ref, cum_ref, gm_ref, gs_ref,
    start_ref, end_ref, cw_ref, dtb_ref, al_ref, skip_ref,
    grad_ref, head_ref, tail_ref, sums_ref,
    state_ref, xw_ref, xu_ref, xs_ref,
):
    length = conv_ref.shape[1]
    channels = conv_ref.shape[2]
    heads = dt_ref.shape[2]
    inner = heads * HEADDIM
    dests, _, _, width = start_ref.shape
    spread = spread_matrix(heads)
    step = dt_ref[0]
    cum = cum_ref[0]
    last = cum[length - 1 :, :]
    weight = jnp.exp(last - cum)
    step_wide = widen(step, spread)
    weight_wide = widen(weight, spread)
    skip_wide = widen_row(skip_ref[...], spread)
    inner_sum = []
    for dest in range(dests):
        cols = slice(dest * width, (dest + 1) * width)
        state_ref[:, cols] = end_ref[dest, 0]
        end = end_ref[dest, 0].astype(f32)
        inner_sum.append(jnp.sum(end * start_ref[dest, 0].astype(f32), axis=0, keepdims=True))
    inner_sum = jnp.concatenate(inner_sum, axis=1)
    write_conv = conv_ref[0, :, inner : inner + STATE]
    write_side = write_conv * sigmoid(write_conv)
    xs_ref[...] = dot2(write_side, state_ref[...], NN) * weight_wide

    start_sums(sums_ref)

    def conv_back(start, grad, conv, sig):
        cols = slice(start, start + 128)
        dconv = grad * (sig * (1.0 + conv * (1.0 - sig)))
        sums_ref[CONV : CONV + 1, cols] += jnp.sum(dconv, axis=0, keepdims=True)
        joined = p_ref[0, :, cols].astype(f32)
        padded = jnp.concatenate([dconv, jnp.zeros((8, 128), f32)], axis=0)
        grad_joined = cw_ref[CONV - 1 : CONV, cols] * dconv
        for tap in range(CONV):
            low = HALO - (CONV - 1) + tap
            sums_ref[tap : tap + 1, cols] += jnp.sum(
                dconv * joined[low : low + length], axis=0, keepdims=True
            )
            if tap < CONV - 1:
                low = CONV - 1 - tap
                grad_joined = grad_joined + cw_ref[tap : tap + 1, cols] * padded[low : low + length]
        grad_ref[0, :, cols] = grad_joined.astype(bf16)
        head_ref[0, :, cols] = dconv[:8]
        tail_ref[0, :, cols] = grad_joined[length - 8 :]

    for start in range(0, inner, 128):
        cols = slice(start, start + 128)
        conv = conv_ref[0, :, cols]
        sig = sigmoid(conv)
        values = conv * sig
        from_state = xs_ref[:, cols]
        total = u_ref[0, :, cols] + from_state
        xu_ref[:, cols] = values * total
        xs_ref[:, cols] = values * from_state
        xw_ref[:, cols] = values * (step_wide[:, cols] * weight_wide[:, cols])
        grad = step_wide[:, cols] * total + skip_wide[:, cols] * gm_ref[0, :, cols].astype(f32)
        conv_back(start, grad, conv, sig)
    grad_write = dw_ref[0] + dot2(xw_ref[...], state_ref[...], NT)
    conv_back(inner, grad_write, write_conv, sigmoid(write_conv))
    read_conv = conv_ref[0, :, inner + STATE :]
    conv_back(inner + STATE, dr_ref[0], read_conv, sigmoid(read_conv))
    direct = dot2(xu_ref[...], spread, NT)
    ends = dot2(xs_ref[...], spread, NT) * step
    held = dot2(jnp.broadcast_to(inner_sum, (16, inner)), spread, NT)[0:1] * jnp.exp(last)
    at_end = jnp.sum(ends, axis=0, keepdims=True) + held
    dcum = gs_ref[0] - skip_ref[...] * xg_ref[0] - step * direct
    sums_ref[CONV + 3 : CONV + 4, :heads] += jnp.sum(xg_ref[0], axis=0, keepdims=True)
    dcum = dcum + jnp.where(iota((length, heads), 0) == length - 1, at_end, 0.0)
    upper = (iota((length, length), 0) <= iota((length, length), 1)).astype(f32)
    da = exact(upper, dcum, NN)
    rate = jnp.exp(al_ref[...])
    sums_ref[CONV + 2 : CONV + 3, :heads] += jnp.sum(da * (-step * rate), axis=0, keepdims=True)
    raw = p_ref[0, HALO:, channels : channels + heads].astype(f32) + dtb_ref[...]
    draw = (direct - da * rate) * sigmoid(raw)
    grad_ref[0, :, channels:] = draw.astype(bf16)
    sums_ref[CONV + 1 : CONV + 2, :heads] += jnp.sum(draw, axis=0, keepdims=True)


def scan_back(u, dw, dr, xg, conv, p_ext, dt, cum, gm, gs, start, end, conv_weight, dt_bias, a_log, skip_gain):
    seqs, length, channels = conv.shape
    heads = dt.shape[2]
    inner = heads * HEADDIM
    dests, _, _, width = start.shape
    row = per_seq((length, inner))
    small = per_seq((length, heads))
    side = per_seq((length, STATE))
    states = per_dest((dests, STATE, width))
    return call(
        back_body,
        seqs,
        [
            row, side, side, small,
            per_seq((length, channels)),
            per_seq(p_ext.shape[1:]),
            small, small, row, small, states, states,
            whole((CONV, channels)),
            whole((1, heads)),
            whole((1, heads)),
            whole((1, heads)),
        ],
        [
            per_seq((length, channels + heads)),
            per_seq((8, channels)),
            per_seq((8, channels)),
            whole((8, channels)),
        ],
        [
            jax.ShapeDtypeStruct((seqs, length, channels + heads), bf16),
            jax.ShapeDtypeStruct((seqs, 8, channels), f32),
            jax.ShapeDtypeStruct((seqs, 8, channels), f32),
            jax.ShapeDtypeStruct((8, channels), f32),
        ],
        [
            pltpu.VMEM((STATE, inner), end.dtype),
            pltpu.VMEM((length, inner), f32),
            pltpu.VMEM((length, inner), f32),
            pltpu.VMEM((length, inner), f32),
        ],
        micros=14,
    )(u, dw, dr, xg, conv, p_ext, dt, cum, gm, gs, start, end, conv_weight,
      dt_bias[None], a_log[None], skip_gain[None])


def swap(x, axis, flip):
    count = lax.axis_size(axis)
    return lax.ppermute(x, axis, [(slot, slot ^ flip) for slot in range(count)])


def small_flips():
    flips = [("seq", 1 << k) for k in range(lax.axis_size("seq").bit_length() - 1)]
    flips[1:1] = [("fsdp", 1 << k) for k in range(lax.axis_size("fsdp").bit_length() - 1)]
    return flips


def one_more(x, flip, *events):
    got = swap(x, *flip)
    return x + (after(got, *events) if events else got)


def shared_slots():
    slot = lax.axis_index("seq")
    return slot // 4, slot // 2 % 2 == 1, slot % 2 == 1, lax.axis_index("fsdp") == 1


def fast_mesh():
    return lax.axis_size("fsdp") == 2 and lax.axis_size("seq") == 16


def halves(x, flag, axis):
    size = x.shape[axis] // 2
    low = lax.slice_in_dim(x, 0, size, axis=axis)
    high = lax.slice_in_dim(x, size, 2 * size, axis=axis)
    return jnp.where(flag, high, low), jnp.where(flag, low, high)


def join(own, other, flag, axis):
    low = jnp.where(flag, other, own)
    high = jnp.where(flag, own, other)
    return jnp.concatenate([low, high], axis=axis)


def after(x, *others):
    return lax.optimization_barrier((x,) + others)[0]


def fetch_rows(w, start=None, late=None):
    _, _, odd, _ = shared_slots()
    mine, _ = halves(w, odd, 0)
    if start is not None:
        mine = after(mine, start)
    fetched = swap(mine, "fsdp", 1)
    if late is not None:
        fetched = after(fetched, late)
    return fetched, swap(fetched, "seq", 1)


def gather_rows(w, start=None, late=None):
    if not fast_mesh():
        return lax.all_gather(w, "fsdp", axis=0, tiled=True)
    _, _, odd, second = shared_slots()
    fetched, shared = fetch_rows(w, start, late)
    return join(w, join(fetched, shared, odd, 0), second, 0)


def reduce_rows(part):
    shard = lax.psum_scatter(part, "fsdp", scatter_dimension=0, tiled=True)
    return lax.psum(shard, "seq")


def send_half(total, axis, flip, dim):
    size = total[0].shape[dim] // 2
    keep = [lax.slice_in_dim(term, 0, size, axis=dim).astype(f32) for term in total]
    give = [lax.slice_in_dim(term, size, 2 * size, axis=dim).astype(f32) for term in total]
    return [sum(keep[1:], keep[0]), swap(sum(give[1:], give[0]).astype(bf16), axis, flip)]


def held(sent, *events):
    return [sent[0]] + [after(piece, *events) for piece in sent[1:]]


def fold_z(total, flag, flip):
    keep, give = halves(total, flag, 0)
    return keep[0], swap(give[0].astype(bf16), "seq", flip)


def both(own, got):
    return jnp.stack([own, got])


def place_body(plan, slots_ref, *refs):
    outs = refs[-1:]
    z, x, core = slots_ref[0], slots_ref[1], slots_ref[2]
    for source, first, rows, base, wide in plan:
        for side in range(2):
            for k in range(2):
                src = refs[4 * source + 2 * side + k]
                at = (lax.rem(core + side, 2) * 2 + lax.rem(x + k, 2)) * 128 * wide
                for shift in range(4):
                    low_bit = lax.rem(z + shift // 2, 2)
                    high_bit = lax.rem(z // 2 + shift % 2, 2)
                    row = base + (2 * high_bit + low_bit) * rows
                    for part in range(wide):
                        low = first + part * rows
                        outs[0][
                            pl.ds(pl.multiple_of(row, 8), rows),
                            pl.ds(pl.multiple_of(at + part * 128, 128), 128),
                        ] = src[shift // 2, shift % 2, low : low + rows, :].astype(f32)


def place(slots, plan, arrays, shape):
    return pl.pallas_call(
        functools.partial(place_body, plan),
        in_specs=[pl.BlockSpec(memory_space=pltpu.SMEM)]
        + [pl.BlockSpec(memory_space=pltpu.VMEM)] * len(arrays),
        out_specs=pl.BlockSpec(memory_space=pltpu.VMEM),
        out_shape=jax.ShapeDtypeStruct(shape, f32),
        compiler_params=pltpu.CompilerParams(vmem_limit_bytes=VMEM_BYTES),
        cost_estimate=cost(6),
    )(slots, *arrays)


def dot(a, b, dims):
    return lax.dot_general(a, b, (dims, ((), ())), preferred_element_type=f32)


STATE_TYPE = bf16


def per_device(
    hidden_in, cotangent, norm_gain, in_weight, conv_weight, conv_bias,
    dt_bias, a_log, skip_gain, gate_gain, out_weight,
):
    seq_count = lax.axis_size("seq")
    seqs, length, width = hidden_in.shape
    rows = seqs * length
    heads = dt_bias.shape[0]
    inner = heads * HEADDIM
    forward = [(slot, slot + 1) for slot in range(seq_count - 1)]
    backward = [(slot + 1, slot) for slot in range(seq_count - 1)]
    fast = fast_mesh()

    w_gate, w_scan = in_weight[:, :inner], in_weight[:, inner:]
    if fast:
        z, x, odd, second = shared_slots()
        scan_give = halves(w_scan, odd, 0)[0]
        hidden_in = after(hidden_in, scan_give)
        scan_fetched = swap(scan_give, "fsdp", 1)
        slots = jnp.stack([z, x.astype(jnp.int32), odd.astype(jnp.int32)]).astype(jnp.int32)

    def prenorm(rows_in):
        inv = lax.rsqrt(jnp.mean(rows_in * rows_in, axis=-1, keepdims=True) + norm_eps)
        return inv, (rows_in * inv * norm_gain).astype(bf16)

    residual = hidden_in.astype(f32)
    inv_rms, scaled_low = prenorm(residual)
    halo = after(hidden_in, scaled_low)[:, length - HALO :]
    halo = lax.ppermute(halo, "seq", forward)
    _, scaled_halo = prenorm(halo.astype(f32))
    scaled_ext = jnp.concatenate([scaled_halo, scaled_low], axis=1)
    scaled_ext = scaled_ext.reshape(seqs * (HALO + length), width)
    scaled_low = scaled_low.reshape(rows, width)
    if fast:
        ext_own, ext_other = halves(scaled_ext, second, 1)
        ext_fetched, ext_shared = halves(ext_other, odd, 1)
        p_ext = dot(ext_own, w_scan, NN)
        scan_fetched = after(scan_fetched, p_ext)
        scan_shared = swap(scan_fetched, "seq", 1)
        p_ext = p_ext + dot(ext_fetched, scan_fetched, NN)
        p_ext = p_ext + dot(ext_shared, scan_shared, NN)
    else:
        scan_full = lax.all_gather(w_scan, "fsdp", axis=0, tiled=True)
        p_ext = dot(scaled_ext, scan_full, NN)
    p_ext = p_ext.astype(bf16).reshape(seqs, HALO + length, -1)

    conv, dt, cum, send = scan_front(
        p_ext, conv_weight, conv_bias, dt_bias, a_log, seq_count, STATE_TYPE
    )
    recv = lax.all_to_all(send, "seq", split_axis=0, concat_axis=0, tiled=True)
    y = scan_within(conv, dt, cum, skip_gain)
    grad_rows = cotangent.reshape(rows, width)
    ready = [y]
    if fast:
        own_side, other_side = halves(scaled_low, second, 1)
        quarters = [halves(side, odd, 1) for side in (own_side, other_side)]
        eighths = [[halves(quarter, x, 1) for quarter in pair] for pair in quarters]
        by_y = [
            jnp.concatenate([eighths[y_side][c][k] for y_side in (0, 1) for k in (0, 1)], axis=1)
            for c in (0, 1)
        ]
        by_x = [
            jnp.concatenate([eighths[y_side][c][k] for k in (0, 1) for y_side in (0, 1)], axis=1)
            for c in (0, 1)
        ]

        sides = [halves(side, x, 1) for side in halves(grad_rows, odd, 1)]
        cot = [jnp.concatenate(side, axis=1) for side in sides]
        ready += by_y + by_x + cot
    start_heads, decay = combine(recv, ready)
    gate_full = gather_rows(w_gate, conv, recv)
    out_full = gather_rows(out_weight, start_heads)
    start = lax.all_to_all(start_heads, "seq", split_axis=0, concat_axis=0, tiled=True)
    gate = dot(scaled_low, gate_full, NN).astype(bf16).reshape(seqs, length, inner)
    grad_normed = dot(grad_rows, out_full, NT).reshape(seqs, length, inner)
    normed, grad_gate, grad_mixed, back_send, gate_sums, gs, cread = middle(
        y, conv, cum, start, gate, gate_gain, grad_normed
    )
    back_recv = lax.all_to_all(back_send, "seq", split_axis=0, concat_axis=0, tiled=True)
    normed = normed.reshape(rows, inner)
    grad_gate = grad_gate.reshape(rows, inner)
    if fast:
        scan_full = join(w_scan, join(scan_fetched, scan_shared, odd, 0), second, 0)
        def near(left, right, *events):
            give = dot(left, right[1], TN).astype(bf16)
            keep = dot(left, right[0], TN)
            return held([keep, swap(give, "seq", 1)], *events)

        out_left = jnp.concatenate(halves(normed, second, 1), axis=1)
        gate_y = send_half(near(grad_gate, by_y), "fsdp", 1, 1)
        out_x = send_half(near(out_left, cot), "seq", 2, 1)
        ready = [out_x[0], gate_y[0]]
    else:
        out_total = reduce_rows(dot(normed, grad_rows, TN))
        gate_total = reduce_rows(dot(scaled_low, grad_gate, TN))
        ready = []
    end_heads = combine_back(back_recv, decay, ready)
    u, dw, dr, xg = scan_within_back(conv, dt, cum, after(grad_mixed, back_recv), cread)
    end = lax.all_to_all(end_heads, "seq", split_axis=0, concat_axis=0, tiled=True)
    hidden_out = (residual.reshape(rows, width) + dot(normed, out_full, NN)).astype(bf16)
    grad_scan, head, tail, conv_sums = scan_back(
        u, dw, dr, xg, conv, p_ext, dt, cum, grad_mixed, gs, start, end,
        conv_weight, dt_bias, a_log, skip_gain,
    )
    grad_raw = grad_scan
    following = lax.ppermute(head, "seq", backward)
    if fast:
        out_y = send_half(held(out_x, grad_raw), "fsdp", 1, 0)
        gate_x = send_half(held(gate_y, grad_raw), "seq", 2, 1)
    for tap in range(CONV - 1):
        reach = following[:, : CONV - 1 - tap]
        low = 8 - (CONV - 1) + tap
        tail = tail + conv_weight[tap] * jnp.pad(reach, ((0, 0), (low, 0), (0, 0)))
    grad_scan = lax.dynamic_update_slice(grad_scan, tail.astype(bf16), (0, length - 8, 0))
    grad_scan = grad_scan.reshape(rows, -1)

    held_back = []

    def lined_up(grad_scan, *events):
        if events:
            grad_scan = after(grad_scan, *events)
        grad_scaled = dot(grad_gate, gate_full, NT) + dot(grad_scan, scan_full, NT)
        rows_in = residual.reshape(rows, width)
        inv = inv_rms.reshape(rows, 1)
        norm_part = jnp.sum(grad_scaled * rows_in * inv, axis=0)
        f = norm_gain * grad_scaled
        mean = jnp.mean(rows_in * f, axis=-1, keepdims=True)
        held_back.append(grad_rows.astype(f32) + inv * f - rows_in * (inv * inv * inv * mean))
        lanes = conv_sums.shape[1]
        wide = [conv_sums[: CONV + 4], gate_sums[:1], norm_part[None]]
        wide = [jnp.pad(part, ((0, 0), (0, lanes - part.shape[1]))) for part in wide]
        return jnp.concatenate(wide, axis=0)

    if fast:
        cut = grad_scan.shape[1] // 64 * 32
        first = near(grad_scan[:, :cut], by_y)
        rest = near(grad_scan[:, cut:], by_x)
        first_y = send_half(first, "fsdp", 1, 1)
        rest_x = send_half(rest, "seq", 2, 1)
        waited = [held(out_y, rest_x[0]), held(gate_x, rest_x[0])]
        out_sum, gate_sum = [pair[0] + pair[1].astype(f32) for pair in waited]
        out_sum = out_sum.reshape(4, -1, 256)
        early = jnp.concatenate(
            [out_sum[:, :, :128], out_sum[:, :, 128:], gate_sum.reshape(4, -1, 128)], axis=1
        )
        low_bit, high_bit = z % 2 == 1, z // 2 == 1
        early = early.reshape(2, 2, -1, 128).swapaxes(0, 1)
        early_low = fold_z(early, low_bit, 4)
        first_x = send_half(first_y, "seq", 2, 1)
        rest_y = send_half(rest_x, "fsdp", 1, 1)
        sums = lined_up(grad_scan, first_x[0])
        flips = small_flips()
        sums = one_more(sums, flips[0], first_x[0])
        early_sum = early_low[0] + after(early_low[1], first_x[0]).astype(f32)
        early_high = fold_z(early_sum, high_bit, 8)
        pair = [
            sent[0] + sent[1].astype(f32)
            for sent in (held(first_x, sums), held(rest_y, sums))
        ]
        late_cut = pair[0].shape[0] // 4
        late = jnp.concatenate([half.reshape(4, -1, 128) for half in pair], axis=1)
        late = late.reshape(2, 2, -1, 128).swapaxes(0, 1)
        late_low = fold_z(late, low_bit, 4)
        early_sum = early_high[0] + after(early_high[1], late_low[0]).astype(f32)
        sums = one_more(sums, flips[1], late_low[0])
        early_own = early_sum.astype(bf16)
        early_own = both(early_own, swap(early_own, "seq", 8))
        late_sum = late_low[0] + after(late_low[1], sums).astype(f32)
        late_high = fold_z(late_sum, high_bit, 8)
        early_own = after(early_own, late_high[0])
        sums = one_more(sums, flips[2], late_high[0])
        early_near = both(early_own, swap(early_own, "seq", 4))
        late_own = (late_high[0] + after(late_high[1], sums).astype(f32)).astype(bf16)
        late_own = both(late_own, swap(late_own, "seq", 8))
        early_near = after(early_near, late_own)
        sums = one_more(sums, flips[3], late_own)
        early_far = swap(early_near, "seq", 2)
        late_near = both(after(late_own, sums), swap(late_own, "seq", 4))
        late_far = swap(late_near, "seq", 2)
        sums = one_more(sums, flips[4], late_near)
        early_far = after(early_far, late_near)
        early_four = [early_near, early_far, swap(early_near, "seq", 1), swap(early_far, "seq", 1)]
        late_four = [late_near, late_far, swap(late_near, "seq", 1), swap(late_far, "seq", 1)]
        size = out_weight.shape[0] // 4
        out_total = place(slots, [(0, 0, size, 0, 2)], early_four, out_weight.shape)
    if not fast:
        sums = lined_up(grad_scan)
        for flip in small_flips():
            sums = one_more(sums, flip)
    grad_hidden = held_back[0]
    conv_sum, bias_sum = sums[:CONV], sums[CONV]
    shift_sum, rate_sum = sums[CONV + 1, :heads], sums[CONV + 2, :heads]
    skip_sum, gain_sum = sums[CONV + 3, :heads], sums[CONV + 4, :inner]
    norm_sum = sums[CONV + 5, :width]
    if fast:
        late_four[3] = after(late_four[3], out_total, skip_sum, grad_hidden)
        plan = [
            (0, 2 * size, inner // 4, 0, 1),
            (1, 0, late_cut, inner, 1),
            (1, late_cut, late.shape[2] - late_cut, inner + cut, 1),
        ]
        in_total = place(slots, plan, early_four + late_four, in_weight.shape[::-1]).T
    else:
        in_total = jnp.concatenate(
            [gate_total, reduce_rows(dot(scaled_low, grad_scan, TN))], axis=1
        )
    return (
        hidden_out.reshape(hidden_in.shape),
        grad_hidden.reshape(hidden_in.shape),
        norm_sum,
        in_total,
        conv_sum,
        bias_sum,
        shift_sum,
        rate_sum,
        skip_sum,
        gain_sum,
        out_total,
    )


def solution(mesh):
    tokens = P("fsdp", "seq", None)
    weights = P("fsdp", None)
    return jax.shard_map(
        per_device,
        mesh=mesh,
        in_specs=(tokens, tokens, P(), weights, P(), P(), P(), P(), P(), P(), weights),
        out_specs=(tokens, tokens, P(), weights, P(), P(), P(), P(), P(), P(), weights),
        check_vma=False,
    )
```

```python
import functools

import jax
import jax.numpy as jnp
from jax import lax
from jax.experimental import pallas as pl
from jax.experimental.pallas import tpu as pltpu
from jax.sharding import PartitionSpec as P

HEADDIM = 64
STATE = 128
CONV = 4
HALO = 16
EXTRA = 16
norm_eps = 1e-05
VMEM_BYTES = 56 * 1024 * 1024
f32 = jnp.float32
bf16 = jnp.bfloat16


def exact(a, b, dims):
    return lax.dot_general(
        a, b, (dims, ((), ())), precision=lax.Precision.HIGHEST, preferred_element_type=f32
    )


NN = ((1,), (0,))
TN = ((0,), (0,))
NT = ((1,), (1,))


def iota(shape, dim):
    return lax.broadcasted_iota(jnp.int32, shape, dim)


def split(a):
    high = a.astype(bf16)
    return high, (a - high.astype(f32)).astype(bf16)


def mxu(a, b, dims):
    return lax.dot_general(a, b, (dims, ((), ())), preferred_element_type=f32)


def dot3(a, b, dims):
    a_high, a_low = split(a)
    b_high, b_low = split(b)
    return mxu(a_high, b_high, dims) + (mxu(a_high, b_low, dims) + mxu(a_low, b_high, dims))


def dot2(a, b, dims):
    a_high, a_low = split(a)
    return mxu(a_high, b, dims) + mxu(a_low, b, dims)


def spread_matrix(heads):
    shape = (heads, heads * HEADDIM)
    return (iota(shape, 1) // HEADDIM == iota(shape, 0)).astype(f32).astype(bf16)


def widen(a, spread):
    high, low = split(a)
    return mxu(jnp.concatenate([high, low], axis=1), jnp.concatenate([spread, spread], axis=0), NN)


def widen_row(a, spread):
    high, low = split(jnp.broadcast_to(a, (16, a.shape[1])))
    rest = a - high[0:1].astype(f32) - low[0:1].astype(f32)
    rest = jnp.broadcast_to(rest, (16, a.shape[1])).astype(bf16)
    return (mxu(high, spread, NN) + (mxu(low, spread, NN) + mxu(rest, spread, NN)))[0:1]


def groups(inner, body, carry):
    def step(group, carry):
        return body(pl.ds(pl.multiple_of(group * 128, 128), 128), carry)

    return lax.fori_loop(0, inner // 128, step, carry, unroll=2)


def sigmoid(v):
    return 0.5 * jnp.tanh(0.5 * v) + 0.5


def start_sums(ref):
    @pl.when(pl.program_id(0) == 0)
    def _():
        ref[...] = jnp.zeros(ref.shape, f32)


def softplus(v):
    return jnp.maximum(v, 0.0) + jnp.log1p(jnp.exp(-jnp.abs(v)))


def whole(shape):
    return pl.BlockSpec(shape, lambda g: (0,) * len(shape))


def per_seq(shape):
    return pl.BlockSpec((1,) + shape, lambda g: (g,) + (0,) * len(shape))


def per_dest(shape):
    return pl.BlockSpec(
        (shape[0], 1) + shape[1:], lambda g: (0, g) + (0,) * (len(shape) - 1)
    )


def cost(micros):
    return pl.CostEstimate(flops=0, bytes_accessed=int(micros * 0.7e6), transcendentals=0)


def call(body, grid, in_specs, out_specs, out_shape, scratch=(), micros=10):
    return pl.pallas_call(
        body,
        grid=(grid,),
        in_specs=in_specs,
        out_specs=out_specs,
        out_shape=out_shape,
        scratch_shapes=list(scratch),
        compiler_params=pltpu.CompilerParams(vmem_limit_bytes=VMEM_BYTES),
        cost_estimate=cost(micros),
    )


def front_body(dests, p_ref, cw_ref, cb_ref, dtb_ref, al_ref, conv_ref, dt_ref, cum_ref, send_ref, xw_ref):
    length = conv_ref.shape[1]
    channels = conv_ref.shape[2]
    heads = dt_ref.shape[2]
    inner = heads * HEADDIM
    step = softplus(p_ref[0, HALO:, channels : channels + heads].astype(f32) + dtb_ref[...])
    decay = -step * jnp.exp(al_ref[...])
    lower = (iota((length, length), 0) >= iota((length, length), 1)).astype(f32)
    cum = exact(lower, decay, NN)
    dt_ref[0] = step
    cum_ref[0] = cum
    last = cum[length - 1 :, :]
    weight = jnp.exp(last - cum) * step
    spread = spread_matrix(heads)
    weight_wide = widen(weight, spread)
    last_wide = widen_row(last, spread)
    write_side = None
    for start in list(range(inner, channels, 128)) + list(range(0, inner, 128)):
        cols = slice(start, start + 128)
        joined = p_ref[0, :, cols].astype(f32)
        total = cb_ref[:, cols]
        for tap in range(CONV):
            low = HALO - (CONV - 1) + tap
            total = total + cw_ref[tap : tap + 1, cols] * joined[low : low + length]
        conv_ref[0, :, cols] = total
        if start == inner:
            write_side = total * sigmoid(total)
        elif start < inner:
            xw_ref[:, cols] = total * sigmoid(total) * weight_wide[:, cols]
    state = dot3(write_side, xw_ref[...], TN)
    width = send_ref.shape[3]
    hi = last_wide.astype(bf16)
    rest = last_wide - hi.astype(f32)
    mid = rest.astype(bf16)
    low_part = (rest - mid.astype(f32)).astype(bf16)
    row = iota((EXTRA, inner), 0)
    tail = jnp.where(
        row == 0,
        hi.astype(f32),
        jnp.where(row == 1, mid.astype(f32), jnp.where(row == 2, low_part.astype(f32), 0.0)),
    )
    for dest in range(dests):
        cols = slice(dest * width, (dest + 1) * width)
        send_ref[dest, 0, :STATE, :] = state[:, cols].astype(send_ref.dtype)
        send_ref[dest, 0, STATE:, :] = tail[:, cols].astype(send_ref.dtype)


def scan_front(p_ext, conv_weight, conv_bias, dt_bias, a_log, dests, kind):
    seqs, rows, _ = p_ext.shape
    length = rows - HALO
    heads = dt_bias.shape[0]
    inner = heads * HEADDIM
    channels = inner + 2 * STATE
    width = inner // dests
    return call(
        functools.partial(front_body, dests),
        seqs,
        [
            per_seq(p_ext.shape[1:]),
            whole((CONV, channels)),
            whole((1, channels)),
            whole((1, heads)),
            whole((1, heads)),
        ],
        [
            per_seq((length, channels)),
            per_seq((length, heads)),
            per_seq((length, heads)),
            per_dest((dests, STATE + EXTRA, width)),
        ],
        [
            jax.ShapeDtypeStruct((seqs, length, channels), f32),
            jax.ShapeDtypeStruct((seqs, length, heads), f32),
            jax.ShapeDtypeStruct((seqs, length, heads), f32),
            jax.ShapeDtypeStruct((dests, seqs, STATE + EXTRA, width), kind),
        ],
        [pltpu.VMEM((length, inner), f32)],
        micros=9,
    )(p_ext, conv_weight, conv_bias[None], dt_bias[None], a_log[None])


def combine_body(recv_ref, *refs):
    start_ref, decay_ref = refs[-2:]
    dests, seqs, _, width = recv_ref.shape
    for seq in range(seqs):
        state = jnp.zeros((STATE, width), f32)
        for src in range(dests):
            start_ref[src, seq] = state.astype(start_ref.dtype)
            total = recv_ref[src, seq, STATE:, :].astype(f32)
            decay = jnp.exp(total[0:1] + total[1:2] + total[2:3])
            decay_ref[src, seq] = jnp.broadcast_to(decay, (8, width))
            state = decay * state + recv_ref[src, seq, :STATE, :].astype(f32)


def combine(recv, ready):
    dests, seqs, _, width = recv.shape
    return pl.pallas_call(
        combine_body,
        in_specs=[pl.BlockSpec(memory_space=pltpu.VMEM)]
        + [pl.BlockSpec(memory_space=pl.ANY)] * len(ready),
        out_shape=[
            jax.ShapeDtypeStruct((dests, seqs, STATE, width), recv.dtype),
            jax.ShapeDtypeStruct((dests, seqs, 8, width), f32),
        ],
        compiler_params=pltpu.CompilerParams(vmem_limit_bytes=VMEM_BYTES),
        cost_estimate=cost(2.5),
    )(recv, *ready)


def combine_back_body(recv_ref, decay_ref, *refs):
    end_ref = refs[-1]
    dests, seqs, _, width = recv_ref.shape
    for seq in range(seqs):
        state = jnp.zeros((STATE, width), f32)
        for src in reversed(range(dests)):
            end_ref[src, seq] = state.astype(end_ref.dtype)
            state = decay_ref[src, seq, 0:1] * state + recv_ref[src, seq].astype(f32)


def combine_back(recv, decay, ready):
    return pl.pallas_call(
        combine_back_body,
        in_specs=[pl.BlockSpec(memory_space=pltpu.VMEM)] * 2
        + [pl.BlockSpec(memory_space=pl.ANY)] * len(ready),
        out_shape=jax.ShapeDtypeStruct(recv.shape, recv.dtype),
        compiler_params=pltpu.CompilerParams(vmem_limit_bytes=VMEM_BYTES),
        cost_estimate=cost(2.5),
    )(recv, decay, *ready)


def columns(array):
    length = array.shape[0]
    eye = (iota((length, length), 0) == iota((length, length), 1)).astype(f32)
    return exact(array, eye, TN)


def within_body(conv_ref, dt_ref, cum_ref, skip_ref, y_ref):
    length = conv_ref.shape[1]
    heads = dt_ref.shape[2]
    inner = heads * HEADDIM
    write_conv = conv_ref[0, :, inner : inner + STATE]
    read_conv = conv_ref[0, :, inner + STATE :]
    products = dot3(read_conv * sigmoid(read_conv), write_conv * sigmoid(write_conv), NT)
    cum = cum_ref[0]
    cum_t = columns(cum)
    spread = spread_matrix(heads)
    dt_wide = widen(dt_ref[0], spread)
    skip_wide = widen_row(skip_ref[...], spread)
    causal = iota((length, length), 0) >= iota((length, length), 1)
    left = iota((length, 2 * HEADDIM), 1) < HEADDIM
    for pair in range(heads // 2):
        cols = slice(pair * 2 * HEADDIM, (pair + 1) * 2 * HEADDIM)
        conv = conv_ref[0, :, cols]
        values = conv * sigmoid(conv)
        scaled = values * dt_wide[:, cols]
        terms = []
        for head in (2 * pair, 2 * pair + 1):
            gap = cum[:, head : head + 1] - cum_t[head : head + 1, :]
            terms += split(jnp.exp(jnp.where(causal, gap, -1e30)) * products)
        every = mxu(
            jnp.concatenate(terms, axis=0), jnp.concatenate(split(scaled), axis=1), NN
        )
        high, low = every[:, : 2 * HEADDIM], every[:, 2 * HEADDIM :]
        parts = [
            high[at : at + length] + (low[at : at + length] + high[at + length : at + 2 * length])
            for at in (0, 2 * length)
        ]
        y_ref[0, :, cols] = jnp.where(left, parts[0], parts[1]) + skip_wide[:, cols] * values


def scan_within(conv, dt, cum, skip_gain):
    seqs, length, channels = conv.shape
    heads = dt.shape[2]
    inner = heads * HEADDIM
    return call(
        within_body,
        seqs,
        [
            per_seq((length, channels)),
            per_seq((length, heads)),
            per_seq((length, heads)),
            whole((1, heads)),
        ],
        per_seq((length, inner)),
        jax.ShapeDtypeStruct((seqs, length, inner), f32),
        micros=9,
    )(conv, dt, cum, skip_gain[None])


def middle_body(
    y_ref, conv_ref, cum_ref, start_ref, gate_ref, gain_ref, gn_ref,
    normed_ref, gg_ref, gm_ref, send_ref, sums_ref, gs_ref, cread_ref,
    state_ref, scan_ref, gated_ref, grow_ref,
):
    length = cum_ref.shape[1]
    heads = cum_ref.shape[2]
    inner = heads * HEADDIM
    dests, _, _, width = start_ref.shape
    for dest in range(dests):
        state_ref[:, dest * width : (dest + 1) * width] = start_ref[dest, 0]
    read_conv = conv_ref[0]
    read_side = read_conv * sigmoid(read_conv)
    spread = spread_matrix(heads)
    grow_ref[...] = widen(jnp.exp(cum_ref[0]), spread)
    scan_ref[...] = dot2(read_side, state_ref[...], NN) * grow_ref[...] + y_ref[0]
    start_sums(sums_ref)

    def gate_step(cols, square):
        mixed = scan_ref[:, cols].astype(bf16).astype(f32)
        gate = gate_ref[0, :, cols].astype(f32)
        gated = mixed * (gate * sigmoid(gate))
        gated_ref[:, cols] = gated
        return square + gated * gated

    zeros = jnp.zeros((length, 128), f32)
    square = groups(inner, gate_step, zeros)
    inv = lax.rsqrt(jnp.sum(square, axis=1, keepdims=True) / inner + norm_eps)

    def norm_step(cols, cross):
        grad = gn_ref[0, :, cols]
        unit = gated_ref[:, cols] * inv
        normed_ref[0, :, cols] = (unit * gain_ref[:, cols]).astype(bf16)
        per_gain = grad * unit
        sums_ref[0:1, cols] += jnp.sum(per_gain, axis=0, keepdims=True)
        return cross + per_gain * gain_ref[:, cols]

    cross = groups(inner, norm_step, zeros)
    mean = jnp.sum(cross, axis=1, keepdims=True) / inner
    factor = inv * inv * mean

    def grad_step(cols, carry):
        scanned = scan_ref[:, cols]
        gate = gate_ref[0, :, cols].astype(f32)
        sig = sigmoid(gate)
        grad_gated = inv * (gain_ref[:, cols] * gn_ref[0, :, cols]) - gated_ref[:, cols] * factor
        mixed = scanned.astype(bf16).astype(f32)
        gg_ref[0, :, cols] = (grad_gated * mixed * (sig * (1.0 + gate * (1.0 - sig)))).astype(bf16)
        grad_low = (grad_gated * (gate * sig)).astype(bf16)
        gm_ref[0, :, cols] = grad_low
        grad_mixed = grad_low.astype(f32)
        scan_ref[:, cols] = scanned * grad_mixed
        gated_ref[:, cols] = grad_mixed * grow_ref[:, cols]
        return carry

    groups(inner, grad_step, 0)
    gs_ref[0] = dot2(scan_ref[...], spread, NT)
    cread_ref[0] = dot2(gated_ref[...], state_ref[...], NT)
    back = dot3(read_side, gated_ref[...], TN)
    for dest in range(dests):
        send_ref[dest, 0] = back[:, dest * width : (dest + 1) * width].astype(send_ref.dtype)


def middle(y, conv, cum, start, gate, gate_gain, grad_normed):
    seqs, length, channels = conv.shape
    heads = cum.shape[2]
    inner = heads * HEADDIM
    dests, _, _, width = start.shape
    row = per_seq((length, inner))
    return call(
        middle_body,
        seqs,
        [
            row,
            pl.BlockSpec((1, length, STATE), lambda g: (g, 0, inner // STATE + 1)),
            per_seq((length, heads)),
            per_dest((dests, STATE, width)),
            row,
            whole((1, inner)),
            row,
        ],
        [
            row, row, row,
            per_dest((dests, STATE, width)),
            whole((8, inner)),
            per_seq((length, heads)),
            per_seq((length, STATE)),
        ],
        [
            jax.ShapeDtypeStruct((seqs, length, inner), bf16),
            jax.ShapeDtypeStruct((seqs, length, inner), bf16),
            jax.ShapeDtypeStruct((seqs, length, inner), bf16),
            jax.ShapeDtypeStruct(start.shape, start.dtype),
            jax.ShapeDtypeStruct((8, inner), f32),
            jax.ShapeDtypeStruct((seqs, length, heads), f32),
            jax.ShapeDtypeStruct((seqs, length, STATE), f32),
        ],
        [
            pltpu.VMEM((STATE, inner), start.dtype),
            pltpu.VMEM((length, inner), f32),
            pltpu.VMEM((length, inner), f32),
            pltpu.VMEM((length, inner), f32),
        ],
        micros=12,
    )(y, conv, cum, start, gate, gate_gain[None], grad_normed)


def within_back_body(
    conv_ref, dt_ref, cum_ref, gm_ref, cread_ref, u_ref, dw_ref, dr_ref, xg_ref, prod_ref
):
    length = conv_ref.shape[1]
    heads = dt_ref.shape[2]
    inner = heads * HEADDIM
    write_conv = conv_ref[0, :, inner : inner + STATE]
    read_conv = conv_ref[0, :, inner + STATE :]
    write_side = write_conv * sigmoid(write_conv)
    read_side = read_conv * sigmoid(read_conv)
    products = dot3(write_side, read_side, NT)
    cum = cum_ref[0]
    cum_t = columns(cum)
    spread = spread_matrix(heads)
    dt_wide = widen(dt_ref[0], spread)
    causal = iota((length, length), 0) <= iota((length, length), 1)
    left = iota((length, 2 * HEADDIM), 1) < HEADDIM
    grad_products = jnp.zeros((length, length), f32)
    for pair in range(heads // 2):
        cols = slice(pair * 2 * HEADDIM, (pair + 1) * 2 * HEADDIM)
        conv = conv_ref[0, :, cols]
        values = conv * sigmoid(conv)
        scaled = values * dt_wide[:, cols]
        grad = gm_ref[0, :, cols]
        prod_ref[:, cols] = values * grad.astype(f32)
        terms, own, decays = [], [], []
        for side, head in enumerate((2 * pair, 2 * pair + 1)):
            gap = cum_t[head : head + 1, :] - cum[:, head : head + 1]
            decays.append(jnp.exp(jnp.where(causal, gap, -1e30)))
            terms += split(decays[side] * products)
            own += split(jnp.where(left if side == 0 else ~left, scaled, 0.0))
        every = mxu(jnp.concatenate(terms, axis=0), grad, NN)
        cross = mxu(jnp.concatenate(own, axis=0), grad, NT)
        parts = []
        for side, at in enumerate((0, 2 * length)):
            parts.append(every[at : at + length] + every[at + length : at + 2 * length])
            cross_head = cross[at : at + length] + cross[at + length : at + 2 * length]
            grad_products = grad_products + decays[side] * cross_head
        u_ref[0, :, cols] = jnp.where(left, parts[0], parts[1])
    xg_ref[0] = dot2(prod_ref[...], spread, NT)
    dw_ref[0] = dot3(grad_products, read_side, NN)
    dr_ref[0] = dot3(grad_products, write_side, TN) + cread_ref[0]


def scan_within_back(conv, dt, cum, grad_mixed, cread):
    seqs, length, channels = conv.shape
    heads = dt.shape[2]
    inner = heads * HEADDIM
    side = per_seq((length, STATE))
    return call(
        within_back_body,
        seqs,
        [
            per_seq((length, channels)),
            per_seq((length, heads)),
            per_seq((length, heads)),
            per_seq((length, inner)),
            side,
        ],
        [per_seq((length, inner)), side, side, per_seq((length, heads))],
        [
            jax.ShapeDtypeStruct((seqs, length, inner), f32),
            jax.ShapeDtypeStruct((seqs, length, STATE), f32),
            jax.ShapeDtypeStruct((seqs, length, STATE), f32),
            jax.ShapeDtypeStruct((seqs, length, heads), f32),
        ],
        [pltpu.VMEM((length, inner), f32)],
        micros=14,
    )(conv, dt, cum, grad_mixed, cread)


def back_body(
    u_ref, dw_ref, dr_ref, xg_ref, conv_ref, p_ref, dt_ref, cum_ref, gm_ref, gs_ref,
    start_ref, end_ref, cw_ref, dtb_ref, al_ref, skip_ref,
    grad_ref, head_ref, tail_ref, sums_ref,
    state_ref, xw_ref, xu_ref, xs_ref,
):
    length = conv_ref.shape[1]
    channels = conv_ref.shape[2]
    heads = dt_ref.shape[2]
    inner = heads * HEADDIM
    dests, _, _, width = start_ref.shape
    spread = spread_matrix(heads)
    step = dt_ref[0]
    cum = cum_ref[0]
    last = cum[length - 1 :, :]
    weight = jnp.exp(last - cum)
    step_wide = widen(step, spread)
    weight_wide = widen(weight, spread)
    skip_wide = widen_row(skip_ref[...], spread)
    inner_sum = []
    for dest in range(dests):
        cols = slice(dest * width, (dest + 1) * width)
        state_ref[:, cols] = end_ref[dest, 0]
        end = end_ref[dest, 0].astype(f32)
        inner_sum.append(jnp.sum(end * start_ref[dest, 0].astype(f32), axis=0, keepdims=True))
    inner_sum = jnp.concatenate(inner_sum, axis=1)
    write_conv = conv_ref[0, :, inner : inner + STATE]
    write_side = write_conv * sigmoid(write_conv)
    xs_ref[...] = dot2(write_side, state_ref[...], NN) * weight_wide

    start_sums(sums_ref)

    def conv_back(start, grad, conv, sig):
        cols = slice(start, start + 128)
        dconv = grad * (sig * (1.0 + conv * (1.0 - sig)))
        sums_ref[CONV : CONV + 1, cols] += jnp.sum(dconv, axis=0, keepdims=True)
        joined = p_ref[0, :, cols].astype(f32)
        padded = jnp.concatenate([dconv, jnp.zeros((8, 128), f32)], axis=0)
        grad_joined = cw_ref[CONV - 1 : CONV, cols] * dconv
        for tap in range(CONV):
            low = HALO - (CONV - 1) + tap
            sums_ref[tap : tap + 1, cols] += jnp.sum(
                dconv * joined[low : low + length], axis=0, keepdims=True
            )
            if tap < CONV - 1:
                low = CONV - 1 - tap
                grad_joined = grad_joined + cw_ref[tap : tap + 1, cols] * padded[low : low + length]
        grad_ref[0, :, cols] = grad_joined.astype(bf16)
        head_ref[0, :, cols] = dconv[:8]
        tail_ref[0, :, cols] = grad_joined[length - 8 :]

    for start in range(0, inner, 128):
        cols = slice(start, start + 128)
        conv = conv_ref[0, :, cols]
        sig = sigmoid(conv)
        values = conv * sig
        from_state = xs_ref[:, cols]
        total = u_ref[0, :, cols] + from_state
        xu_ref[:, cols] = values * total
        xs_ref[:, cols] = values * from_state
        xw_ref[:, cols] = values * (step_wide[:, cols] * weight_wide[:, cols])
        grad = step_wide[:, cols] * total + skip_wide[:, cols] * gm_ref[0, :, cols].astype(f32)
        conv_back(start, grad, conv, sig)
    grad_write = dw_ref[0] + dot2(xw_ref[...], state_ref[...], NT)
    conv_back(inner, grad_write, write_conv, sigmoid(write_conv))
    read_conv = conv_ref[0, :, inner + STATE :]
    conv_back(inner + STATE, dr_ref[0], read_conv, sigmoid(read_conv))
    direct = dot2(xu_ref[...], spread, NT)
    ends = dot2(xs_ref[...], spread, NT) * step
    held = dot2(jnp.broadcast_to(inner_sum, (16, inner)), spread, NT)[0:1] * jnp.exp(last)
    at_end = jnp.sum(ends, axis=0, keepdims=True) + held
    dcum = gs_ref[0] - skip_ref[...] * xg_ref[0] - step * direct
    sums_ref[CONV + 3 : CONV + 4, :heads] += jnp.sum(xg_ref[0], axis=0, keepdims=True)
    dcum = dcum + jnp.where(iota((length, heads), 0) == length - 1, at_end, 0.0)
    upper = (iota((length, length), 0) <= iota((length, length), 1)).astype(f32)
    da = exact(upper, dcum, NN)
    rate = jnp.exp(al_ref[...])
    sums_ref[CONV + 2 : CONV + 3, :heads] += jnp.sum(da * (-step * rate), axis=0, keepdims=True)
    raw = p_ref[0, HALO:, channels : channels + heads].astype(f32) + dtb_ref[...]
    draw = (direct - da * rate) * sigmoid(raw)
    grad_ref[0, :, channels:] = draw.astype(bf16)
    sums_ref[CONV + 1 : CONV + 2, :heads] += jnp.sum(draw, axis=0, keepdims=True)


def scan_back(u, dw, dr, xg, conv, p_ext, dt, cum, gm, gs, start, end, conv_weight, dt_bias, a_log, skip_gain):
    seqs, length, channels = conv.shape
    heads = dt.shape[2]
    inner = heads * HEADDIM
    dests, _, _, width = start.shape
    row = per_seq((length, inner))
    small = per_seq((length, heads))
    side = per_seq((length, STATE))
    states = per_dest((dests, STATE, width))
    return call(
        back_body,
        seqs,
        [
            row, side, side, small,
            per_seq((length, channels)),
            per_seq(p_ext.shape[1:]),
            small, small, row, small, states, states,
            whole((CONV, channels)),
            whole((1, heads)),
            whole((1, heads)),
            whole((1, heads)),
        ],
        [
            per_seq((length, channels + heads)),
            per_seq((8, channels)),
            per_seq((8, channels)),
            whole((8, channels)),
        ],
        [
            jax.ShapeDtypeStruct((seqs, length, channels + heads), bf16),
            jax.ShapeDtypeStruct((seqs, 8, channels), f32),
            jax.ShapeDtypeStruct((seqs, 8, channels), f32),
            jax.ShapeDtypeStruct((8, channels), f32),
        ],
        [
            pltpu.VMEM((STATE, inner), end.dtype),
            pltpu.VMEM((length, inner), f32),
            pltpu.VMEM((length, inner), f32),
            pltpu.VMEM((length, inner), f32),
        ],
        micros=14,
    )(u, dw, dr, xg, conv, p_ext, dt, cum, gm, gs, start, end, conv_weight,
      dt_bias[None], a_log[None], skip_gain[None])


def swap(x, axis, flip):
    count = lax.axis_size(axis)
    return lax.ppermute(x, axis, [(slot, slot ^ flip) for slot in range(count)])


def small_flips():
    flips = [("seq", 1 << k) for k in range(lax.axis_size("seq").bit_length() - 1)]
    flips[1:1] = [("fsdp", 1 << k) for k in range(lax.axis_size("fsdp").bit_length() - 1)]
    return flips


def one_more(x, flip, *events):
    got = swap(x, *flip)
    return x + (after(got, *events) if events else got)


def shared_slots():
    slot = lax.axis_index("seq")
    return slot // 4, slot // 2 % 2 == 1, slot % 2 == 1, lax.axis_index("fsdp") == 1


def fast_mesh():
    return lax.axis_size("fsdp") == 2 and lax.axis_size("seq") == 16


def halves(x, flag, axis):
    size = x.shape[axis] // 2
    low = lax.slice_in_dim(x, 0, size, axis=axis)
    high = lax.slice_in_dim(x, size, 2 * size, axis=axis)
    return jnp.where(flag, high, low), jnp.where(flag, low, high)


def join(own, other, flag, axis):
    low = jnp.where(flag, other, own)
    high = jnp.where(flag, own, other)
    return jnp.concatenate([low, high], axis=axis)


def after(x, *others):
    return lax.optimization_barrier((x,) + others)[0]


def fetch_rows(w, start=None, late=None):
    _, _, odd, _ = shared_slots()
    mine, _ = halves(w, odd, 0)
    if start is not None:
        mine = after(mine, start)
    fetched = swap(mine, "fsdp", 1)
    if late is not None:
        fetched = after(fetched, late)
    return fetched, swap(fetched, "seq", 1)


def gather_rows(w, start=None, late=None):
    if not fast_mesh():
        return lax.all_gather(w, "fsdp", axis=0, tiled=True)
    _, _, odd, second = shared_slots()
    fetched, shared = fetch_rows(w, start, late)
    return join(w, join(fetched, shared, odd, 0), second, 0)


def reduce_rows(part):
    shard = lax.psum_scatter(part, "fsdp", scatter_dimension=0, tiled=True)
    return lax.psum(shard, "seq")


def send_half(total, axis, flip, dim):
    size = total[0].shape[dim] // 2
    keep = [lax.slice_in_dim(term, 0, size, axis=dim).astype(f32) for term in total]
    give = [lax.slice_in_dim(term, size, 2 * size, axis=dim).astype(f32) for term in total]
    return [sum(keep[1:], keep[0]), swap(sum(give[1:], give[0]).astype(bf16), axis, flip)]


def held(sent, *events):
    return [sent[0]] + [after(piece, *events) for piece in sent[1:]]


def fold_z(total, flag, flip):
    keep, give = halves(total, flag, 0)
    return keep[0], swap(give[0].astype(bf16), "seq", flip)


def both(own, got):
    return jnp.stack([own, got])


def place_body(plan, slots_ref, *refs):
    outs = refs[-1:]
    z, x, core = slots_ref[0], slots_ref[1], slots_ref[2]
    for source, first, rows, base, wide in plan:
        for side in range(2):
            for k in range(2):
                src = refs[4 + side] if source else refs[2 * side + k]
                at = (lax.rem(core + side, 2) * 2 + lax.rem(x + k, 2)) * 128 * wide
                for shift in range(4):
                    low_bit = lax.rem(z + shift // 2, 2)
                    high_bit = lax.rem(z // 2 + shift % 2, 2)
                    row = base + (2 * high_bit + low_bit) * rows
                    for part in range(wide):
                        low = first + part * rows
                        outs[0][
                            pl.ds(pl.multiple_of(row, 8), rows),
                            pl.ds(pl.multiple_of(at + part * 128, 128), 128),
                        ] = (
                            src[shift // 2, shift % 2, k, low : low + rows, :]
                            if source
                            else src[shift // 2, shift % 2, low : low + rows, :]
                        ).astype(f32)


def place(slots, plan, arrays, shape):
    return pl.pallas_call(
        functools.partial(place_body, plan),
        in_specs=[pl.BlockSpec(memory_space=pltpu.SMEM)]
        + [pl.BlockSpec(memory_space=pltpu.VMEM)] * len(arrays),
        out_specs=pl.BlockSpec(memory_space=pltpu.VMEM),
        out_shape=jax.ShapeDtypeStruct(shape, f32),
        compiler_params=pltpu.CompilerParams(vmem_limit_bytes=VMEM_BYTES),
        cost_estimate=cost(6),
    )(slots, *arrays)


def dot(a, b, dims):
    return lax.dot_general(a, b, (dims, ((), ())), preferred_element_type=f32)


STATE_TYPE = bf16


def per_device(
    hidden_in, cotangent, norm_gain, in_weight, conv_weight, conv_bias,
    dt_bias, a_log, skip_gain, gate_gain, out_weight,
):
    seq_count = lax.axis_size("seq")
    seqs, length, width = hidden_in.shape
    rows = seqs * length
    heads = dt_bias.shape[0]
    inner = heads * HEADDIM
    forward = [(slot, slot + 1) for slot in range(seq_count - 1)]
    backward = [(slot + 1, slot) for slot in range(seq_count - 1)]
    fast = fast_mesh()

    w_gate, w_scan = in_weight[:, :inner], in_weight[:, inner:]
    if fast:
        z, x, odd, second = shared_slots()
        scan_give = halves(w_scan, odd, 0)[0]
        hidden_in = after(hidden_in, scan_give)
        scan_fetched = swap(scan_give, "fsdp", 1)
        slots = jnp.stack([z, x.astype(jnp.int32), odd.astype(jnp.int32)]).astype(jnp.int32)

    def prenorm(rows_in):
        inv = lax.rsqrt(jnp.mean(rows_in * rows_in, axis=-1, keepdims=True) + norm_eps)
        return inv, (rows_in * inv * norm_gain).astype(bf16)

    residual = hidden_in.astype(f32)
    inv_rms, scaled_low = prenorm(residual)
    halo = after(hidden_in, scaled_low)[:, length - HALO :]
    halo = lax.ppermute(halo, "seq", forward)
    _, scaled_halo = prenorm(halo.astype(f32))
    scaled_ext = jnp.concatenate([scaled_halo, scaled_low], axis=1)
    scaled_ext = scaled_ext.reshape(seqs * (HALO + length), width)
    scaled_low = scaled_low.reshape(rows, width)
    if fast:
        ext_own, ext_other = halves(scaled_ext, second, 1)
        ext_fetched, ext_shared = halves(ext_other, odd, 1)
        p_ext = dot(ext_own, w_scan, NN)
        scan_fetched = after(scan_fetched, p_ext)
        scan_shared = swap(scan_fetched, "seq", 1)
        p_ext = p_ext + dot(ext_fetched, scan_fetched, NN)
        p_ext = p_ext + dot(ext_shared, scan_shared, NN)
    else:
        scan_full = lax.all_gather(w_scan, "fsdp", axis=0, tiled=True)
        p_ext = dot(scaled_ext, scan_full, NN)
    p_ext = p_ext.astype(bf16).reshape(seqs, HALO + length, -1)

    conv, dt, cum, send = scan_front(
        p_ext, conv_weight, conv_bias, dt_bias, a_log, seq_count, STATE_TYPE
    )
    recv = lax.all_to_all(send, "seq", split_axis=0, concat_axis=0, tiled=True)
    y = scan_within(conv, dt, cum, skip_gain)
    grad_rows = cotangent.reshape(rows, width)
    ready = [y]
    if fast:
        own_side, other_side = halves(scaled_low, second, 1)
        quarters = [halves(side, odd, 1) for side in (own_side, other_side)]
        eighths = [[halves(quarter, x, 1) for quarter in pair] for pair in quarters]
        by_y = [
            jnp.concatenate([eighths[y_side][c][k] for y_side in (0, 1) for k in (0, 1)], axis=1)
            for c in (0, 1)
        ]
        by_x = [
            jnp.concatenate([eighths[y_side][c][k] for k in (0, 1) for y_side in (0, 1)], axis=1)
            for c in (0, 1)
        ]

        sides = [halves(side, x, 1) for side in halves(grad_rows, odd, 1)]
        cot = [jnp.concatenate(side, axis=1) for side in sides]
        ready += by_y + by_x + cot
    start_heads, decay = combine(recv, ready)
    gate_full = gather_rows(w_gate, conv, recv)
    out_full = gather_rows(out_weight, start_heads)
    start = lax.all_to_all(start_heads, "seq", split_axis=0, concat_axis=0, tiled=True)
    gate = dot(scaled_low, gate_full, NN).astype(bf16).reshape(seqs, length, inner)
    grad_normed = dot(grad_rows, out_full, NT).reshape(seqs, length, inner)
    normed, grad_gate, grad_mixed, back_send, gate_sums, gs, cread = middle(
        y, conv, cum, start, gate, gate_gain, grad_normed
    )
    back_recv = lax.all_to_all(back_send, "seq", split_axis=0, concat_axis=0, tiled=True)
    normed = normed.reshape(rows, inner)
    grad_gate = grad_gate.reshape(rows, inner)
    if fast:
        scan_full = join(w_scan, join(scan_fetched, scan_shared, odd, 0), second, 0)
        def near(left, right, *events):
            give = dot(left, right[1], TN).astype(bf16)
            keep = dot(left, right[0], TN)
            return held([keep, swap(give, "seq", 1)], *events)

        out_left = jnp.concatenate(halves(normed, second, 1), axis=1)
        gate_y = send_half(near(grad_gate, by_y), "fsdp", 1, 1)
        out_x = send_half(near(out_left, cot), "seq", 2, 1)
        ready = [out_x[0], gate_y[0]]
    else:
        out_total = reduce_rows(dot(normed, grad_rows, TN))
        gate_total = reduce_rows(dot(scaled_low, grad_gate, TN))
        ready = []
    end_heads = combine_back(back_recv, decay, ready)
    u, dw, dr, xg = scan_within_back(conv, dt, cum, after(grad_mixed, back_recv), cread)
    end = lax.all_to_all(end_heads, "seq", split_axis=0, concat_axis=0, tiled=True)
    hidden_out = (residual.reshape(rows, width) + dot(normed, out_full, NN)).astype(bf16)
    grad_scan, head, tail, conv_sums = scan_back(
        u, dw, dr, xg, conv, p_ext, dt, cum, grad_mixed, gs, start, end,
        conv_weight, dt_bias, a_log, skip_gain,
    )
    grad_raw = grad_scan
    following = lax.ppermute(head, "seq", backward)
    if fast:
        out_y = send_half(held(out_x, grad_raw), "fsdp", 1, 0)
        gate_x = send_half(held(gate_y, grad_raw), "seq", 2, 1)
    for tap in range(CONV - 1):
        reach = following[:, : CONV - 1 - tap]
        low = 8 - (CONV - 1) + tap
        tail = tail + conv_weight[tap] * jnp.pad(reach, ((0, 0), (low, 0), (0, 0)))
    grad_scan = lax.dynamic_update_slice(grad_scan, tail.astype(bf16), (0, length - 8, 0))
    grad_scan = grad_scan.reshape(rows, -1)

    held_back = []

    def lined_up(grad_scan, *events):
        if events:
            grad_scan = after(grad_scan, *events)
        grad_scaled = dot(grad_gate, gate_full, NT) + dot(grad_scan, scan_full, NT)
        rows_in = residual.reshape(rows, width)
        inv = inv_rms.reshape(rows, 1)
        norm_part = jnp.sum(grad_scaled * rows_in * inv, axis=0)
        f = norm_gain * grad_scaled
        mean = jnp.mean(rows_in * f, axis=-1, keepdims=True)
        held_back.append(grad_rows.astype(f32) + inv * f - rows_in * (inv * inv * inv * mean))
        lanes = conv_sums.shape[1]
        wide = [conv_sums[: CONV + 4], gate_sums[:1], norm_part[None]]
        wide = [jnp.pad(part, ((0, 0), (0, lanes - part.shape[1]))) for part in wide]
        return jnp.concatenate(wide, axis=0)

    if fast:
        cut = grad_scan.shape[1] // 64 * 32
        first = near(grad_scan[:, :cut], by_y)
        rest = near(grad_scan[:, cut:], by_x)
        first_y = send_half(first, "fsdp", 1, 1)
        rest_x = send_half(rest, "seq", 2, 1)
        waited = [held(out_y, rest_x[0]), held(gate_x, rest_x[0])]
        out_sum, gate_sum = [pair[0] + pair[1].astype(f32) for pair in waited]
        out_sum = out_sum.reshape(4, -1, 256)
        early = jnp.concatenate(
            [out_sum[:, :, :128], out_sum[:, :, 128:], gate_sum.reshape(4, -1, 128)], axis=1
        )
        low_bit, high_bit = z % 2 == 1, z // 2 == 1
        early = early.reshape(2, 2, -1, 128).swapaxes(0, 1)
        early_low = fold_z(early, low_bit, 4)
        sums = lined_up(grad_scan, first_y[0], rest_x[0])
        first_x = send_half(held(first_y, sums), "seq", 2, 1)
        rest_y = send_half(rest_x, "fsdp", 1, 1)
        flips = [("seq", 8), ("seq", 1), ("seq", 2), ("fsdp", 1), ("seq", 4)]
        sums = one_more(sums, flips[0])
        early_sum = early_low[0] + after(early_low[1], first_x[0], rest_y[0]).astype(f32)
        early_high = fold_z(early_sum, high_bit, 8)
        pair = [sent[0] + after(sent[1], sums).astype(f32) for sent in (first_x, rest_y)]
        late_cut = pair[0].shape[0] // 4
        late = jnp.concatenate([half.reshape(4, -1, 128) for half in pair], axis=1)
        late = late.reshape(2, 2, -1, 128).swapaxes(0, 1)
        late_low = fold_z(late, low_bit, 4)
        sums = one_more(after(sums, first_x[0], rest_y[0]), flips[1])
        early_sum = early_high[0] + after(early_high[1], late_low[0]).astype(f32)
        early_own = early_sum.astype(bf16)
        early_own = both(early_own, swap(early_own, "seq", 8))
        late_sum = late_low[0] + after(late_low[1], sums).astype(f32)
        late_high = fold_z(late_sum, high_bit, 8)
        early_own = after(early_own, late_high[0])
        sums = one_more(after(sums, late_low[0]), flips[2])
        early_near = both(early_own, swap(early_own, "seq", 4))
        late_got = after(late_high[1], sums, hidden_out, held_back[0])
        late_own = (late_high[0] + late_got.astype(f32)).astype(bf16)
        sums = one_more(after(sums, late_high[0]), flips[3])
        late_all = both(late_own, after(swap(late_own, "seq", 2), sums))
        early_near = after(early_near, late_own)
        early_far = swap(early_near, "seq", 2)
        sums = one_more(after(sums, late_own), flips[4])
        late_wide = both(late_all, after(swap(late_all, "seq", 8), sums))
        near_other = swap(early_near, "seq", 1)
        late_all = both(late_wide, swap(late_wide, "seq", 4))
        early_four = [early_near, early_far, near_other, swap(early_far, "seq", 1)]
        late_two = [late_all, swap(late_all, "seq", 1)]
        size = out_weight.shape[0] // 4
        out_total = place(slots, [(0, 0, size, 0, 2)], early_four, out_weight.shape)
    if not fast:
        sums = lined_up(grad_scan)
        for flip in small_flips():
            sums = one_more(sums, flip)
    grad_hidden = held_back[0]
    conv_sum, bias_sum = sums[:CONV], sums[CONV]
    shift_sum, rate_sum = sums[CONV + 1, :heads], sums[CONV + 2, :heads]
    skip_sum, gain_sum = sums[CONV + 3, :heads], sums[CONV + 4, :inner]
    norm_sum = sums[CONV + 5, :width]
    if fast:
        late_two[1] = after(late_two[1], out_total, skip_sum)
        plan = [
            (0, 2 * size, inner // 4, 0, 1),
            (1, 0, late_cut, inner, 1),
            (1, late_cut, late.shape[2] - late_cut, inner + cut, 1),
        ]
        in_total = place(slots, plan, early_four + late_two, in_weight.shape[::-1]).T
    else:
        in_total = jnp.concatenate(
            [gate_total, reduce_rows(dot(scaled_low, grad_scan, TN))], axis=1
        )
    return (
        hidden_out.reshape(hidden_in.shape),
        grad_hidden.reshape(hidden_in.shape),
        norm_sum,
        in_total,
        conv_sum,
        bias_sum,
        shift_sum,
        rate_sum,
        skip_sum,
        gain_sum,
        out_total,
    )


def solution(mesh):
    tokens = P("fsdp", "seq", None)
    weights = P("fsdp", None)
    return jax.shard_map(
        per_device,
        mesh=mesh,
        in_specs=(tokens, tokens, P(), weights, P(), P(), P(), P(), P(), P(), weights),
        out_specs=(tokens, tokens, P(), weights, P(), P(), P(), P(), P(), P(), weights),
        check_vma=False,
    )
```

```python
import functools

import jax
import jax.numpy as jnp
from jax import lax
from jax.experimental import pallas as pl
from jax.experimental.pallas import tpu as pltpu
from jax.sharding import PartitionSpec as P

HEADDIM = 64
STATE = 128
CONV = 4
HALO = 16
EXTRA = 16
norm_eps = 1e-05
VMEM_BYTES = 56 * 1024 * 1024
f32 = jnp.float32
bf16 = jnp.bfloat16


def exact(a, b, dims):
    return lax.dot_general(
        a, b, (dims, ((), ())), precision=lax.Precision.HIGHEST, preferred_element_type=f32
    )


NN = ((1,), (0,))
TN = ((0,), (0,))
NT = ((1,), (1,))


def iota(shape, dim):
    return lax.broadcasted_iota(jnp.int32, shape, dim)


def split(a):
    high = a.astype(bf16)
    return high, (a - high.astype(f32)).astype(bf16)


def mxu(a, b, dims):
    return lax.dot_general(a, b, (dims, ((), ())), preferred_element_type=f32)


def dot3(a, b, dims):
    a_high, a_low = split(a)
    b_high, b_low = split(b)
    return mxu(a_high, b_high, dims) + (mxu(a_high, b_low, dims) + mxu(a_low, b_high, dims))


def dot2(a, b, dims):
    a_high, a_low = split(a)
    return mxu(a_high, b, dims) + mxu(a_low, b, dims)


def spread_matrix(heads):
    shape = (heads, heads * HEADDIM)
    return (iota(shape, 1) // HEADDIM == iota(shape, 0)).astype(f32).astype(bf16)


def widen(a, spread):
    high, low = split(a)
    return mxu(jnp.concatenate([high, low], axis=1), jnp.concatenate([spread, spread], axis=0), NN)


def widen_row(a, spread):
    high, low = split(jnp.broadcast_to(a, (16, a.shape[1])))
    rest = a - high[0:1].astype(f32) - low[0:1].astype(f32)
    rest = jnp.broadcast_to(rest, (16, a.shape[1])).astype(bf16)
    return (mxu(high, spread, NN) + (mxu(low, spread, NN) + mxu(rest, spread, NN)))[0:1]


def sigmoid(v):
    return 0.5 * jnp.tanh(0.5 * v) + 0.5


def start_sums(ref):
    @pl.when(pl.program_id(0) == 0)
    def _():
        ref[...] = jnp.zeros(ref.shape, f32)


def softplus(v):
    return jnp.maximum(v, 0.0) + jnp.log1p(jnp.exp(-jnp.abs(v)))


def whole(shape):
    return pl.BlockSpec(shape, lambda g: (0,) * len(shape))


def per_seq(shape):
    return pl.BlockSpec((1,) + shape, lambda g: (g,) + (0,) * len(shape))


def per_dest(shape):
    return pl.BlockSpec(
        (shape[0], 1) + shape[1:], lambda g: (0, g) + (0,) * (len(shape) - 1)
    )


def cost(micros):
    return pl.CostEstimate(flops=0, bytes_accessed=int(micros * 0.7e6), transcendentals=0)


def call(body, grid, in_specs, out_specs, out_shape, scratch=(), micros=10):
    return pl.pallas_call(
        body,
        grid=(grid,),
        in_specs=in_specs,
        out_specs=out_specs,
        out_shape=out_shape,
        scratch_shapes=list(scratch),
        compiler_params=pltpu.CompilerParams(vmem_limit_bytes=VMEM_BYTES),
        cost_estimate=cost(micros),
    )


def front_body(dests, p_ref, cw_ref, cb_ref, dtb_ref, al_ref, conv_ref, dt_ref, cum_ref, send_ref, xw_ref):
    length = conv_ref.shape[1]
    channels = conv_ref.shape[2]
    heads = dt_ref.shape[2]
    inner = heads * HEADDIM
    step = softplus(p_ref[0, HALO:, channels : channels + heads].astype(f32) + dtb_ref[...])
    decay = -step * jnp.exp(al_ref[...])
    lower = (iota((length, length), 0) >= iota((length, length), 1)).astype(f32)
    cum = exact(lower, decay, NN)
    dt_ref[0] = step
    cum_ref[0] = cum
    last = cum[length - 1 :, :]
    weight = jnp.exp(last - cum) * step
    spread = spread_matrix(heads)
    weight_wide = widen(weight, spread)
    last_wide = widen_row(last, spread)
    write_side = None
    for start in list(range(inner, channels, 128)) + list(range(0, inner, 128)):
        cols = slice(start, start + 128)
        joined = p_ref[0, :, cols].astype(f32)
        total = cb_ref[:, cols]
        for tap in range(CONV):
            low = HALO - (CONV - 1) + tap
            total = total + cw_ref[tap : tap + 1, cols] * joined[low : low + length]
        conv_ref[0, :, cols] = total
        if start == inner:
            write_side = total * sigmoid(total)
        elif start < inner:
            xw_ref[:, cols] = total * sigmoid(total) * weight_wide[:, cols]
    state = dot3(write_side, xw_ref[...], TN)
    width = send_ref.shape[3]
    hi = last_wide.astype(bf16)
    rest = last_wide - hi.astype(f32)
    mid = rest.astype(bf16)
    low_part = (rest - mid.astype(f32)).astype(bf16)
    row = iota((EXTRA, inner), 0)
    tail = jnp.where(
        row == 0,
        hi.astype(f32),
        jnp.where(row == 1, mid.astype(f32), jnp.where(row == 2, low_part.astype(f32), 0.0)),
    )
    for dest in range(dests):
        cols = slice(dest * width, (dest + 1) * width)
        send_ref[dest, 0, :STATE, :] = state[:, cols].astype(send_ref.dtype)
        send_ref[dest, 0, STATE:, :] = tail[:, cols].astype(send_ref.dtype)


def scan_front(p_ext, conv_weight, conv_bias, dt_bias, a_log, dests, kind):
    seqs, rows, _ = p_ext.shape
    length = rows - HALO
    heads = dt_bias.shape[0]
    inner = heads * HEADDIM
    channels = inner + 2 * STATE
    width = inner // dests
    return call(
        functools.partial(front_body, dests),
        seqs,
        [
            per_seq(p_ext.shape[1:]),
            whole((CONV, channels)),
            whole((1, channels)),
            whole((1, heads)),
            whole((1, heads)),
        ],
        [
            per_seq((length, channels)),
            per_seq((length, heads)),
            per_seq((length, heads)),
            per_dest((dests, STATE + EXTRA, width)),
        ],
        [
            jax.ShapeDtypeStruct((seqs, length, channels), f32),
            jax.ShapeDtypeStruct((seqs, length, heads), f32),
            jax.ShapeDtypeStruct((seqs, length, heads), f32),
            jax.ShapeDtypeStruct((dests, seqs, STATE + EXTRA, width), kind),
        ],
        [pltpu.VMEM((length, inner), f32)],
        micros=9,
    )(p_ext, conv_weight, conv_bias[None], dt_bias[None], a_log[None])


def combine_body(recv_ref, *refs):
    start_ref, decay_ref = refs[-2:]
    dests, seqs, _, width = recv_ref.shape
    for seq in range(seqs):
        state = jnp.zeros((STATE, width), f32)
        for src in range(dests):
            start_ref[src, seq] = state.astype(start_ref.dtype)
            total = recv_ref[src, seq, STATE:, :].astype(f32)
            decay = jnp.exp(total[0:1] + total[1:2] + total[2:3])
            decay_ref[src, seq] = jnp.broadcast_to(decay, (8, width))
            state = decay * state + recv_ref[src, seq, :STATE, :].astype(f32)


def combine(recv, ready):
    dests, seqs, _, width = recv.shape
    return pl.pallas_call(
        combine_body,
        in_specs=[pl.BlockSpec(memory_space=pltpu.VMEM)]
        + [pl.BlockSpec(memory_space=pl.ANY)] * len(ready),
        out_shape=[
            jax.ShapeDtypeStruct((dests, seqs, STATE, width), recv.dtype),
            jax.ShapeDtypeStruct((dests, seqs, 8, width), f32),
        ],
        compiler_params=pltpu.CompilerParams(vmem_limit_bytes=VMEM_BYTES),
        cost_estimate=cost(2.5),
    )(recv, *ready)


def combine_back_body(recv_ref, decay_ref, *refs):
    end_ref = refs[-1]
    dests, seqs, _, width = recv_ref.shape
    for seq in range(seqs):
        state = jnp.zeros((STATE, width), f32)
        for src in reversed(range(dests)):
            end_ref[src, seq] = state.astype(end_ref.dtype)
            state = decay_ref[src, seq, 0:1] * state + recv_ref[src, seq].astype(f32)


def combine_back(recv, decay, ready):
    return pl.pallas_call(
        combine_back_body,
        in_specs=[pl.BlockSpec(memory_space=pltpu.VMEM)] * 2
        + [pl.BlockSpec(memory_space=pl.ANY)] * len(ready),
        out_shape=jax.ShapeDtypeStruct(recv.shape, recv.dtype),
        compiler_params=pltpu.CompilerParams(vmem_limit_bytes=VMEM_BYTES),
        cost_estimate=cost(2.5),
    )(recv, decay, *ready)


def columns(array):
    length = array.shape[0]
    eye = (iota((length, length), 0) == iota((length, length), 1)).astype(f32)
    return exact(array, eye, TN)


def within_body(conv_ref, dt_ref, cum_ref, skip_ref, y_ref):
    length = conv_ref.shape[1]
    heads = dt_ref.shape[2]
    inner = heads * HEADDIM
    write_conv = conv_ref[0, :, inner : inner + STATE]
    read_conv = conv_ref[0, :, inner + STATE :]
    products = dot3(read_conv * sigmoid(read_conv), write_conv * sigmoid(write_conv), NT)
    cum = cum_ref[0]
    cum_t = columns(cum)
    spread = spread_matrix(heads)
    dt_wide = widen(dt_ref[0], spread)
    skip_wide = widen_row(skip_ref[...], spread)
    causal = iota((length, length), 0) >= iota((length, length), 1)
    left = iota((length, 2 * HEADDIM), 1) < HEADDIM
    for pair in range(heads // 2):
        cols = slice(pair * 2 * HEADDIM, (pair + 1) * 2 * HEADDIM)
        conv = conv_ref[0, :, cols]
        values = conv * sigmoid(conv)
        scaled = values * dt_wide[:, cols]
        terms = []
        for head in (2 * pair, 2 * pair + 1):
            gap = cum[:, head : head + 1] - cum_t[head : head + 1, :]
            terms += split(jnp.exp(jnp.where(causal, gap, -1e30)) * products)
        every = mxu(
            jnp.concatenate(terms, axis=0), jnp.concatenate(split(scaled), axis=1), NN
        )
        high, low = every[:, : 2 * HEADDIM], every[:, 2 * HEADDIM :]
        parts = [
            high[at : at + length] + (low[at : at + length] + high[at + length : at + 2 * length])
            for at in (0, 2 * length)
        ]
        y_ref[0, :, cols] = jnp.where(left, parts[0], parts[1]) + skip_wide[:, cols] * values


def scan_within(conv, dt, cum, skip_gain):
    seqs, length, channels = conv.shape
    heads = dt.shape[2]
    inner = heads * HEADDIM
    return call(
        within_body,
        seqs,
        [
            per_seq((length, channels)),
            per_seq((length, heads)),
            per_seq((length, heads)),
            whole((1, heads)),
        ],
        per_seq((length, inner)),
        jax.ShapeDtypeStruct((seqs, length, inner), f32),
        micros=9,
    )(conv, dt, cum, skip_gain[None])


def middle_body(
    y_ref, conv_ref, cum_ref, start_ref, gate_ref, gain_ref, gn_ref,
    normed_ref, gg_ref, gm_ref, send_ref, sums_ref, gs_ref, cread_ref,
    state_ref, scan_ref, gated_ref,
):
    length = cum_ref.shape[1]
    heads = cum_ref.shape[2]
    inner = heads * HEADDIM
    dests, _, _, width = start_ref.shape
    for dest in range(dests):
        state_ref[:, dest * width : (dest + 1) * width] = start_ref[dest, 0]
    read_conv = conv_ref[0]
    read_side = read_conv * sigmoid(read_conv)
    spread = spread_matrix(heads)
    grow_wide = widen(jnp.exp(cum_ref[0]), spread)
    scan_ref[...] = dot2(read_side, state_ref[...], NN) * grow_wide + y_ref[0]
    start_sums(sums_ref)
    square = jnp.zeros((length, 128), f32)
    for start in range(0, inner, 128):
        cols = slice(start, start + 128)
        mixed = scan_ref[:, cols].astype(bf16).astype(f32)
        gate = gate_ref[0, :, cols].astype(f32)
        gated = mixed * (gate * sigmoid(gate))
        gated_ref[:, cols] = gated
        square = square + gated * gated
    inv = lax.rsqrt(jnp.sum(square, axis=1, keepdims=True) / inner + norm_eps)
    cross = jnp.zeros((length, 128), f32)
    for start in range(0, inner, 128):
        cols = slice(start, start + 128)
        grad = gn_ref[0, :, cols]
        unit = gated_ref[:, cols] * inv
        normed_ref[0, :, cols] = (unit * gain_ref[:, cols]).astype(bf16)
        per_gain = grad * unit
        sums_ref[0:1, cols] += jnp.sum(per_gain, axis=0, keepdims=True)
        cross = cross + per_gain * gain_ref[:, cols]
    mean = jnp.sum(cross, axis=1, keepdims=True) / inner
    factor = inv * inv * mean
    for start in range(0, inner, 128):
        cols = slice(start, start + 128)
        scanned = scan_ref[:, cols]
        gate = gate_ref[0, :, cols].astype(f32)
        sig = sigmoid(gate)
        grad_gated = inv * (gain_ref[:, cols] * gn_ref[0, :, cols]) - gated_ref[:, cols] * factor
        mixed = scanned.astype(bf16).astype(f32)
        gg_ref[0, :, cols] = (grad_gated * mixed * (sig * (1.0 + gate * (1.0 - sig)))).astype(bf16)
        grad_low = (grad_gated * (gate * sig)).astype(bf16)
        gm_ref[0, :, cols] = grad_low
        grad_mixed = grad_low.astype(f32)
        scan_ref[:, cols] = scanned * grad_mixed
        gated_ref[:, cols] = grad_mixed * grow_wide[:, cols]
    gs_ref[0] = dot2(scan_ref[...], spread, NT)
    cread_ref[0] = dot2(gated_ref[...], state_ref[...], NT)
    back = dot3(read_side, gated_ref[...], TN)
    for dest in range(dests):
        send_ref[dest, 0] = back[:, dest * width : (dest + 1) * width].astype(send_ref.dtype)


def middle(y, conv, cum, start, gate, gate_gain, grad_normed):
    seqs, length, channels = conv.shape
    heads = cum.shape[2]
    inner = heads * HEADDIM
    dests, _, _, width = start.shape
    row = per_seq((length, inner))
    return call(
        middle_body,
        seqs,
        [
            row,
            pl.BlockSpec((1, length, STATE), lambda g: (g, 0, inner // STATE + 1)),
            per_seq((length, heads)),
            per_dest((dests, STATE, width)),
            row,
            whole((1, inner)),
            row,
        ],
        [
            row, row, row,
            per_dest((dests, STATE, width)),
            whole((8, inner)),
            per_seq((length, heads)),
            per_seq((length, STATE)),
        ],
        [
            jax.ShapeDtypeStruct((seqs, length, inner), bf16),
            jax.ShapeDtypeStruct((seqs, length, inner), bf16),
            jax.ShapeDtypeStruct((seqs, length, inner), bf16),
            jax.ShapeDtypeStruct(start.shape, start.dtype),
            jax.ShapeDtypeStruct((8, inner), f32),
            jax.ShapeDtypeStruct((seqs, length, heads), f32),
            jax.ShapeDtypeStruct((seqs, length, STATE), f32),
        ],
        [
            pltpu.VMEM((STATE, inner), start.dtype),
            pltpu.VMEM((length, inner), f32),
            pltpu.VMEM((length, inner), f32),
        ],
        micros=12,
    )(y, conv, cum, start, gate, gate_gain[None], grad_normed)


def within_back_body(
    conv_ref, dt_ref, cum_ref, gm_ref, cread_ref, u_ref, dw_ref, dr_ref, xg_ref, prod_ref
):
    length = conv_ref.shape[1]
    heads = dt_ref.shape[2]
    inner = heads * HEADDIM
    write_conv = conv_ref[0, :, inner : inner + STATE]
    read_conv = conv_ref[0, :, inner + STATE :]
    write_side = write_conv * sigmoid(write_conv)
    read_side = read_conv * sigmoid(read_conv)
    products = dot3(write_side, read_side, NT)
    cum = cum_ref[0]
    cum_t = columns(cum)
    spread = spread_matrix(heads)
    dt_wide = widen(dt_ref[0], spread)
    causal = iota((length, length), 0) <= iota((length, length), 1)
    left = iota((length, 2 * HEADDIM), 1) < HEADDIM
    grad_products = jnp.zeros((length, length), f32)
    for pair in range(heads // 2):
        cols = slice(pair * 2 * HEADDIM, (pair + 1) * 2 * HEADDIM)
        conv = conv_ref[0, :, cols]
        values = conv * sigmoid(conv)
        scaled = values * dt_wide[:, cols]
        grad = gm_ref[0, :, cols]
        prod_ref[:, cols] = values * grad.astype(f32)
        terms, own, decays = [], [], []
        for side, head in enumerate((2 * pair, 2 * pair + 1)):
            gap = cum_t[head : head + 1, :] - cum[:, head : head + 1]
            decays.append(jnp.exp(jnp.where(causal, gap, -1e30)))
            terms += split(decays[side] * products)
            own += split(jnp.where(left if side == 0 else ~left, scaled, 0.0))
        every = mxu(jnp.concatenate(terms, axis=0), grad, NN)
        cross = mxu(jnp.concatenate(own, axis=0), grad, NT)
        parts = []
        for side, at in enumerate((0, 2 * length)):
            parts.append(every[at : at + length] + every[at + length : at + 2 * length])
            cross_head = cross[at : at + length] + cross[at + length : at + 2 * length]
            grad_products = grad_products + decays[side] * cross_head
        u_ref[0, :, cols] = jnp.where(left, parts[0], parts[1])
    xg_ref[0] = dot2(prod_ref[...], spread, NT)
    dw_ref[0] = dot3(grad_products, read_side, NN)
    dr_ref[0] = dot3(grad_products, write_side, TN) + cread_ref[0]


def scan_within_back(conv, dt, cum, grad_mixed, cread):
    seqs, length, channels = conv.shape
    heads = dt.shape[2]
    inner = heads * HEADDIM
    side = per_seq((length, STATE))
    return call(
        within_back_body,
        seqs,
        [
            per_seq((length, channels)),
            per_seq((length, heads)),
            per_seq((length, heads)),
            per_seq((length, inner)),
            side,
        ],
        [per_seq((length, inner)), side, side, per_seq((length, heads))],
        [
            jax.ShapeDtypeStruct((seqs, length, inner), f32),
            jax.ShapeDtypeStruct((seqs, length, STATE), f32),
            jax.ShapeDtypeStruct((seqs, length, STATE), f32),
            jax.ShapeDtypeStruct((seqs, length, heads), f32),
        ],
        [pltpu.VMEM((length, inner), f32)],
        micros=14,
    )(conv, dt, cum, grad_mixed, cread)


def back_body(
    u_ref, dw_ref, dr_ref, xg_ref, conv_ref, p_ref, dt_ref, cum_ref, gm_ref, gs_ref,
    start_ref, end_ref, cw_ref, dtb_ref, al_ref, skip_ref,
    grad_ref, head_ref, tail_ref, sums_ref,
    state_ref, xw_ref, xu_ref, xs_ref,
):
    length = conv_ref.shape[1]
    channels = conv_ref.shape[2]
    heads = dt_ref.shape[2]
    inner = heads * HEADDIM
    dests, _, _, width = start_ref.shape
    spread = spread_matrix(heads)
    step = dt_ref[0]
    cum = cum_ref[0]
    last = cum[length - 1 :, :]
    weight = jnp.exp(last - cum)
    step_wide = widen(step, spread)
    weight_wide = widen(weight, spread)
    skip_wide = widen_row(skip_ref[...], spread)
    inner_sum = []
    for dest in range(dests):
        cols = slice(dest * width, (dest + 1) * width)
        state_ref[:, cols] = end_ref[dest, 0]
        end = end_ref[dest, 0].astype(f32)
        inner_sum.append(jnp.sum(end * start_ref[dest, 0].astype(f32), axis=0, keepdims=True))
    inner_sum = jnp.concatenate(inner_sum, axis=1)
    write_conv = conv_ref[0, :, inner : inner + STATE]
    write_side = write_conv * sigmoid(write_conv)
    xs_ref[...] = dot2(write_side, state_ref[...], NN) * weight_wide

    start_sums(sums_ref)

    def conv_back(start, grad, conv, sig):
        cols = slice(start, start + 128)
        dconv = grad * (sig * (1.0 + conv * (1.0 - sig)))
        sums_ref[CONV : CONV + 1, cols] += jnp.sum(dconv, axis=0, keepdims=True)
        joined = p_ref[0, :, cols].astype(f32)
        padded = jnp.concatenate([dconv, jnp.zeros((8, 128), f32)], axis=0)
        grad_joined = cw_ref[CONV - 1 : CONV, cols] * dconv
        for tap in range(CONV):
            low = HALO - (CONV - 1) + tap
            sums_ref[tap : tap + 1, cols] += jnp.sum(
                dconv * joined[low : low + length], axis=0, keepdims=True
            )
            if tap < CONV - 1:
                low = CONV - 1 - tap
                grad_joined = grad_joined + cw_ref[tap : tap + 1, cols] * padded[low : low + length]
        grad_ref[0, :, cols] = grad_joined.astype(bf16)
        head_ref[0, :, cols] = dconv[:8]
        tail_ref[0, :, cols] = grad_joined[length - 8 :]

    for start in range(0, inner, 128):
        cols = slice(start, start + 128)
        conv = conv_ref[0, :, cols]
        sig = sigmoid(conv)
        values = conv * sig
        from_state = xs_ref[:, cols]
        total = u_ref[0, :, cols] + from_state
        xu_ref[:, cols] = values * total
        xs_ref[:, cols] = values * from_state
        xw_ref[:, cols] = values * (step_wide[:, cols] * weight_wide[:, cols])
        grad = step_wide[:, cols] * total + skip_wide[:, cols] * gm_ref[0, :, cols].astype(f32)
        conv_back(start, grad, conv, sig)
    grad_write = dw_ref[0] + dot2(xw_ref[...], state_ref[...], NT)
    conv_back(inner, grad_write, write_conv, sigmoid(write_conv))
    read_conv = conv_ref[0, :, inner + STATE :]
    conv_back(inner + STATE, dr_ref[0], read_conv, sigmoid(read_conv))
    direct = dot2(xu_ref[...], spread, NT)
    ends = dot2(xs_ref[...], spread, NT) * step
    held = dot2(jnp.broadcast_to(inner_sum, (16, inner)), spread, NT)[0:1] * jnp.exp(last)
    at_end = jnp.sum(ends, axis=0, keepdims=True) + held
    dcum = gs_ref[0] - skip_ref[...] * xg_ref[0] - step * direct
    sums_ref[CONV + 3 : CONV + 4, :heads] += jnp.sum(xg_ref[0], axis=0, keepdims=True)
    dcum = dcum + jnp.where(iota((length, heads), 0) == length - 1, at_end, 0.0)
    upper = (iota((length, length), 0) <= iota((length, length), 1)).astype(f32)
    da = exact(upper, dcum, NN)
    rate = jnp.exp(al_ref[...])
    sums_ref[CONV + 2 : CONV + 3, :heads] += jnp.sum(da * (-step * rate), axis=0, keepdims=True)
    raw = p_ref[0, HALO:, channels : channels + heads].astype(f32) + dtb_ref[...]
    draw = (direct - da * rate) * sigmoid(raw)
    grad_ref[0, :, channels:] = draw.astype(bf16)
    sums_ref[CONV + 1 : CONV + 2, :heads] += jnp.sum(draw, axis=0, keepdims=True)


def scan_back(u, dw, dr, xg, conv, p_ext, dt, cum, gm, gs, start, end, conv_weight, dt_bias, a_log, skip_gain):
    seqs, length, channels = conv.shape
    heads = dt.shape[2]
    inner = heads * HEADDIM
    dests, _, _, width = start.shape
    row = per_seq((length, inner))
    small = per_seq((length, heads))
    side = per_seq((length, STATE))
    states = per_dest((dests, STATE, width))
    return call(
        back_body,
        seqs,
        [
            row, side, side, small,
            per_seq((length, channels)),
            per_seq(p_ext.shape[1:]),
            small, small, row, small, states, states,
            whole((CONV, channels)),
            whole((1, heads)),
            whole((1, heads)),
            whole((1, heads)),
        ],
        [
            per_seq((length, channels + heads)),
            per_seq((8, channels)),
            per_seq((8, channels)),
            whole((8, channels)),
        ],
        [
            jax.ShapeDtypeStruct((seqs, length, channels + heads), bf16),
            jax.ShapeDtypeStruct((seqs, 8, channels), f32),
            jax.ShapeDtypeStruct((seqs, 8, channels), f32),
            jax.ShapeDtypeStruct((8, channels), f32),
        ],
        [
            pltpu.VMEM((STATE, inner), end.dtype),
            pltpu.VMEM((length, inner), f32),
            pltpu.VMEM((length, inner), f32),
            pltpu.VMEM((length, inner), f32),
        ],
        micros=14,
    )(u, dw, dr, xg, conv, p_ext, dt, cum, gm, gs, start, end, conv_weight,
      dt_bias[None], a_log[None], skip_gain[None])


def swap(x, axis, flip):
    count = lax.axis_size(axis)
    return lax.ppermute(x, axis, [(slot, slot ^ flip) for slot in range(count)])


def small_flips():
    flips = [("seq", 1 << k) for k in range(lax.axis_size("seq").bit_length() - 1)]
    flips[1:1] = [("fsdp", 1 << k) for k in range(lax.axis_size("fsdp").bit_length() - 1)]
    return flips


def one_more(x, flip, *events):
    got = swap(x, *flip)
    return x + (after(got, *events) if events else got)


def shared_slots():
    slot = lax.axis_index("seq")
    return slot // 4, slot // 2 % 2 == 1, slot % 2 == 1, lax.axis_index("fsdp") == 1


def fast_mesh():
    return lax.axis_size("fsdp") == 2 and lax.axis_size("seq") == 16


def halves(x, flag, axis):
    size = x.shape[axis] // 2
    low = lax.slice_in_dim(x, 0, size, axis=axis)
    high = lax.slice_in_dim(x, size, 2 * size, axis=axis)
    return jnp.where(flag, high, low), jnp.where(flag, low, high)


def join(own, other, flag, axis):
    low = jnp.where(flag, other, own)
    high = jnp.where(flag, own, other)
    return jnp.concatenate([low, high], axis=axis)


def after(x, *others):
    return lax.optimization_barrier((x,) + others)[0]


def fetch_rows(w, start=None, late=None):
    _, _, odd, _ = shared_slots()
    mine, _ = halves(w, odd, 0)
    if start is not None:
        mine = after(mine, start)
    fetched = swap(mine, "fsdp", 1)
    if late is not None:
        fetched = after(fetched, late)
    return fetched, swap(fetched, "seq", 1)


def gather_rows(w, start=None, late=None):
    if not fast_mesh():
        return lax.all_gather(w, "fsdp", axis=0, tiled=True)
    _, _, odd, second = shared_slots()
    fetched, shared = fetch_rows(w, start, late)
    return join(w, join(fetched, shared, odd, 0), second, 0)


def reduce_rows(part):
    shard = lax.psum_scatter(part, "fsdp", scatter_dimension=0, tiled=True)
    return lax.psum(shard, "seq")


def send_half(total, axis, flip, dim):
    size = total[0].shape[dim] // 2
    keep = [lax.slice_in_dim(term, 0, size, axis=dim).astype(f32) for term in total]
    give = [lax.slice_in_dim(term, size, 2 * size, axis=dim).astype(f32) for term in total]
    return [sum(keep[1:], keep[0]), swap(sum(give[1:], give[0]).astype(bf16), axis, flip)]


def held(sent, *events):
    return [sent[0]] + [after(piece, *events) for piece in sent[1:]]


def fold_z(total, flag, flip):
    keep, give = halves(total, flag, 0)
    return keep[0], swap(give[0].astype(bf16), "seq", flip)


def both(own, got):
    return jnp.stack([own, got])


def place_body(plan, slots_ref, *refs):
    outs = refs[-1:]
    z, x, core = slots_ref[0], slots_ref[1], slots_ref[2]
    for source, first, rows, base, wide in plan:
        for side in range(2):
            for k in range(2):
                src = refs[4 + side] if source else refs[2 * side + k]
                at = (lax.rem(core + side, 2) * 2 + lax.rem(x + k, 2)) * 128 * wide
                for shift in range(4):
                    low_bit = lax.rem(z + shift // 2, 2)
                    high_bit = lax.rem(z // 2 + shift % 2, 2)
                    row = base + (2 * high_bit + low_bit) * rows
                    for part in range(wide):
                        low = first + part * rows
                        outs[0][
                            pl.ds(pl.multiple_of(row, 8), rows),
                            pl.ds(pl.multiple_of(at + part * 128, 128), 128),
                        ] = (
                            src[shift // 2, shift % 2, k, low : low + rows, :]
                            if source
                            else src[shift // 2, shift % 2, low : low + rows, :]
                        ).astype(f32)


def place(slots, plan, arrays, shape):
    return pl.pallas_call(
        functools.partial(place_body, plan),
        in_specs=[pl.BlockSpec(memory_space=pltpu.SMEM)]
        + [pl.BlockSpec(memory_space=pltpu.VMEM)] * len(arrays),
        out_specs=pl.BlockSpec(memory_space=pltpu.VMEM),
        out_shape=jax.ShapeDtypeStruct(shape, f32),
        compiler_params=pltpu.CompilerParams(vmem_limit_bytes=VMEM_BYTES),
        cost_estimate=cost(6),
    )(slots, *arrays)


def dot(a, b, dims):
    return lax.dot_general(a, b, (dims, ((), ())), preferred_element_type=f32)


STATE_TYPE = bf16


def per_device(
    hidden_in, cotangent, norm_gain, in_weight, conv_weight, conv_bias,
    dt_bias, a_log, skip_gain, gate_gain, out_weight,
):
    seq_count = lax.axis_size("seq")
    seqs, length, width = hidden_in.shape
    rows = seqs * length
    heads = dt_bias.shape[0]
    inner = heads * HEADDIM
    forward = [(slot, slot + 1) for slot in range(seq_count - 1)]
    backward = [(slot + 1, slot) for slot in range(seq_count - 1)]
    fast = fast_mesh()

    w_gate, w_scan = in_weight[:, :inner], in_weight[:, inner:]
    if fast:
        z, x, odd, second = shared_slots()
        scan_give = halves(w_scan, odd, 0)[0]
        hidden_in = after(hidden_in, scan_give)
        scan_fetched = swap(scan_give, "fsdp", 1)
        slots = jnp.stack([z, x.astype(jnp.int32), odd.astype(jnp.int32)]).astype(jnp.int32)

    def prenorm(rows_in):
        inv = lax.rsqrt(jnp.mean(rows_in * rows_in, axis=-1, keepdims=True) + norm_eps)
        return inv, (rows_in * inv * norm_gain).astype(bf16)

    residual = hidden_in.astype(f32)
    inv_rms, scaled_low = prenorm(residual)
    halo = after(hidden_in, scaled_low)[:, length - HALO :]
    halo = lax.ppermute(halo, "seq", forward)
    _, scaled_halo = prenorm(halo.astype(f32))
    scaled_ext = jnp.concatenate([scaled_halo, scaled_low], axis=1)
    scaled_ext = scaled_ext.reshape(seqs * (HALO + length), width)
    scaled_low = scaled_low.reshape(rows, width)
    if fast:
        ext_own, ext_other = halves(scaled_ext, second, 1)
        ext_fetched, ext_shared = halves(ext_other, odd, 1)
        p_ext = dot(ext_own, w_scan, NN)
        scan_fetched = after(scan_fetched, p_ext)
        scan_shared = swap(scan_fetched, "seq", 1)
        p_ext = p_ext + dot(ext_fetched, scan_fetched, NN)
        p_ext = p_ext + dot(ext_shared, scan_shared, NN)
    else:
        scan_full = lax.all_gather(w_scan, "fsdp", axis=0, tiled=True)
        p_ext = dot(scaled_ext, scan_full, NN)
    p_ext = p_ext.astype(bf16).reshape(seqs, HALO + length, -1)

    conv, dt, cum, send = scan_front(
        p_ext, conv_weight, conv_bias, dt_bias, a_log, seq_count, STATE_TYPE
    )
    recv = lax.all_to_all(send, "seq", split_axis=0, concat_axis=0, tiled=True)
    y = scan_within(conv, dt, cum, skip_gain)
    grad_rows = cotangent.reshape(rows, width)
    ready = [y]
    if fast:
        own_side, other_side = halves(scaled_low, second, 1)
        quarters = [halves(side, odd, 1) for side in (own_side, other_side)]
        eighths = [[halves(quarter, x, 1) for quarter in pair] for pair in quarters]
        by_y = [
            jnp.concatenate([eighths[y_side][c][k] for y_side in (0, 1) for k in (0, 1)], axis=1)
            for c in (0, 1)
        ]
        by_x = [
            jnp.concatenate([eighths[y_side][c][k] for k in (0, 1) for y_side in (0, 1)], axis=1)
            for c in (0, 1)
        ]

        sides = [halves(side, x, 1) for side in halves(grad_rows, odd, 1)]
        cot = [jnp.concatenate(side, axis=1) for side in sides]
        ready += by_y + by_x + cot
    start_heads, decay = combine(recv, ready)
    gate_full = gather_rows(w_gate, conv, recv)
    out_full = gather_rows(out_weight, start_heads)
    start = lax.all_to_all(start_heads, "seq", split_axis=0, concat_axis=0, tiled=True)
    gate = dot(scaled_low, gate_full, NN).astype(bf16).reshape(seqs, length, inner)
    grad_normed = dot(grad_rows, out_full, NT).reshape(seqs, length, inner)
    normed, grad_gate, grad_mixed, back_send, gate_sums, gs, cread = middle(
        y, conv, cum, start, gate, gate_gain, grad_normed
    )
    back_recv = lax.all_to_all(back_send, "seq", split_axis=0, concat_axis=0, tiled=True)
    normed = normed.reshape(rows, inner)
    grad_gate = grad_gate.reshape(rows, inner)
    if fast:
        scan_full = join(w_scan, join(scan_fetched, scan_shared, odd, 0), second, 0)
        def near(left, right, *events):
            give = dot(left, right[1], TN).astype(bf16)
            keep = dot(left, right[0], TN)
            return held([keep, swap(give, "seq", 1)], *events)

        out_left = jnp.concatenate(halves(normed, second, 1), axis=1)
        gate_y = send_half(near(grad_gate, by_y), "fsdp", 1, 1)
        out_x = send_half(near(out_left, cot), "seq", 2, 1)
        ready = [out_x[0], gate_y[0]]
    else:
        out_total = reduce_rows(dot(normed, grad_rows, TN))
        gate_total = reduce_rows(dot(scaled_low, grad_gate, TN))
        ready = []
    end_heads = combine_back(back_recv, decay, ready)
    u, dw, dr, xg = scan_within_back(conv, dt, cum, after(grad_mixed, back_recv), cread)
    end = lax.all_to_all(end_heads, "seq", split_axis=0, concat_axis=0, tiled=True)
    hidden_out = (residual.reshape(rows, width) + dot(normed, out_full, NN)).astype(bf16)
    grad_scan, head, tail, conv_sums = scan_back(
        u, dw, dr, xg, conv, p_ext, dt, cum, grad_mixed, gs, start, end,
        conv_weight, dt_bias, a_log, skip_gain,
    )
    grad_raw = grad_scan
    following = lax.ppermute(head, "seq", backward)
    if fast:
        out_y = send_half(held(out_x, grad_raw), "fsdp", 1, 0)
        gate_x = send_half(held(gate_y, grad_raw), "seq", 2, 1)
    for tap in range(CONV - 1):
        reach = following[:, : CONV - 1 - tap]
        low = 8 - (CONV - 1) + tap
        tail = tail + conv_weight[tap] * jnp.pad(reach, ((0, 0), (low, 0), (0, 0)))
    grad_scan = lax.dynamic_update_slice(grad_scan, tail.astype(bf16), (0, length - 8, 0))
    grad_scan = grad_scan.reshape(rows, -1)

    held_back = []

    def lined_up(grad_scan, *events):
        if events:
            grad_scan = after(grad_scan, *events)
        grad_scaled = dot(grad_gate, gate_full, NT) + dot(grad_scan, scan_full, NT)
        rows_in = residual.reshape(rows, width)
        inv = inv_rms.reshape(rows, 1)
        norm_part = jnp.sum(grad_scaled * rows_in * inv, axis=0)
        f = norm_gain * grad_scaled
        mean = jnp.mean(rows_in * f, axis=-1, keepdims=True)
        held_back.append(grad_rows.astype(f32) + inv * f - rows_in * (inv * inv * inv * mean))
        lanes = conv_sums.shape[1]
        wide = [conv_sums[: CONV + 4], gate_sums[:1], norm_part[None]]
        wide = [jnp.pad(part, ((0, 0), (0, lanes - part.shape[1]))) for part in wide]
        return jnp.concatenate(wide, axis=0)

    if fast:
        cut = grad_scan.shape[1] // 64 * 32
        first = near(grad_scan[:, :cut], by_y)
        rest = near(grad_scan[:, cut:], by_x)
        first_y = send_half(first, "fsdp", 1, 1)
        rest_x = send_half(rest, "seq", 2, 1)
        waited = [held(out_y, rest_x[0]), held(gate_x, rest_x[0])]
        out_sum, gate_sum = [pair[0] + pair[1].astype(f32) for pair in waited]
        out_sum = out_sum.reshape(4, -1, 256)
        early = jnp.concatenate(
            [out_sum[:, :, :128], out_sum[:, :, 128:], gate_sum.reshape(4, -1, 128)], axis=1
        )
        low_bit, high_bit = z % 2 == 1, z // 2 == 1
        early = early.reshape(2, 2, -1, 128).swapaxes(0, 1)
        early_low = fold_z(early, low_bit, 4)
        sums = lined_up(grad_scan, first_y[0], rest_x[0])
        first_x = send_half(held(first_y, sums), "seq", 2, 1)
        rest_y = send_half(rest_x, "fsdp", 1, 1)
        flips = [("seq", 8), ("seq", 1), ("seq", 2), ("fsdp", 1), ("seq", 4)]
        sums = one_more(sums, flips[0])
        early_sum = early_low[0] + after(early_low[1], first_x[0], rest_y[0]).astype(f32)
        early_high = fold_z(early_sum, high_bit, 8)
        pair = [sent[0] + after(sent[1], sums).astype(f32) for sent in (first_x, rest_y)]
        late_cut = pair[0].shape[0] // 4
        late = jnp.concatenate([half.reshape(4, -1, 128) for half in pair], axis=1)
        late = late.reshape(2, 2, -1, 128).swapaxes(0, 1)
        late_low = fold_z(late, low_bit, 4)
        sums = one_more(after(sums, first_x[0], rest_y[0]), flips[1])
        early_sum = early_high[0] + after(early_high[1], late_low[0]).astype(f32)
        early_own = early_sum.astype(bf16)
        early_own = both(early_own, swap(early_own, "seq", 8))
        late_sum = late_low[0] + after(late_low[1], sums).astype(f32)
        late_high = fold_z(late_sum, high_bit, 8)
        early_own = after(early_own, late_high[0])
        sums = one_more(after(sums, late_low[0]), flips[2])
        early_near = both(early_own, swap(early_own, "seq", 4))
        late_got = after(late_high[1], sums, hidden_out, held_back[0])
        late_own = (late_high[0] + late_got.astype(f32)).astype(bf16)
        sums = one_more(after(sums, late_high[0]), flips[3])
        late_all = both(late_own, after(swap(late_own, "seq", 2), sums))
        early_near = after(early_near, late_own)
        early_far = swap(early_near, "seq", 2)
        sums = one_more(after(sums, late_own), flips[4])
        late_wide = both(late_all, after(swap(late_all, "seq", 8), sums))
        near_other = swap(early_near, "seq", 1)
        late_all = both(late_wide, swap(late_wide, "seq", 4))
        early_four = [early_near, early_far, near_other, swap(early_far, "seq", 1)]
        late_two = [late_all, swap(late_all, "seq", 1)]
        size = out_weight.shape[0] // 4
        out_total = place(slots, [(0, 0, size, 0, 2)], early_four, out_weight.shape)
    if not fast:
        sums = lined_up(grad_scan)
        for flip in small_flips():
            sums = one_more(sums, flip)
    grad_hidden = held_back[0]
    conv_sum, bias_sum = sums[:CONV], sums[CONV]
    shift_sum, rate_sum = sums[CONV + 1, :heads], sums[CONV + 2, :heads]
    skip_sum, gain_sum = sums[CONV + 3, :heads], sums[CONV + 4, :inner]
    norm_sum = sums[CONV + 5, :width]
    if fast:
        late_two[1] = after(late_two[1], out_total, skip_sum)
        plan = [
            (0, 2 * size, inner // 4, 0, 1),
            (1, 0, late_cut, inner, 1),
            (1, late_cut, late.shape[2] - late_cut, inner + cut, 1),
        ]
        in_total = place(slots, plan, early_four + late_two, in_weight.shape[::-1]).T
    else:
        in_total = jnp.concatenate(
            [gate_total, reduce_rows(dot(scaled_low, grad_scan, TN))], axis=1
        )
    return (
        hidden_out.reshape(hidden_in.shape),
        grad_hidden.reshape(hidden_in.shape),
        norm_sum,
        in_total,
        conv_sum,
        bias_sum,
        shift_sum,
        rate_sum,
        skip_sum,
        gain_sum,
        out_total,
    )


def solution(mesh):
    tokens = P("fsdp", "seq", None)
    weights = P("fsdp", None)
    return jax.shard_map(
        per_device,
        mesh=mesh,
        in_specs=(tokens, tokens, P(), weights, P(), P(), P(), P(), P(), P(), weights),
        out_specs=(tokens, tokens, P(), weights, P(), P(), P(), P(), P(), P(), weights),
        check_vma=False,
    )
```
